128 devices in a mesh: dp: 64 (over x, z_lo, y, core), tensor: 2 (over z_hi).
Axes of the slice: x: 4, y: 4, z: 4 (z_hi: 2, z_lo: 2; z = z_hi * 2 + z_lo), core: 2. Of those that a mesh axis runs over, the one named last changes fastest.
Arguments:
- tokens: bfloat16 [49152, 896], P(('dp', 'tensor')), may hold values from -6 to 6
- long_count: int32 [64], P('dp'), may hold values from 0 to 1
- attn_gain: bfloat16 [896], replicated, may hold values from 0.5 to 1.5
- w_query: bfloat16 [896, 896], P(None, 'tensor'), may hold values from -0.1875 to 0.1875
- b_query: bfloat16 [896], P('tensor'), may hold values from -3 to 3
- w_key: bfloat16 [896, 128], P(None, 'tensor'), may hold values from -0.1875 to 0.1875
- b_key: bfloat16 [128], P('tensor'), may hold values from -3 to 3
- w_value: bfloat16 [896, 128], P(None, 'tensor'), may hold values from -0.1875 to 0.1875
- b_value: bfloat16 [128], P('tensor'), may hold values from -3 to 3
- w_out: bfloat16 [896, 896], P('tensor'), may hold values from -0.75 to 0.75
- mlp_gain: bfloat16 [896], replicated, may hold values from 0.5 to 1.5
- w_gate: bfloat16 [896, 4864], P(None, 'tensor'), may hold values from -0.1875 to 0.1875
- w_up: bfloat16 [896, 4864], P(None, 'tensor'), may hold values from -0.1875 to 0.1875
- w_down: bfloat16 [4864, 896], P('tensor'), may hold values from -0.078125 to 0.078125
- cotangent: bfloat16 [49152, 896], P(('dp', 'tensor')), may hold values from -6 to 6
Outputs:
- output: bfloat16 [49152, 896], P(('dp', 'tensor'))
- grad_tokens: bfloat16 [49152, 896], P(('dp', 'tensor'))
- grad_attn_gain: float32 [896], replicated
- grad_w_query: float32 [896, 896], P(None, 'tensor')
- grad_b_query: float32 [896], P('tensor')
- grad_w_key: float32 [896, 128], P(None, 'tensor')
- grad_b_key: float32 [128], P('tensor')
- grad_w_value: float32 [896, 128], P(None, 'tensor')
- grad_b_value: float32 [128], P('tensor')
- grad_w_out: float32 [896, 896], P('tensor')
- grad_mlp_gain: float32 [896], replicated
- grad_w_gate: float32 [896, 4864], P(None, 'tensor')
- grad_w_up: float32 [896, 4864], P(None, 'tensor')
- grad_w_down: float32 [4864, 896], P('tensor')
The draws below stay inside these ranges and needn't reach their ends.
Inputs may be any that keep to these rules, and one draw needn't show every extreme that they name: `long_count`: 1 where the group holds a sequence of 512 tokens followed by one of 256; 0 where it holds three sequences of 256.
All inputs are finite; a program needn't handle non-finite values.
Results may differ from the reference program's by a relative error of at most 0.025.
Values may be sent and summed in bfloat16 or wider, within the bound.
No kernel may reach another device: no remote copies, remote signals or barrier semaphores. Data moves between devices by JAX's collectives and lax.ppermute only.
A program may use at most 192 MiB of HBM per device.

```python
import math
import jax
import jax.numpy as jnp
from jax import lax

D = 896
HEADS = 14
KV = 2
HD = 64
FF = 4864
SHORT = 256
TOK_DEV = 384
TOKENS = 49152
N_DP = 64
N_TENSOR = 2


def touch_ends(values, rng, smallest, top_value):
    spot = [jax.random.randint(jax.random.fold_in(rng, axis), (), 0, length) for axis, length in enumerate(values.shape)]
    longest = values.shape.index(max(values.shape))
    beside = spot[:longest] + [(spot[longest] + 1) % values.shape[longest]] + spot[longest + 1:]
    return values.at[tuple(spot)].set(smallest).at[tuple(beside)].set(top_value)


def level_of(stream_key, shape, pieces, low, largest):
    loudness = 1.0
    for axis_at, blocks in pieces:
        heights = jax.random.uniform(jax.random.fold_in(jax.random.fold_in(stream_key, 6), axis_at), (blocks,), jnp.float32, low / len(pieces), largest / len(pieces))
        loudness = loudness * jnp.repeat(jnp.exp(heights), shape[axis_at] // blocks).reshape((-1,) + (1,) * (len(shape) - 1 - axis_at))
    return loudness


def centred(rng, extent, deviation, most, cuts=(), kind=jnp.bfloat16):
    gain = level_of(rng, extent, cuts, -0.22, 0.18) if cuts else 1.0
    array = jax.random.normal(rng, extent, jnp.float32) * deviation * gain
    return jnp.minimum(jnp.maximum(array, -most), most).astype(kind)


def setup_inputs(seed: int = 0) -> dict:
    key_of = jax.random.split(jax.random.key(seed), 16)
    tokens = centred(key_of[0], (TOKENS, D), 1.0, 6.0, ((0, 128),))
    long_count = touch_ends(jax.random.randint(key_of[1], (N_DP,), 0, 2), jax.random.fold_in(key_of[1], 1), 0, 1).astype(jnp.int32)
    attn_gain = jnp.clip(1.0 + 0.1 * jax.random.normal(key_of[2], (D,), jnp.float32), 0.5, 1.5).astype(jnp.bfloat16)
    w_query = centred(key_of[3], (D, HEADS * HD), D ** -0.5, 0.1875, ((1, 2),))
    b_query = centred(key_of[4], (HEADS * HD,), 0.5, 3.0, ((0, 2),))
    w_key = centred(key_of[5], (D, KV * HD), D ** -0.5, 0.1875, ((1, 2),))
    b_key = centred(key_of[6], (KV * HD,), 0.5, 3.0, ((0, 2),))
    w_value = centred(key_of[7], (D, KV * HD), D ** -0.5, 0.1875, ((1, 2),))
    b_value = centred(key_of[8], (KV * HD,), 0.5, 3.0, ((0, 2),))
    w_out = centred(key_of[9], (HEADS * HD, D), (HEADS * HD // 16) ** -0.5, 0.75, ((0, 2),))
    mlp_gain = jnp.clip(1.0 + 0.1 * jax.random.normal(key_of[10], (D,), jnp.float32), 0.5, 1.5).astype(jnp.bfloat16)
    w_gate = centred(key_of[11], (D, FF), D ** -0.5, 0.1875, ((1, 2),))
    w_up = centred(key_of[12], (D, FF), D ** -0.5, 0.1875, ((1, 2),))
    w_down = centred(key_of[13], (FF, D), FF ** -0.5, 0.078125, ((0, 2),))
    cotangent = centred(key_of[14], (TOKENS, D), 1.0, 6.0, ((0, 128),))
    return {"tokens": tokens, "long_count": long_count, "attn_gain": attn_gain, "w_query": w_query, "b_query": b_query, "w_key": w_key, "b_key": b_key, "w_value": w_value, "b_value": b_value, "w_out": w_out, "mlp_gain": mlp_gain, "w_gate": w_gate, "w_up": w_up, "w_down": w_down, "cotangent": cotangent}


@jax.custom_vjp
def low(v):
    return lax.optimization_barrier(v.astype(jnp.bfloat16)).astype(jnp.float32)

@jax.custom_vjp
def low_back(v):
    return v

def low_keep(v):
    return (low(v), None)

def low_pass(kept, grad):
    return (grad,)

def back_keep(v):
    return (v, None)

def back_low(kept, grad):
    return (low(grad),)
low.defvjp(low_keep, low_pass)
low_back.defvjp(back_keep, back_low)
EPSILON = 1e-06
ROPE_BASE = 1000000.0

def normalize(field):
    return field * lax.rsqrt(lax.optimization_barrier(jnp.mean(field * field, axis=-1, keepdims=True)) + EPSILON)

def highest(left, right):
    return jnp.dot(left, right, precision=lax.Precision.HIGHEST, preferred_element_type=jnp.float32)

def rotate(field, cosine, sine):
    halfway = field.shape[-1] // 2
    first_half = field[..., :halfway]
    second_half = field[..., halfway:]
    return jnp.concatenate([first_half * cosine - second_half * sine, second_half * cosine + first_half * sine], axis=-1)

def attend(items):
    queries, keys, values, segment = items
    group_rows = queries.shape[0]
    row_index = jnp.arange(group_rows, dtype=jnp.int32)
    allowed = (segment[:, None] == segment[None, :]) & (row_index[None, :] <= row_index[:, None])
    scores = jnp.einsum('qcgd,kcd->cgqk', queries, keys, precision=lax.Precision.HIGHEST) * (1.0 / math.sqrt(HD))
    scores = low_back(scores)
    scores = jnp.where(allowed, scores, -1e+30)
    chance = jax.nn.softmax(scores, axis=-1)
    mixed = jnp.einsum('cgqk,kcd->qcgd', low(chance), values, precision=lax.Precision.HIGHEST)
    return low(low_back(mixed))

def reference(tokens, long_count, attn_gain, w_query, b_query, w_key, b_key, w_value, b_value, w_out, mlp_gain, w_gate, w_up, w_down, cotangent):
    group_rows = TOK_DEV * N_TENSOR
    row_index = jnp.arange(group_rows, dtype=jnp.int32)[None, :]
    is_long = long_count[:, None] == 1
    second = (row_index >= 2 * SHORT).astype(jnp.int32)
    segment = jnp.where(is_long, second, row_index // SHORT).astype(jnp.int32)
    offset = jnp.where(is_long, second * 2 * SHORT, row_index // SHORT * SHORT).astype(jnp.int32)
    position = (row_index - offset).astype(jnp.float32)
    freq_index = jnp.arange(HD // 2, dtype=jnp.float32)
    inverse = ROPE_BASE ** (-2.0 * freq_index / HD)
    angle = position[:, :, None] * inverse[None, None, :]
    cosine = jnp.cos(angle)[:, :, None, :]
    sine = jnp.sin(angle)[:, :, None, :]

    def forward(resid, gain_one, wq, bq, wk, bk, wv, bv, wo, gain_two, wg, wu, wd):
        attn_in = low(normalize(resid) * gain_one)
        query_lin = low_back(highest(attn_in, wq) + bq)
        key_lin = low_back(highest(attn_in, wk) + bk)
        value_lin = low_back(highest(attn_in, wv) + bv)
        queries = low(rotate(query_lin.reshape(N_DP, group_rows, HEADS, HD), cosine, sine))
        keys = low(rotate(key_lin.reshape(N_DP, group_rows, KV, HD), cosine, sine))
        values = low(value_lin.reshape(N_DP, group_rows, KV, HD))
        queries = queries.reshape(N_DP, group_rows, KV, HEADS // KV, HD)
        attended = lax.map(jax.checkpoint(attend), (queries, keys, values, segment))
        attended = attended.reshape(TOKENS, HEADS * HD)
        hidden_mid = resid + low_back(highest(attended, wo))
        mlp_in = low(normalize(hidden_mid) * gain_two)
        gate_val = low_back(highest(mlp_in, wg))
        up_val = low_back(highest(mlp_in, wu))
        active = low(jax.nn.silu(gate_val) * up_val)
        return hidden_mid + low_back(highest(active, wd))
    floats = [arr.astype(jnp.float32) for arr in (tokens, attn_gain, w_query, b_query, w_key, b_key, w_value, b_value, w_out, mlp_gain, w_gate, w_up, w_down)]
    result, pullback = jax.vjp(forward, *floats)
    grads = pullback(cotangent.astype(jnp.float32))
    return (result.astype(jnp.bfloat16), grads[0].astype(jnp.bfloat16), grads[1], grads[2], grads[3], grads[4], grads[5], grads[6], grads[7], grads[8], grads[9], grads[10], grads[11], grads[12])
```

```python
import functools

import jax
import jax.numpy as jnp
from jax import lax
from jax.experimental import pallas as pl
from jax.experimental.pallas import tpu as pltpu
from jax.sharding import Mesh
from jax.sharding import PartitionSpec as P

HD = 64
EPSILON = 1e-06
ROPE_BASE = 1000000.0
BF = jnp.bfloat16
F32 = jnp.float32

D = 896
HALF = 384
ROWS = 768
HEADS = 7
PIECE = 56
SLAB = 224
HID = 1280
STEP = 1152
CHUNK = 256
MIB = 1024 * 1024

VM = pl.BlockSpec(memory_space=pltpu.VMEM)
SM = pl.BlockSpec(memory_space=pltpu.SMEM)


def sds(shape, dtype):
    return jax.ShapeDtypeStruct(shape, dtype)


def nn(a, b):
    return lax.dot_general(a, b, (((1,), (0,)), ((), ())), preferred_element_type=F32)


def nt(a, b):
    return lax.dot_general(a, b, (((1,), (1,)), ((), ())), preferred_element_type=F32)


def tn(a, b):
    return lax.dot_general(a, b, (((0,), (0,)), ((), ())), preferred_element_type=F32)


def factor_of(field):
    return lax.rsqrt(jnp.mean(field * field, axis=-1, keepdims=True) + EPSILON)


def params(mib):
    return pltpu.CompilerParams(vmem_limit_bytes=mib * MIB)


def cost(flops, size, trans=0):
    return pl.CostEstimate(flops=flops, bytes_accessed=size, transcendentals=trans)


def half_offsets(place):
    mine = pl.multiple_of(place * HALF, HALF)
    other = pl.multiple_of((1 - place) * HALF, HALF)
    return mine, other


def masks(is_long):
    row = lax.broadcasted_iota(jnp.int32, (256, 256), 0)
    col = lax.broadcasted_iota(jnp.int32, (256, 256), 1)
    causal = jnp.where(col <= row, 0.0, -1e30).astype(F32)
    before = jnp.full((256, 256), jnp.where(is_long == 1, 0.0, -1e30).astype(F32))
    return causal, jnp.concatenate([before, causal], axis=1)


SPANS = ((0, 0, 256), (256, 0, 512), (512, 512, 768))


def attention_kernel(info, tok_own, tok_rec, gain, w_all, b_all, cosine, sine,
                     attn_in, rotated, value, stats, att_send, att_keep):
    mine, other = half_offsets(info[0])
    for src, off in ((tok_own, mine), (tok_rec, other)):
        field = src[...].astype(F32)
        attn_in[pl.ds(off, HALF), :] = (field * factor_of(field) * gain[...]).astype(BF)
    for block in range(3):
        rows = slice(256 * block, 256 * block + 256)
        lin = nn(attn_in[rows, :], w_all[...]) + b_all[...]
        cos_b, sin_b = cosine[rows, :], sine[rows, :]
        for head in range(HEADS + 1):
            part = lin[:, 128 * head : 128 * head + 128]
            turned = part * cos_b + pltpu.roll(part, 64, 1) * sin_b
            rotated[rows, 128 * head : 128 * head + 128] = turned.astype(BF)
        value[rows, :] = lin[:, 1024:1152].astype(BF)
    causal, wide = masks(info[1])
    lane = lax.broadcasted_iota(jnp.int32, (256, 128), 1)
    for block, (first, low, high) in enumerate(SPANS):
        rows = slice(first, first + 256)
        mask = wide if block == 1 else causal
        keys = rotated[low:high, 1024 - 128 :]
        vals = value[low:high, :]
        kept = jnp.zeros((256, 128), F32)
        outs = []
        for head in range(HEADS):
            scores = nt(rotated[rows, 128 * head : 128 * head + 128], keys) * 0.0625 + mask
            top = jnp.max(scores, axis=-1, keepdims=True)
            expo = jnp.exp(scores - top)
            total = jnp.sum(expo, axis=-1, keepdims=True)
            kept = jnp.where(lane == head, top + jnp.log(total), kept)
            outs.append(nn(expo.astype(BF), vals) * (1.0 / total))
        stats[rows, :] = kept
        outs.append(jnp.zeros((256, 128), F32))
        for pair in range(4):
            both = jnp.where(lane < 64, outs[2 * pair], outs[2 * pair + 1]).astype(BF)
            att_keep[rows, 128 * pair : 128 * pair + 128] = both
            if pair < 3:
                att_send[rows, 128 * pair : 128 * pair + 128] = both
            else:
                att_send[rows, 384:448] = both[:, :64]


def attention(info, tok_own, tok_rec, gain, w_all, b_all, cosine, sine):
    return pl.pallas_call(
        attention_kernel,
        name="attention_forward",
        in_specs=[SM] + [VM] * 7,
        out_specs=[VM] * 6,
        out_shape=[
            sds((ROWS, D), BF),
            sds((ROWS, 1024), BF),
            sds((ROWS, 128), BF),
            sds((ROWS, 128), F32),
            sds((ROWS, 448), BF),
            sds((ROWS, 512), BF),
        ],
        compiler_params=params(48),
        cost_estimate=cost(4 * 10**9, 12 * 10**6, 3 * 10**6),
    )(info, tok_own, tok_rec, gain, w_all, b_all, cosine, sine)


def project_kernel(info, att_own, att_rec, wo_own, wo_rec, tok_own, tok_rec, gain, hidden, mlp_in):
    mine, other = half_offsets(info[0])
    for src, off in ((tok_own, mine), (tok_rec, other)):
        rows = pl.ds(off, HALF)
        field = (
            nn(att_own[rows, :], wo_own[...]) + nn(att_rec[rows, :], wo_rec[...])
        ) + src[...].astype(F32)
        hidden[rows, :] = field
        mlp_in[rows, :] = (field * factor_of(field) * gain[...]).astype(BF)


def project(info, att_own, att_rec, wo_own, wo_rec, tok_own, tok_rec, gain):
    return pl.pallas_call(
        project_kernel,
        name="project_norm",
        in_specs=[SM] + [VM] * 7,
        out_specs=[VM] * 2,
        out_shape=[sds((ROWS, D), F32), sds((ROWS, D), BF)],
        compiler_params=params(40),
        cost_estimate=cost(13 * 10**8, 10 * 10**6),
    )(info, att_own, att_rec, wo_own, wo_rec, tok_own, tok_rec, gain)


def turn_kernel(info, own, rec, by_x, by_y):
    for at, src in enumerate((own, rec)):
        cols = slice(ROWS * at, ROWS * at + ROWS)
        for slab in range(4):
            turned = src[:, SLAB * slab : SLAB * slab + SLAB].astype(F32).T.astype(BF)
            for place, out in ((info[2], by_x), (info[3], by_y)):
                slot = lax.rem(slab - place + 4, 4)
                out[pl.ds(pl.multiple_of(slot * SLAB, SLAB), SLAB), cols] = turned


def turn(info, own, rec):
    return pl.pallas_call(
        turn_kernel,
        name="transpose_rows",
        in_specs=[SM] + [VM] * 2,
        out_specs=[VM] * 2,
        out_shape=[sds((D, 2 * ROWS), BF)] * 2,
        compiler_params=params(48),
        cost_estimate=cost(10**6, 8 * 10**6),
    )(info, own, rec)


def feed_kernel(first, lanes, m_own, m_rec, g_own, g_rec, m_x, m_y, g_t, wg, wu, wd, *rest):
    rest = list(rest)
    starts = [rest.pop(0) for _ in range(0 if first else 4)]
    slots_x = [rest.pop(0) for _ in range(4)]
    slots_y = [rest.pop(0) for _ in range(4)]
    ends = [rest.pop(0) for _ in range(4)]
    act_s, gate_s, up_s, *sums = rest
    step = pl.program_id(0)

    @pl.when(step == 0)
    def _():
        for at in range(4):
            sums[at][...] = jnp.zeros((ROWS, D), F32) if first else starts[at][...].astype(F32)

    for at, (m, g) in enumerate(((m_own, g_own), (m_rec, g_rec))):
        rows = slice(ROWS * at, ROWS * at + ROWS)
        gate = nn(m[...], wg[...])
        up = nn(m[...], wu[...])
        grad = nt(g[...], wd[...])
        sig = 1.0 / (1.0 + jnp.exp(-gate))
        swish = gate * sig
        act_s[rows, :] = (swish * up).astype(BF)
        up_s[rows, :] = (grad * swish).astype(BF)
        gate_s[rows, :] = (grad * up * (sig + swish * (1.0 - sig))).astype(BF)
        sums[at][...] += nn(act_s[rows, :], wd[...])
        sums[2 + at][...] += nt(gate_s[rows, :], wg[...]) + nt(up_s[rows, :], wu[...])
    at_x = pl.ds(pl.multiple_of(step * CHUNK, CHUNK), CHUNK)
    at_down = pl.ds(pl.multiple_of(step * CHUNK + lanes, CHUNK), CHUNK)
    for left, right, slots, cols in (
        (m_x, gate_s, slots_x, at_x),
        (m_y, up_s, slots_y, at_x),
        (g_t, act_s, slots_x if first else slots_y, at_down),
    ):
        product = nn(left[...], right[...])
        for slot in range(4):
            for piece in range(4):
                low = SLAB * slot + PIECE * piece
                slots[slot][piece, :, cols] = product[low : low + PIECE, :].astype(BF)

    @pl.when(step == pl.num_programs(0) - 1)
    def _():
        for at in range(4):
            ends[at][...] = sums[at][...].astype(BF)


def feed(first, m_own, m_rec, g_own, g_rec, m_x, m_y, g_t, wg, wu, wd, starts):
    steps = 3 if first else 2
    at = 0 if first else 3
    lanes = steps * CHUNK
    wide_x, wide_y = (2 * lanes, lanes) if first else (lanes, 2 * lanes)

    def whole(shape):
        zeros = (0,) * len(shape)
        return pl.BlockSpec(shape, lambda j: zeros, pipeline_mode=pl.Buffered(1))

    rows = whole((ROWS, D))
    turned = whole((D, 2 * ROWS))
    wide = pl.BlockSpec((D, CHUNK), lambda j: (0, j + at))
    tall = pl.BlockSpec((CHUNK, D), lambda j: (j + at, 0))
    return pl.pallas_call(
        functools.partial(feed_kernel, first, lanes),
        name="feed_first" if first else "feed_second",
        grid=(steps,),
        in_specs=[rows] * 4 + [turned] * 3 + [wide, wide, tall] + [rows] * len(starts),
        out_specs=[whole((4, PIECE, wide_x))] * 4 + [whole((4, PIECE, wide_y))] * 4 + [rows] * 4,
        out_shape=[sds((4, PIECE, wide_x), BF)] * 4
        + [sds((4, PIECE, wide_y), BF)] * 4
        + [sds((ROWS, D), BF)] * 4,
        scratch_shapes=[pltpu.VMEM((2 * ROWS, CHUNK), BF)] * 3 + [pltpu.VMEM((ROWS, D), F32)] * 4,
        compiler_params=params(63),
        cost_estimate=cost(steps * 63 * 10**8, 30 * 10**6, steps * 4 * 10**5),
    )(m_own, m_rec, g_own, g_rec, m_x, m_y, g_t, wg, wu, wd, *starts)


def fold_kernel(info, *refs):
    ins_x, ins_y, outs_x, outs_y = refs[:4], refs[4:8], refs[8:12], refs[12:]
    for place, ins, outs in ((info[3], ins_x, outs_x), (info[2], ins_y, outs_y)):
        for slot in range(4):
            piece = lax.rem(place + slot, 4)
            total = ins[0][piece].astype(F32)
            for ref in ins[1:]:
                total = total + ref[piece].astype(F32)
            outs[slot][...] = total.astype(BF)


def fold(info, ins_x, ins_y):
    wide_x, wide_y = ins_x[0].shape[-1], ins_y[0].shape[-1]
    return pl.pallas_call(
        fold_kernel,
        name="sum_slabs",
        in_specs=[SM] + [VM] * 8,
        out_specs=[VM] * 8,
        out_shape=[sds((PIECE, wide_x), BF)] * 4 + [sds((PIECE, wide_y), BF)] * 4,
        compiler_params=params(32),
        cost_estimate=cost(10**7, 6 * 10**6),
    )(info, *ins_x, *ins_y)


def join_kernel(*refs):
    ins_x, ins_y, out = refs[:4], refs[4:8], refs[8]
    wide = ins_x[0].shape[-1]
    for ins, cols in ((ins_x, slice(0, wide)), (ins_y, slice(wide, None))):
        total = ins[0][...].astype(F32)
        for ref in ins[1:]:
            total = total + ref[...].astype(F32)
        out[:, cols] = total.astype(BF)


def join(ins_x, ins_y):
    wide = ins_x[0].shape[-1] + ins_y[0].shape[-1]
    return pl.pallas_call(
        join_kernel,
        name="sum_pieces",
        in_specs=[VM] * 8,
        out_specs=VM,
        out_shape=sds((PIECE, wide), BF),
        compiler_params=params(16),
        cost_estimate=cost(10**6, 2 * 10**6),
    )(*ins_x, *ins_y)


def back_kernel(info, dm_own, dm_rec, cot, hidden, gain_two, tok_own, tok_rec, gain_one,
                wo_dup, att, rotated, value, stats, cosine, sine, attn_in, w_cat,
                grad_mid, da_own, da_send, pack_a, pack_b,
                branch, grad_att, lin, grad_in):
    mine, other = half_offsets(info[0])
    sum_two = jnp.zeros((1, D), F32)
    for own, off in ((True, mine), (False, other)):
        rows = pl.ds(off, HALF)
        field = hidden[rows, :]
        factor = factor_of(field)
        normed = field * factor
        grad = dm_own[rows, :].astype(F32) + dm_rec[rows, :].astype(F32)
        scaled = grad * gain_two[...]
        middle = cot[rows, :].astype(F32) + factor * (
            scaled - normed * jnp.mean(scaled * normed, axis=-1, keepdims=True)
        )
        branch[rows, :] = middle.astype(BF)
        if own:
            grad_mid[...] = middle
            sum_two = jnp.sum(grad * normed, axis=0, keepdims=True)
    grad_att[...] = nt(branch[...], wo_dup[...]).astype(BF)
    causal, wide = masks(info[1])
    lane = lax.broadcasted_iota(jnp.int32, (256, 128), 1)
    grad_k = [jnp.zeros((256, 128), F32) for _ in range(3)]
    grad_v = [jnp.zeros((256, 128), F32) for _ in range(3)]
    for block, (first, low, high) in enumerate(SPANS):
        rows = slice(first, first + 256)
        mask = wide if block == 1 else causal
        keys = rotated[low:high, 896:1024]
        vals = value[low:high, :]
        cos_b, sin_b = cosine[rows, :], sine[rows, :]
        kept = stats[rows, :]
        turned = []
        for head in range(HEADS):
            cols = slice(128 * head, 128 * head + 128)
            query, grad_o = rotated[rows, cols], grad_att[rows, cols]
            base = jnp.sum(jnp.where(lane == head, kept, 0.0), axis=-1, keepdims=True)
            chance = jnp.exp(nt(query, keys) * 0.0625 + mask - base)
            grad_p = nt(grad_o, vals) * 0.5
            inner = jnp.sum(chance * grad_p, axis=-1, keepdims=True)
            grad_s = (chance * (grad_p - inner)).astype(BF)
            low_p = chance.astype(BF)
            back = nn(grad_s, keys) * 0.125
            turned.append(back * cos_b - pltpu.roll(back, 64, 1) * sin_b)
            for at in range((high - low) // 256):
                part = slice(256 * at, 256 * at + 256)
                grad_k[low // 256 + at] += tn(grad_s[:, part], query)
                grad_v[low // 256 + at] += tn(low_p[:, part], grad_o)
        turned.append(jnp.zeros((256, 128), F32))
        for pair in range(4):
            right = pltpu.roll(turned[2 * pair + 1], 64, 1)
            lin[rows, 128 * pair : 128 * pair + 128] = jnp.where(
                lane < 64, turned[2 * pair], right
            ).astype(BF)
    for block in range(3):
        rows = slice(256 * block, 256 * block + 256)
        back = grad_k[block] * 0.125
        back = back * cosine[rows, :] - pltpu.roll(back, 64, 1) * sine[rows, :]
        back = pltpu.roll(back, 64, 1).astype(BF)
        lin[rows, 384:512] = jnp.where(lane < 64, lin[rows, 384:512], back)
        lin[rows, 512:640] = jnp.where(lane < 64, 0.0, grad_v[block]).astype(BF)
    grad_in[...] = nt(lin[...], w_cat[...])
    sum_one = jnp.zeros((1, D), F32)
    for src, out, off in ((tok_own, da_own, mine), (tok_rec, da_send, other)):
        rows = pl.ds(off, HALF)
        field = src[...].astype(F32)
        grad = grad_in[rows, :]
        out[...] = grad.astype(out.dtype)
        sum_one = sum_one + jnp.sum(grad * (field * factor_of(field)), axis=0, keepdims=True)
    sum_b = jnp.sum(lin[...].astype(F32), axis=0, keepdims=True)
    grad_w = tn(attn_in[...], lin[...])
    grad_o = tn(branch[...], att[...])
    first_w = grad_w[:, :512]
    second_w = jnp.concatenate([grad_o[:, :384], grad_o[:, 384:] + grad_w[:, 512:]], axis=1)
    nothing = jnp.zeros((8, 512), F32)

    def eight(row):
        return jnp.broadcast_to(row, (8, 512))

    zeros_128 = jnp.zeros((1, 128), F32)
    extra_a = {0: sum_b[:, :512], 1: sum_one[:, :512], 2: sum_two[:, :512]}
    extra_b = {
        0: jnp.concatenate([zeros_128] * 3 + [sum_b[:, 512:]], axis=1),
        1: jnp.concatenate([sum_one[:, 512:], zeros_128], axis=1),
        2: jnp.concatenate([sum_two[:, 512:], zeros_128], axis=1),
    }
    for piece in range(16):
        rows = slice(PIECE * piece, PIECE * piece + PIECE)
        for out, grads, extra in ((pack_a, first_w, extra_a), (pack_b, second_w, extra_b)):
            more = eight(extra[piece]) if piece in extra else nothing
            out[piece] = jnp.concatenate([grads[rows, :], more], axis=0).astype(BF)


def back(info, *args):
    return pl.pallas_call(
        back_kernel,
        name="attention_backward",
        in_specs=[SM] + [VM] * 17,
        out_specs=[VM] * 5,
        out_shape=[
            sds((HALF, D), F32),
            sds((HALF, D), F32),
            sds((HALF, D), BF),
            sds((16, 64, 512), BF),
            sds((16, 64, 512), BF),
        ],
        scratch_shapes=[
            pltpu.VMEM((ROWS, D), BF),
            pltpu.VMEM((ROWS, D), BF),
            pltpu.VMEM((ROWS, 640), BF),
            pltpu.VMEM((ROWS, D), F32),
        ],
        compiler_params=params(60),
        cost_estimate=cost(9 * 10**9, 24 * 10**6, 3 * 10**6),
    )(info, *args)


def wide_kernel(info, a_own, a_rec, b_own, b_rec, gate, up):
    first = info[4] == 0
    for out, in_a, in_b in ((gate, slice(0, 768), slice(0, 512)), (up, slice(1536, 2304), slice(512, 1024))):
        ours_a, theirs_a = a_own[0, :, in_a].astype(F32), a_rec[0, :, in_a].astype(F32)
        ours_b, theirs_b = b_own[0, :, in_b].astype(F32), b_rec[0, :, in_b].astype(F32)
        out[:, 0:768] = jnp.where(first, ours_a, theirs_a)
        out[:, 768:1280] = jnp.where(first, ours_b, theirs_b)
        out[:, 1280:1920] = jnp.where(first, theirs_a, ours_a)[:, 128:]
        out[:, 1920:2432] = jnp.where(first, theirs_b, ours_b)


def wide(info, a_own, a_rec, b_own, b_rec):
    block_a = pl.BlockSpec((1, PIECE, 2304), lambda p: (p, 0, 0))
    block_b = pl.BlockSpec((1, PIECE, 1536), lambda p: (p, 0, 0))
    return pl.pallas_call(
        wide_kernel,
        name="gradients_wide",
        grid=(16,),
        in_specs=[SM, block_a, block_a, block_b, block_b],
        out_specs=[
            pl.BlockSpec((PIECE, 2432), lambda p: (p, 0)),
            pl.BlockSpec((PIECE, 2432), lambda p: ((p % 4) * 4 + p // 4, 0)),
        ],
        out_shape=[sds((D, 2432), F32)] * 2,
        compiler_params=params(32),
        cost_estimate=cost(10**7, 28 * 10**6),
    )(info, a_own, a_rec, b_own, b_rec)


def tall_kernel(info, a_own, a_rec, b_own, b_rec, down):
    step = pl.program_id(0)
    first = (info[4] == 0) == (step < 10)
    tile = jnp.where(step < 10, step, step - 9)

    @pl.when(tile < 6)
    def _():
        picked = jnp.where(first, a_own[...].astype(F32), a_rec[...].astype(F32))
        down[...] = picked.reshape(D, 128).T

    @pl.when(tile >= 6)
    def _():
        picked = jnp.where(first, b_own[...].astype(F32), b_rec[...].astype(F32))
        order = [picked[4 * (q % 4) + q // 4] for q in range(16)]
        down[...] = jnp.concatenate(order, axis=0).T


def tall(info, a_own, a_rec, b_own, b_rec):
    def tile(k):
        return jnp.where(k < 10, k, k - 9)

    block_a = pl.BlockSpec((16, PIECE, 128), lambda k: (0, 0, 6 + jnp.minimum(tile(k), 5)))
    block_b = pl.BlockSpec((16, PIECE, 128), lambda k: (0, 0, 8 + jnp.maximum(tile(k) - 6, 0)))
    return pl.pallas_call(
        tall_kernel,
        name="gradients_tall",
        grid=(19,),
        in_specs=[SM, block_a, block_a, block_b, block_b],
        out_specs=pl.BlockSpec((128, D), lambda k: (k, 0)),
        out_shape=sds((2432, D), F32),
        compiler_params=params(32),
        cost_estimate=cost(10**7, 14 * 10**6),
    )(info, a_own, a_rec, b_own, b_rec)


def send(field, axis, shift=1):
    size = lax.axis_size(axis)
    return lax.ppermute(field, axis, [(i, (i + shift) % size) for i in range(size)])


def after(field, *others):
    return lax.optimization_barrier((field, *others))[0]


def by_place(place, own, rec, axis=0):
    first = place == 0
    return jnp.concatenate([jnp.where(first, own, rec), jnp.where(first, rec, own)], axis=axis)


def swapped(weight):
    return jnp.concatenate([-weight[..., HD // 2 :], weight[..., : HD // 2]], axis=-1)


def tables(is_long):
    row = jnp.arange(ROWS, dtype=jnp.int32)
    second = (row >= 512).astype(jnp.int32) * 512
    offset = jnp.where(is_long == 1, second, row // 256 * 256)
    freq_index = jnp.arange(HD // 2, dtype=F32)
    inverse = ROPE_BASE ** (-2.0 * freq_index / HD)
    angle = (row - offset).astype(F32)[:, None] * inverse[None, :]
    cosine, sine = jnp.cos(angle), jnp.sin(angle)
    return (
        jnp.concatenate([cosine] * 4, axis=1),
        jnp.concatenate([sine, sine, -sine, -sine], axis=1),
    )


def scatter_x_y(info, slots_x, slots_y):
    got_x = [slots_x[0]] + [send(slots_x[s], "x", s) for s in (1, 2, 3)]
    got_y = [slots_y[0]] + [send(slots_y[s], "y", s) for s in (1, 2, 3)]
    mid = fold(info, got_x, got_y)
    mid_x, mid_y = mid[:4], mid[4:]
    got_x = [mid_x[0]] + [send(mid_x[s], "y", s) for s in (1, 2, 3)]
    got_y = [mid_y[0]] + [send(mid_y[s], "x", s) for s in (1, 2, 3)]
    part = join(got_x, got_y)
    return add(part, send(part, "zl"))


def add(one, two):
    return (one.astype(F32) + two.astype(F32)).astype(BF)


def gather(part):
    return lax.all_gather(part, ("x", "y"), axis=0, tiled=False)


def shards(tokens, long_count, attn_gain, w_query, b_query, w_key, b_key, w_value, b_value,
           w_out, mlp_gain, w_gate, w_up, w_down, cotangent):
    at_x, at_y, at_c, at_t = (lax.axis_index(a) for a in ("x", "y", "c", "t"))
    info = jnp.stack([at_t, long_count[0], at_x, at_y, at_c]).astype(jnp.int32)
    gain_one = attn_gain.astype(F32)[None, :]
    gain_two = mlp_gain.astype(F32)[None, :]

    tok_rec = send(tokens, "t")
    half_out = lax.dynamic_slice(w_out, (at_c * SLAB, 0), (SLAB, D))
    half_out = send(after(half_out, tok_rec), "t")
    other_out = by_place(at_c, half_out, send(half_out, "c"))

    heads = w_query.reshape(D, HEADS, HD)
    heads = jnp.concatenate([heads, swapped(heads)], axis=-1).reshape(D, HEADS * 128)
    w_all = jnp.concatenate([heads, w_key, swapped(w_key), w_value, w_value], axis=1)
    bias = b_query.reshape(HEADS, HD)
    bias = jnp.concatenate([bias, swapped(bias)], axis=-1).reshape(HEADS * 128)
    b_all = jnp.concatenate([bias, b_key, swapped(b_key), b_value, b_value]).astype(F32)[None, :]
    w_cat = jnp.concatenate([w_query, w_key, jnp.zeros((D, HD), BF), w_value], axis=1)
    wo_dup = w_out.reshape(HEADS, HD, D)
    wo_dup = jnp.concatenate([wo_dup, wo_dup], axis=1).reshape(HEADS * 128, D)
    cosine, sine = tables(long_count[0])
    first_hid = at_c * STEP
    wg = lax.dynamic_slice(w_gate, (0, first_hid), (D, HID))
    wu = lax.dynamic_slice(w_up, (0, first_hid), (D, HID))
    wd = lax.dynamic_slice(w_down, (first_hid, 0), (HID, D))
    shared = (lax.iota(jnp.int32, HID) < 128) & (at_c == 1)
    wd = jnp.where(shared[:, None], jnp.zeros((), BF), wd)

    attn_in, rotated, value, stats, att_send, att_keep = attention(
        info, tokens, tok_rec, gain_one, w_all, b_all, cosine, sine
    )
    att_rec = send(att_send, "t")
    cot_rec = send(after(cotangent, half_out), "t")
    cot = by_place(at_t, cotangent, cot_rec)
    cot_other = send(cot, "c")
    g_x, g_y = turn(info, cot, cot_other)
    hidden, mlp_in = project(info, att_send, att_rec, w_out, other_out, tokens, tok_rec, gain_two)
    mlp_other = send(mlp_in, "c")
    m_x, m_y = turn(info, mlp_in, mlp_other)
    one = feed(True, mlp_in, mlp_other, cot, cot_other, m_x, m_y, g_x, wg, wu, wd, ())
    two = feed(False, mlp_in, mlp_other, cot, cot_other, m_x, m_y, g_y, wg, wu, wd, one[8:])
    out_own, out_other, dm_own, dm_other = two[8:]

    sum_one = scatter_x_y(info, one[:4], one[4:8])
    all_one = gather(sum_one)

    dm_sum = add(dm_own, send(dm_other, "c"))
    dm_rec = send(dm_sum, "t")
    out_sum = out_own.astype(F32) + send(out_other, "c").astype(F32)
    out_mine = lax.dynamic_slice(out_sum, (at_t * HALF, 0), (HALF, D))
    out_theirs = lax.dynamic_slice(out_sum, ((1 - at_t) * HALF, 0), (HALF, D)).astype(BF)
    hidden_mine = lax.dynamic_slice(hidden, (at_t * HALF, 0), (HALF, D))
    output = (hidden_mine + out_mine + send(out_theirs, "t").astype(F32)).astype(BF)

    sum_two = scatter_x_y(info, two[:4], two[4:8])
    all_two = gather(sum_two)

    grad_mid, da_own, da_send, pack_a, pack_b = back(
        info, dm_sum, dm_rec, cot, hidden, gain_two, tokens, tok_rec, gain_one, wo_dup, att_keep,
        rotated, value, stats, cosine, sine, attn_in, w_cat,
    )
    pack_send = jnp.where(at_c == 0, pack_b, pack_a)
    pack_keep = jnp.where(at_c == 0, pack_a, pack_b)
    pack = add(pack_keep, send(pack_send, "c"))
    pack = lax.psum_scatter(pack, ("x", "y"), scatter_dimension=0, tiled=True)
    pack = gather(add(pack, send(pack, "zl"))[0])

    da_rec = send(da_send, "t")
    field = tokens.astype(F32)
    factor = factor_of(field)
    normed = field * factor
    scaled = (da_own + da_rec.astype(F32)) * gain_one
    grad_tokens = grad_mid + factor * (
        scaled - normed * jnp.mean(scaled * normed, axis=-1, keepdims=True)
    )
    grad_tokens = grad_tokens.astype(BF)

    one_rec, two_rec, pack_rec = send(all_one, "c"), send(all_two, "c"), send(pack, "c")
    grad_w_gate, grad_w_up = wide(info, all_one, one_rec, all_two, two_rec)
    grad_w_down = tall(info, all_one, one_rec, all_two, two_rec)
    pack_a = jnp.where(at_c == 0, pack, pack_rec).astype(F32)
    pack_b = jnp.where(at_c == 0, pack_rec, pack).astype(F32)
    rows_a = pack_a[:, :PIECE].reshape(D, 512)
    rows_b = pack_b[:, :PIECE].reshape(D, 512)
    gains = jnp.concatenate([pack_a[1:3, PIECE], pack_b[1:3, PIECE, :384]], axis=1)
    gains = gains + send(gains, "t")
    return (
        output,
        grad_tokens,
        gains[0],
        rows_a[:, :448],
        pack_a[0, PIECE, :448],
        rows_a[:, 448:],
        pack_a[0, PIECE, 448:],
        rows_b[:, 448:],
        pack_b[0, PIECE, 448:],
        rows_b[:, :448].T,
        gains[1],
        grad_w_gate,
        grad_w_up,
        grad_w_down,
    )


def solution(mesh):
    fine = Mesh(mesh.devices.reshape(4, 2, 4, 2, 2), ("x", "zl", "y", "c", "t"))
    dp = ("x", "zl", "y", "c")
    rows, cols, split = P((*dp, "t"), None), P(None, "t"), P("t")
    down = P("t", None)
    return jax.shard_map(
        shards,
        mesh=fine,
        in_specs=(
            rows, P(dp), P(), cols, split, cols, split, cols, split, down, P(), cols, cols, down,
            rows,
        ),
        out_specs=(
            rows, rows, P(), cols, split, cols, split, cols, split, down, P(), cols, cols, down,
        ),
        check_vma=False,
    )
```

```python
import functools

import jax
import jax.numpy as jnp
import numpy as np
from jax import lax
from jax.experimental import pallas as pl
from jax.experimental.pallas import tpu as pltpu
from jax.sharding import Mesh
from jax.sharding import PartitionSpec as P

HD = 64
EPSILON = 1e-06
ROPE_BASE = 1000000.0
BF = jnp.bfloat16
F32 = jnp.float32

D = 896
HALF = 384
ROWS = 768
HEADS = 7
PIECE = 56
SLAB = 224
HID = 1280
SPLIT = 768
STEP = 1152
CHUNK = 256
MIB = 1024 * 1024

VM = pl.BlockSpec(memory_space=pltpu.VMEM)
SM = pl.BlockSpec(memory_space=pltpu.SMEM)


def sds(shape, dtype):
    return jax.ShapeDtypeStruct(shape, dtype)


def nn(a, b):
    return lax.dot_general(a, b, (((1,), (0,)), ((), ())), preferred_element_type=F32)


def nt(a, b):
    return lax.dot_general(a, b, (((1,), (1,)), ((), ())), preferred_element_type=F32)


def tn(a, b):
    return lax.dot_general(a, b, (((0,), (0,)), ((), ())), preferred_element_type=F32)


def factor_of(field):
    return lax.rsqrt(jnp.mean(field * field, axis=-1, keepdims=True) + EPSILON)


def params(mib):
    return pltpu.CompilerParams(vmem_limit_bytes=mib * MIB)


def cost(flops, size, trans=0):
    return pl.CostEstimate(flops=flops // 1000, bytes_accessed=size // 1000, transcendentals=trans // 1000)


def masks(is_long, keys_first=False):
    row = lax.broadcasted_iota(jnp.int32, (256, 256), 0)
    col = lax.broadcasted_iota(jnp.int32, (256, 256), 1)
    causal = jnp.where(row <= col if keys_first else col <= row, 0.0, -1e30).astype(F32)
    before = jnp.full((256, 256), jnp.where(is_long == 1, 0.0, -1e30).astype(F32))
    return causal, jnp.concatenate([before, causal], axis=0 if keys_first else 1)


def turns(ref, block, is_long):
    start = ref[:256, :]
    return jnp.where(is_long == 1, ref[256:, :], start) if block == 1 else start


SPANS = ((0, 0, 256), (256, 0, 512), (512, 512, 768))


def attention_kernel(info, tok_0, tok_1, gain, w_all, b_all, cosine, sine,
                     attn_in, rotated, value, stats, att_0, att_1, att_keep):
    for half, src in enumerate((tok_0, tok_1)):
        field = src[...].astype(F32)
        normed = (field * factor_of(field) * gain[...]).astype(BF)
        attn_in[HALF * half : HALF * half + HALF, :] = normed
    for block in range(3):
        rows = slice(256 * block, 256 * block + 256)
        lin = nt(attn_in[rows, :], w_all[...]) + b_all[...]
        cos_b, sin_b = turns(cosine, block, info[1]), turns(sine, block, info[1])
        for head in range(HEADS + 1):
            part = lin[:, 128 * head : 128 * head + 128]
            turned = part * cos_b + pltpu.roll(part, 64, 1) * sin_b
            rotated[rows, 128 * head : 128 * head + 128] = turned.astype(BF)
        value[rows, :] = lin[:, 1024:1152].astype(BF)
    causal, wide = masks(info[1])
    lane = lax.broadcasted_iota(jnp.int32, (256, 128), 1)
    for block, (first, low, high) in enumerate(SPANS):
        rows = slice(first, first + 256)
        mask = wide if block == 1 else causal
        keys = rotated[low:high, 1024 - 128 :]
        vals = value[low:high, :]
        kept = jnp.zeros((256, 128), F32)
        outs = []
        for head in range(HEADS):
            scores = nt(rotated[rows, 128 * head : 128 * head + 128], keys) * 0.0625 + mask
            top = jnp.max(scores, axis=-1, keepdims=True)
            expo = jnp.exp(scores - top)
            total = jnp.sum(expo, axis=-1, keepdims=True)
            kept = jnp.where(lane == head, top + jnp.log(total), kept)
            outs.append(nn(expo.astype(BF), vals) * (1.0 / total))
        stats[:, rows] = kept.T[:8, :]
        outs.append(jnp.zeros((256, 128), F32))
        for pair in range(4):
            both = jnp.where(lane < 64, outs[2 * pair], outs[2 * pair + 1])
            att_keep[rows, 128 * pair : 128 * pair + 128] = both.astype(BF)
    lane = lax.broadcasted_iota(jnp.int32, (64, 128), 1)
    for half, out in enumerate((att_0, att_1)):
        rows = slice(HALF * half, HALF * half + HALF)
        out[:HALF, :] = att_keep[rows, :384]
        for pair in range(3):
            low = HALF * half + 128 * pair
            left = att_keep[low : low + 64, 384:].astype(F32)
            right = pltpu.roll(att_keep[low + 64 : low + 128, 384:].astype(F32), 64, 1)
            out[HALF:, 128 * pair : 128 * pair + 128] = jnp.where(lane < 64, left, right).astype(BF)


def attention(info, tok_0, tok_1, gain, w_all, b_all, cosine, sine):
    return pl.pallas_call(
        attention_kernel,
        name="attention_forward",
        in_specs=[SM] + [VM] * 7,
        out_specs=[VM] * 7,
        out_shape=[
            sds((ROWS, D), BF),
            sds((ROWS, 1024), BF),
            sds((ROWS, 128), BF),
            sds((8, ROWS), F32),
            sds((448, 384), BF),
            sds((448, 384), BF),
            sds((ROWS, 512), BF),
        ],
        compiler_params=params(48),
        cost_estimate=cost(4 * 10**9, 12 * 10**6, 3 * 10**6),
    )(info, tok_0, tok_1, gain, w_all, b_all, cosine, sine)


def project_kernel(att_own, att_rec, wo_own, wo_rec, tok, gain, hidden, mlp_in, full):
    lane = lax.broadcasted_iota(jnp.int32, (64, 128), 1)
    field = tok[...].astype(F32)
    for att, weight in ((att_own, wo_own), (att_rec, wo_rec)):
        full[:, :384] = att[:HALF, :]
        for pair in range(3):
            both = att[HALF:, 128 * pair : 128 * pair + 128].astype(F32)
            low = 128 * pair
            full[low : low + 64, 384:] = jnp.where(lane < 64, both, 0.0).astype(BF)
            both = jnp.where(lane < 64, pltpu.roll(both, 64, 1), 0.0)
            full[low + 64 : low + 128, 384:] = both.astype(BF)
        field = field + nn(full[...], weight[...])
    hidden[...] = field
    mlp_in[...] = (field * factor_of(field) * gain[...]).astype(BF)


def project(att_own, att_rec, wo_own, wo_rec, tok, gain):
    return pl.pallas_call(
        project_kernel,
        name="project_norm",
        in_specs=[VM] * 6,
        out_specs=[VM] * 2,
        out_shape=[sds((HALF, D), F32), sds((HALF, D), BF)],
        scratch_shapes=[pltpu.VMEM((HALF, 512), BF)],
        compiler_params=params(32),
        cost_estimate=cost(7 * 10**8, 6 * 10**6),
    )(att_own, att_rec, wo_own, wo_rec, tok, gain)


def turn_kernel(info, own, rec, first, second):
    for at, src in enumerate((own, rec)):
        cols = slice(HALF * at, HALF * at + HALF)
        for slab in range(4):
            turned = src[:, SLAB * slab : SLAB * slab + SLAB].astype(F32).T.astype(BF)
            for mask, out in ((info[2], first), (info[3], second)):
                slot = lax.bitwise_xor(jnp.int32(slab), mask // 4)
                out[pl.ds(pl.multiple_of(slot * SLAB, SLAB), SLAB), cols] = turned


def turn(info, own, rec, weigh=10**6):
    return pl.pallas_call(
        turn_kernel,
        name="transpose_rows",
        in_specs=[SM] + [VM] * 2,
        out_specs=[VM] * 2,
        out_shape=[sds((D, 2 * HALF), BF)] * 2,
        compiler_params=params(32),
        cost_estimate=cost(weigh, 4 * 10**6),
    )(info, own, rec)


def flip_kernel(source, out):
    for block in range(3):
        rows = slice(256 * block, 256 * block + 256)
        out[:, rows] = source[rows, :].astype(F32).T.astype(BF)


def flip(source):
    return pl.pallas_call(
        flip_kernel,
        name="transpose_whole",
        in_specs=[VM],
        out_specs=VM,
        out_shape=sds((D, ROWS), BF),
        compiler_params=params(16),
        cost_estimate=cost(10**6, 3 * 10**6),
    )(source)


def order_kernel(info, own, rec, first, second):
    @pl.when(info[0] == 0)
    def _():
        first[...] = own[...]
        second[...] = rec[...]

    @pl.when(info[0] == 1)
    def _():
        first[...] = rec[...]
        second[...] = own[...]


def order(info, own, rec):
    return pl.pallas_call(
        order_kernel,
        name="order_rows",
        in_specs=[SM] + [VM] * 2,
        out_specs=[VM] * 2,
        out_shape=[sds(own.shape, own.dtype)] * 2,
        compiler_params=params(16),
        cost_estimate=cost(3 * 10**13, 10**6),
    )(info, own, rec)


def feed_kernel(info, m_own, m_rec, g_own, g_rec, wg, wu, wd_in, act, gate_g, up_g, *rest):
    ends, sums, wd = rest[:4], rest[4:8], rest[8]
    step = pl.program_id(0)
    wd[...] = wd_in[...]

    @pl.when((step == 0) & (info[4] == 1))
    def _():
        wd[:128, :] = jnp.zeros((128, D), BF)

    @pl.when(step == 0)
    def _():
        for total in sums:
            total[...] = jnp.zeros_like(total)

    for at, (m, g) in enumerate(((m_own, g_own), (m_rec, g_rec))):
        rows = slice(HALF * at, HALF * at + HALF)
        gate = nn(m[...], wg[...])
        up = nn(m[...], wu[...])
        grad = nt(g[...], wd[...])
        sig = 1.0 / (1.0 + jnp.exp(-gate))
        swish = gate * sig
        act[rows, :] = (swish * up).astype(BF)
        up_g[rows, :] = (grad * swish).astype(BF)
        gate_g[rows, :] = (grad * up * (sig + swish * (1.0 - sig))).astype(BF)
        sums[at][...] += nn(act[rows, :], wd[...])
        sums[2 + at][...] += nt(gate_g[rows, :], wg[...]) + nt(up_g[rows, :], wu[...])

    @pl.when(step == pl.num_programs(0) - 1)
    def _():
        for end, total in zip(ends, sums, strict=True):
            end[...] = total[...].astype(BF)


def whole(shape):
    zeros = (0,) * len(shape)
    return pl.BlockSpec(shape, lambda *_: zeros, pipeline_mode=pl.Buffered(1))


def feed(info, m_own, m_rec, g_own, g_rec, wg, wu, wd):
    rows = whole((HALF, D))

    def start(j, info):
        return pl.multiple_of(info[4] * STEP + j * CHUNK, 128)

    wide = pl.BlockSpec((pl.Element(D), pl.Element(CHUNK)), lambda j, info: (0, start(j, info)))
    tall = pl.BlockSpec((pl.Element(CHUNK), pl.Element(D)), lambda j, info: (start(j, info), 0))
    kept = pl.BlockSpec((2 * HALF, CHUNK), lambda j, info: (0, j))
    return pl.pallas_call(
        feed_kernel,
        name="feed_forward_and_back",
        grid_spec=pltpu.PrefetchScalarGridSpec(
            num_scalar_prefetch=1,
            grid=(HID // CHUNK,),
            in_specs=[rows] * 4 + [wide, wide, tall],
            out_specs=[kept] * 3 + [rows] * 4,
            scratch_shapes=[pltpu.VMEM((HALF, D), F32)] * 4 + [pltpu.VMEM((CHUNK, D), BF)],
        ),
        out_shape=[sds((2 * HALF, HID), BF)] * 3 + [sds((HALF, D), BF)] * 4,
        compiler_params=params(48),
        cost_estimate=cost(10**10, 20 * 10**6, 10**6),
    )(info, m_own, m_rec, g_own, g_rec, wg, wu, wd)


def weight_kernel(left_0, left_1, right_0, right_1, keep, give):
    product = nn(left_0[...], right_0[...]) + nn(left_1[...], right_1[...])
    for piece in range(8):
        low = PIECE * piece
        keep[piece] = product[low : low + PIECE, :].astype(BF)
        give[piece] = product[D // 2 + low : D // 2 + low + PIECE, :].astype(BF)


def weight_grad(left_0, left_1, right_0, right_1, chunk, first, count):
    left = whole((D, 2 * HALF))
    right = pl.BlockSpec((2 * HALF, chunk), lambda j: (0, j + first))
    eight = pl.BlockSpec((8, PIECE, chunk), lambda j: (0, 0, j))
    return pl.pallas_call(
        weight_kernel,
        name="weight_gradient",
        grid=(count,),
        in_specs=[left] * 2 + [right] * 2,
        out_specs=[eight] * 2,
        out_shape=[sds((8, PIECE, chunk * count), BF)] * 2,
        compiler_params=params(48),
        cost_estimate=cost(28 * 10**5 * chunk * count, 8 * 10**6),
    )(left_0, left_1, right_0, right_1)


def fold_kernel(plan, ways, info, *refs):
    ins = list(refs[: sum(count for group in plan for count, _, _ in group)])
    outs = list(refs[len(ins) :])
    for group in plan:
        out = [outs.pop(0) for _ in range(ways)]
        low = 0
        for count, mask, bits in group:
            terms = [ins.pop(0) for _ in range(count)]
            pieces, _, wide = terms[0].shape
            each = pieces // ways
            for at in range(pieces):
                piece = at
                if mask is not None:
                    piece = lax.bitwise_xor(jnp.int32(at), lax.bitwise_and(info[mask], bits))
                total = terms[0][piece].astype(F32)
                for term in terms[1:]:
                    total = total + term[piece].astype(F32)
                out[at // each][at % each, :, low : low + wide] = total.astype(BF)
            low += wide


def fold(info, ways, *groups, weigh=10**7):
    plan = [[(len(terms), mask, bits) for terms, mask, bits in group] for group in groups]
    ins = [ref for group in groups for terms, _, _ in group for ref in terms]
    shapes = []
    for group in groups:
        wide = sum(terms[0].shape[-1] for terms, _, _ in group)
        shapes += [sds((group[0][0][0].shape[0] // ways, PIECE, wide), BF)] * ways
    out = pl.pallas_call(
        functools.partial(fold_kernel, plan, ways),
        name="sum_parts",
        in_specs=[SM] + [VM] * len(ins),
        out_specs=[VM] * len(shapes),
        out_shape=shapes,
        compiler_params=params(40),
        cost_estimate=cost(weigh, 6 * 10**6),
    )(info, *ins)
    return [out[ways * at : ways * at + ways] for at in range(len(groups))]


def branch_kernel(info, dm_own_0, dm_own_1, dm_rec_0, dm_rec_1, cot_0, cot_1, hid_0, hid_1,
                  gain_two, wo_dup, grad_mid, branch, grad_att, sums):
    sum_two = jnp.zeros((1, D), F32)
    for half, (own, rec, cot, hid) in enumerate(
        ((dm_own_0, dm_rec_0, cot_0, hid_0), (dm_own_1, dm_rec_1, cot_1, hid_1))
    ):
        rows = slice(HALF * half, HALF * half + HALF)
        field = hid[...]
        factor = factor_of(field)
        normed = field * factor
        grad = own[...].astype(F32) + rec[...].astype(F32)
        scaled = grad * gain_two[...]
        middle = cot[...].astype(F32) + factor * (
            scaled - normed * jnp.mean(scaled * normed, axis=-1, keepdims=True)
        )
        branch[rows, :] = middle.astype(BF)
        part = jnp.sum(grad * normed, axis=0, keepdims=True)
        sum_two = jnp.where(info[0] == half, part, sum_two)

        @pl.when(info[0] == half)
        def _(middle=middle):
            grad_mid[...] = middle

    grad_att[...] = nt(branch[...], wo_dup[...]).astype(BF)
    sums[...] = sum_two


def branch_back(info, *args):
    return pl.pallas_call(
        branch_kernel,
        name="norm_and_projection_backward",
        in_specs=[SM] + [VM] * 10,
        out_specs=[VM] * 4,
        out_shape=[sds((HALF, D), F32), sds((ROWS, D), BF), sds((ROWS, D), BF), sds((1, D), F32)],
        compiler_params=params(48),
        cost_estimate=cost(10**9, 10**7),
    )(info, *args)


def back_kernel(blocks, info, grad_att, rotated, value, stats, cosine, sine, lin):
    causal, wide = masks(info[1], keys_first=True)
    lane = lax.broadcasted_iota(jnp.int32, (256, 128), 1)
    base = 256 * blocks[0]
    grad_k = [jnp.zeros((256, 128), F32) for _ in blocks]
    grad_v = [jnp.zeros((256, 128), F32) for _ in blocks]
    for block in blocks:
        first, low, high = SPANS[block]
        rows = slice(first, first + 256)
        to = slice(first - base, first - base + 256)
        mask = wide if block == 1 else causal
        keys = rotated[low:high, 896:1024]
        vals = value[low:high, :]
        cos_b, sin_b = turns(cosine, block, info[1]), turns(sine, block, info[1])
        turned = []
        for head in range(HEADS):
            cols = slice(128 * head, 128 * head + 128)
            query, grad_o = rotated[rows, cols], grad_att[rows, cols]
            chance = jnp.exp(nt(keys, query) * 0.0625 + mask - stats[head : head + 1, rows])
            grad_p = nt(vals, grad_o) * 0.5
            inner = jnp.sum(chance * grad_p, axis=0, keepdims=True)
            grad_s = (chance * (grad_p - inner)).astype(BF)
            low_p = chance.astype(BF)
            back = tn(grad_s, keys) * 0.125
            turned.append(back * cos_b - pltpu.roll(back, 64, 1) * sin_b)
            for at in range((high - low) // 256):
                part = slice(256 * at, 256 * at + 256)
                grad_k[(low - base) // 256 + at] += nn(grad_s[part, :], query)
                grad_v[(low - base) // 256 + at] += nn(low_p[part, :], grad_o)
        turned.append(jnp.zeros((256, 128), F32))
        for pair in range(4):
            right = pltpu.roll(turned[2 * pair + 1], 64, 1)
            lin[to, 128 * pair : 128 * pair + 128] = jnp.where(
                lane < 64, turned[2 * pair], right
            ).astype(BF)
    for at, block in enumerate(blocks):
        rows = slice(256 * at, 256 * at + 256)
        cos_b, sin_b = turns(cosine, block, info[1]), turns(sine, block, info[1])
        back = grad_k[at] * 0.125
        back = back * cos_b - pltpu.roll(back, 64, 1) * sin_b
        back = pltpu.roll(back, 64, 1).astype(BF)
        lin[rows, 384:512] = jnp.where(lane < 64, lin[rows, 384:512], back)
        lin[rows, 512:640] = jnp.where(lane < 64, 0.0, grad_v[at]).astype(BF)


def back(blocks, info, *args):
    return pl.pallas_call(
        functools.partial(back_kernel, blocks),
        name="attention_backward",
        in_specs=[SM] + [VM] * 6,
        out_specs=VM,
        out_shape=sds((256 * len(blocks), 640), BF),
        compiler_params=params(48),
        cost_estimate=cost(10**9, 10**7, 10**6),
    )(info, *args)


def last_kernel(info, branch, lin_a, lin_b, sum_two, att, attn_t, w_cat, tok_0, tok_1,
                da_own, da_send, pack_keep, pack_send, grad_in):
    grad_in[:512, :] = nn(lin_a[...], w_cat[...])
    grad_in[512:, :] = nn(lin_b[...], w_cat[...])
    mine = pl.multiple_of(info[0] * HALF, HALF)
    other = pl.multiple_of((1 - info[0]) * HALF, HALF)
    da_own[...] = grad_in[pl.ds(mine, HALF), :]
    da_send[...] = grad_in[pl.ds(other, HALF), :].astype(BF)
    sum_one = jnp.zeros((1, D), F32)
    for half, src in enumerate((tok_0, tok_1)):
        field = src[...].astype(F32)
        grad = grad_in[HALF * half : HALF * half + HALF, :]
        sum_one = sum_one + jnp.sum(grad * (field * factor_of(field)), axis=0, keepdims=True)
    sum_b = jnp.sum(lin_a[...].astype(F32), axis=0, keepdims=True)
    sum_b = sum_b + jnp.sum(lin_b[...].astype(F32), axis=0, keepdims=True)
    grad_w = nn(attn_t[:, :512], lin_a[...]) + nn(attn_t[:, 512:], lin_b[...])
    grad_o = tn(branch[...], att[...])
    first_w = grad_w[:, :512]
    second_w = jnp.concatenate([grad_o[:, :384], grad_o[:, 384:] + grad_w[:, 512:]], axis=1)
    sum_two = sum_two[...]
    extra_a = {0: sum_b[:, :512], 1: sum_one[:, :512], 2: sum_two[:, :512]}
    extra_b = {0: sum_b[:, 512:], 1: sum_one[:, 512:], 2: sum_two[:, 512:]}

    def lines(extra):
        count = extra.shape[1] // 128
        parts = [extra[:, 128 * at : 128 * at + 128] for at in range(count)]
        return jnp.concatenate([*parts, jnp.zeros((PIECE - count, 128), F32)], axis=0)

    for piece in range(16):
        rows = slice(PIECE * piece, PIECE * piece + PIECE)
        packs = []
        for grads, extra in ((first_w, extra_a), (second_w, extra_b)):
            more = lines(extra[piece]) if piece in extra else jnp.zeros((PIECE, 128), F32)
            packs.append((grads[rows, :], more))
        for at, cols in ((0, slice(0, 512)), (1, slice(512, 640))):
            low, high = packs[0][at], packs[1][at]
            pack_keep[piece, :, cols] = jnp.where(info[4] == 0, low, high).astype(BF)
            pack_send[piece, :, cols] = jnp.where(info[4] == 0, high, low).astype(BF)


def last(info, *args):
    return pl.pallas_call(
        last_kernel,
        name="attention_weight_gradients",
        in_specs=[SM] + [VM] * 9,
        out_specs=[VM] * 4,
        out_shape=[
            sds((HALF, D), F32),
            sds((HALF, D), BF),
            sds((16, PIECE, 640), BF),
            sds((16, PIECE, 640), BF),
        ],
        scratch_shapes=[pltpu.VMEM((ROWS, D), F32)],
        compiler_params=params(60),
        cost_estimate=cost(3 * 10**9, 16 * 10**6),
    )(info, *args)


def wide_kernel(got, info, own, other, *refs):
    out, stage, sems = refs[-3:]
    copies = []
    for at, (slot, src) in enumerate(((2, own), (5, other))):
        half = lax.bitwise_xor(info[slot] // 8, got)
        core = lax.rem(info[4] + at, 2)
        for piece in range(8):
            stage[at, piece] = src[piece].astype(F32)
            place = lax.bitwise_xor(jnp.int32(piece), lax.rem(info[slot], 8))
            sem = sems.at[at, piece]
            first = pltpu.make_async_copy(
                stage.at[at, piece], out.at[half, place, :, pl.ds(0, HID)], sem
            )
            second = pltpu.make_async_copy(
                stage.at[at, piece, :, pl.ds(128, HID - 128)],
                out.at[half, place, :, pl.ds(HID, HID - 128)],
                sem,
            )
            pl.when(core == 0)(first.start)
            pl.when(core == 1)(second.start)
            copies.append((core, first, second))
    for core, first, second in copies:
        pl.when(core == 0)(first.wait)
        pl.when(core == 1)(second.wait)


def lanes(pieces, low, count):
    return pl.BlockSpec(
        (pl.Element(pieces), pl.Element(PIECE), pl.Element(count)), lambda _: (0, 0, low)
    )


def wide(info, part, own, other, before=None):
    info = jnp.stack([info[0], info[1], info[2 + part], info[3], info[4], info[5 + part], info[6]])
    more = [] if before is None else [before]
    anywhere = pl.BlockSpec(memory_space=pl.ANY)
    return pl.pallas_call(
        functools.partial(wide_kernel, len(more)),
        name="gradients_wide",
        grid=(1,),
        in_specs=[SM] + [lanes(8, 0, HID)] * 2 + [anywhere] * len(more),
        out_specs=anywhere,
        out_shape=sds((2, 8, PIECE, 2432), F32),
        scratch_shapes=[pltpu.VMEM((2, 8, PIECE, HID), F32), pltpu.SemaphoreType.DMA((2, 8))],
        input_output_aliases={3: 0} if more else {},
        compiler_params=params(48),
        cost_estimate=cost(10**7, 14 * 10**6),
    )(info, own, other, *more)


def model_order(info, mask, own, got, cols):
    pieces = []
    for q in range(16):
        place = lax.bitwise_xor(jnp.int32(q), info[mask])
        at = lax.rem(place, 8)
        ours, theirs = own[at, :, cols].astype(F32), got[at, :, cols].astype(F32)
        pieces.append(jnp.where(place < 8, ours, theirs))
    return jnp.concatenate(pieces, axis=0)


def tall_kernel(info, *refs):
    down, stage, sems = refs[-3:]
    copies = []
    for step in range(19):
        tile = step if step < 10 else step - 9
        part = int(tile >= SPLIT // 128)
        own, got, other, other_got = refs[4 * part : 4 * part + 4]
        low = 128 * tile - SPLIT * part
        cols = slice(low, low + 128)

        def ours(step=step, part=part, own=own, got=got, cols=cols):
            stage[step] = model_order(info, 2 + part, own, got, cols).T

        def theirs(step=step, part=part, own=other, got=other_got, cols=cols):
            stage[step] = model_order(info, 5 + part, own, got, cols).T

        pl.when((info[4] == 0) == (step < 10))(ours)
        pl.when((info[4] == 0) != (step < 10))(theirs)
        rows = pl.ds(128 * step, 128)
        copies.append(pltpu.make_async_copy(stage.at[step], down.at[rows, :], sems.at[step]))
        copies[-1].start()
    for copy in copies:
        copy.wait()


def tall(info, first, second):
    return pl.pallas_call(
        tall_kernel,
        name="gradients_tall",
        grid=(1,),
        in_specs=[SM] + [lanes(8, 0, SPLIT)] * 4 + [lanes(8, 0, HID - SPLIT)] * 4,
        out_specs=pl.BlockSpec(memory_space=pl.ANY),
        out_shape=sds((2432, D), F32),
        scratch_shapes=[pltpu.VMEM((19, 128, D), F32), pltpu.SemaphoreType.DMA((19,))],
        compiler_params=params(48),
        cost_estimate=cost(10**7, 14 * 10**6),
    )(info, *first, *second)


def small_kernel(info, own, got, other, other_got, query, key, value, out, extras):
    for first in (True, False):
        here = (info[4] == 0) == first

        def write(mask, one, two, first=first):
            for tile in range(4):
                turned = model_order(info, mask, one, two, slice(128 * tile, 128 * tile + 128)).T
                big, little = (query, key) if first else (out, value)
                if tile < 3:
                    big[128 * tile : 128 * tile + 128, :] = turned
                else:
                    big[384:, :] = turned[:64, :]
                    little[...] = turned[64:, :]
            more = model_order(info, mask, one, two, slice(512, 640))
            for piece in range(3):
                extras[0 if first else 1, piece] = more[PIECE * piece : PIECE * piece + 8, :]

        @pl.when(here)
        def _(write=write):
            write(3, own, got)

        @pl.when(jnp.logical_not(here))
        def _(write=write):
            write(6, other, other_got)


def small(info, *arrays):
    kept = [(448, D), (64, D), (64, D), (448, D), (2, 3, 8, 128)]
    return pl.pallas_call(
        small_kernel,
        name="gradients_small",
        grid=(1,),
        in_specs=[SM] + [lanes(8, HID - SPLIT, 640)] * 4,
        out_specs=[VM] * len(kept),
        out_shape=[sds(shape, F32) for shape in kept],
        compiler_params=params(40),
        cost_estimate=cost(10**7, 6 * 10**6),
    )(info, *arrays)


def send(field, axis, shift=1):
    size = lax.axis_size(axis)
    return lax.ppermute(field, axis, [(i, (i + shift) % size) for i in range(size)])


def after(field, *others):
    return lax.optimization_barrier((field, *others))[0]


def after_all(fields, *others):
    return lax.optimization_barrier((*fields, *others))[: len(fields)]


def in_order(place, own, rec):
    first = place == 0
    return jnp.where(first, own, rec), jnp.where(first, rec, own)


def swapped(weight, axis=-1):
    first, second = jnp.split(weight, 2, axis=axis)
    return jnp.concatenate([-second, first], axis=axis)


def tables():
    freq_index = np.arange(HD // 2, dtype=np.float32)
    inverse = np.float32(ROPE_BASE) ** (np.float32(-2.0) * freq_index / np.float32(HD))
    angle = np.arange(512, dtype=np.float32)[:, None] * inverse.astype(np.float32)[None, :]
    cosine, sine = np.cos(angle), np.sin(angle)
    return (
        jnp.asarray(np.concatenate([cosine] * 4, axis=1)),
        jnp.asarray(np.concatenate([sine, sine, -sine, -sine], axis=1)),
    )


ORDERS = (
    (("x", "a"), ("x", "b"), ("y", "a"), ("y", "b")),
    (("x", "b"), ("x", "a"), ("y", "b"), ("y", "a")),
), (
    (("y", "a"), ("y", "b"), ("x", "a"), ("x", "b")),
    (("y", "b"), ("y", "a"), ("x", "b"), ("x", "a")),
)
CHIPS = ("x", "zl", "y", "c")


def bit(place, kind):
    return (place ^ (place >> 1)) & 1 if kind == "a" else place >> 1


def mask_of(part, core, places):
    mask = 0
    for axis, kind in ORDERS[part][core]:
        mask = 2 * mask + bit(places[axis], kind)
    return mask


def swap(field, part, *steps):
    pairs = []
    for x in range(4):
        for zl in range(2):
            for y in range(4):
                for c in range(2):
                    to = {"x": x, "y": y}
                    for axis, kind in (ORDERS[part][c][step] for step in steps):
                        to[axis] = to[axis] ^ 1 if kind == "a" else 3 - to[axis]
                    here = ((x * 2 + zl) * 4 + y) * 2 + c
                    pairs.append((here, ((to["x"] * 2 + zl) * 4 + to["y"]) * 2 + c))
    return lax.ppermute(field, CHIPS, pairs)


def swap_two(one, two, step):
    return swap(one, 0, step), swap(two, 1, step)


def spread(one, two, one_r, two_r):
    one, two = jnp.concatenate([one, one_r]), jnp.concatenate([two, two_r])
    return lax.optimization_barrier((one, two))


def add(one, two):
    return (one.astype(F32) + two.astype(F32)).astype(BF)


def shards(tokens, long_count, attn_gain, w_query, b_query, w_key, b_key, w_value, b_value,
           w_out, mlp_gain, w_gate, w_up, w_down, cotangent):
    at_x, at_y, at_c, at_t = (lax.axis_index(a) for a in ("x", "y", "c", "t"))
    places = {"x": at_x, "y": at_y}
    masks_0 = [mask_of(part, 0, places) for part in (0, 1)]
    masks_1 = [mask_of(part, 1, places) for part in (0, 1)]
    mine = [jnp.where(at_c == 0, a, b) for a, b in zip(masks_0, masks_1, strict=True)]
    theirs = [jnp.where(at_c == 0, b, a) for a, b in zip(masks_0, masks_1, strict=True)]
    info = jnp.stack([at_t, long_count[0], *mine, at_c, *theirs]).astype(jnp.int32)
    gain_one = attn_gain.astype(F32)[None, :]
    gain_two = mlp_gain.astype(F32)[None, :]

    tok_rec = send(tokens, "t")
    half_out = lax.dynamic_slice(w_out, (at_c * SLAB, 0), (SLAB, D))
    half_out = send(after(half_out, tok_rec), "t")
    cot_rec = send(after(cotangent, tok_rec), "t")

    wq, wk, wv = w_query.T, w_key.T, w_value.T
    heads = wq.reshape(HEADS, HD, D)
    heads = jnp.concatenate([heads, swapped(heads, 1)], axis=1).reshape(HEADS * 128, D)
    w_all = jnp.concatenate([heads, wk, swapped(wk, 0), wv, wv], axis=0)
    bias = b_query.reshape(HEADS, HD)
    bias = jnp.concatenate([bias, swapped(bias)], axis=-1).reshape(HEADS * 128)
    b_all = jnp.concatenate([bias, b_key, swapped(b_key), b_value, b_value]).astype(F32)[None, :]
    cosine, sine = tables()
    tok_0, tok_1 = in_order(at_t, tokens, tok_rec)
    attn_in, rotated, value, stats, att_0, att_1, att_keep = attention(
        info, tok_0, tok_1, gain_one, w_all, b_all, cosine, sine
    )
    rec_0 = send(att_0, "t")
    rec_1 = send(att_1, "t")

    half_out, wq, w_out, _ = lax.optimization_barrier((half_out, wq, w_out, att_0))
    half_out = in_order(at_c, half_out, send(half_out, "c"))
    no_rows = jnp.zeros((HD, D), BF)
    other_out = jnp.concatenate([*half_out, no_rows])
    this_out = jnp.concatenate([w_out, no_rows])
    cot_0, cot_1 = order(info, cotangent, cot_rec)
    cot_0_rec, cot_1_rec = send(cot_0, "c"), send(cot_1, "c")
    w_cat = jnp.concatenate([wq, wk, jnp.zeros((HD, D), BF), wv], axis=0)
    wo_dup = w_out.reshape(HEADS, HD, D)
    wo_dup = jnp.concatenate([wo_dup, wo_dup], axis=1).reshape(HEADS * 128, D)
    attn_t = flip(attn_in)
    rec_0, w_cat, wo_dup, attn_t, cot_0_rec, cot_1_rec = lax.optimization_barrier(
        (rec_0, w_cat, wo_dup, attn_t, cot_0_rec, cot_1_rec)
    )

    hid_0, m_0 = project(att_0, rec_0, this_out, other_out, tok_0, gain_two)
    m_0_rec = send(m_0, "c")
    g_0x, g_0y = turn(info, after(cot_0, m_0), cot_0_rec)
    act_0, gate_0, up_0, out_0, out_0_oth, dm_0, dm_0_oth = feed(
        info, m_0, after(m_0_rec, g_0x), cot_0, cot_0_rec, w_gate, w_up, w_down
    )
    hid_1, m_1 = project(att_1, after(rec_1, act_0), this_out, other_out, tok_1, gain_two)
    m_1_rec = send(m_1, "c")
    m_0x, m_0y = turn(info, after(m_0, m_1), m_0_rec)
    dm_0 = add(dm_0, after(send(dm_0_oth, "c"), m_0x))
    dm_0_rec = send(dm_0, "t")
    act_1, gate_1, up_1, out_1, out_1_oth, dm_1, dm_1_oth = feed(
        info, after(m_1, dm_0), m_1_rec, cot_1, cot_1_rec, w_gate, w_up, w_down
    )
    m_1x, m_1y = turn(info, after(m_1, dm_1, dm_0_rec), m_1_rec)
    dm_1 = add(dm_1, after(send(dm_1_oth, "c"), m_1x))
    dm_1_rec = send(dm_1, "t")

    gate_k, gate_g = weight_grad(m_0x, m_1x, gate_0, after(gate_1, dm_1, dm_0_rec), CHUNK, 0, 5)
    gate_r = swap(gate_g, 0, 0)
    up_k, up_g = weight_grad(m_0y, m_1y, up_0, after(up_1, gate_g), CHUNK, 0, 5)
    up_r = swap(up_g, 1, 0)
    g_1x, g_1y = turn(info, after(cot_1, up_g), cot_1_rec, 3 * 10**13)
    low_k, low_g = weight_grad(g_0x, g_1x, act_0, after(act_1, dm_1_rec), CHUNK, 0, 3)
    high_k, high_g = weight_grad(g_0y, g_1y, act_0, after(act_1, low_g), CHUNK, 3, 2)
    grad_mid, branch, grad_att, sum_two = branch_back(
        info, dm_0, dm_1, dm_0_rec, after(dm_1_rec, high_g), cot_0, cot_1, hid_0, hid_1,
        gain_two, wo_dup,
    )
    (gate_k, gate_g), (up_k, up_g) = fold(
        info, 2, [((gate_k, after(gate_r, grad_att)), None, 0)], [((up_k, up_r), None, 0)]
    )
    gate_r, up_r = swap_two(gate_g, up_g, 1)
    low_r, high_r = swap_two(*after_all((low_g, high_g), gate_g), 0)

    lin_a = back((0, 1), info, after(grad_att, gate_g), rotated, value, stats, cosine, sine)
    (gate_k, gate_g), (up_k, up_g) = fold(
        info, 2, [((gate_k, after(gate_r, lin_a)), 2, 3)], [((up_k, up_r), 3, 3)]
    )
    gate_r, up_r = swap_two(gate_g, up_g, 2)
    (low_k, low_g), (high_k, high_g) = fold(
        info, 2, [((low_k, after(low_r, gate_g)), None, 0)], [((high_k, high_r), None, 0)]
    )
    low_r, high_r = swap_two(low_g, high_g, 1)
    lin_b = back((2,), info, after(grad_att, low_g), rotated, value, stats, cosine, sine)
    (gate_k, gate_g), (up_k, up_g) = fold(
        info, 2, [((gate_k, after(gate_r, lin_b)), None, 0)], [((up_k, up_r), None, 0)]
    )
    gate_r, up_r = swap_two(gate_g, up_g, 3)
    (low_k, low_g), (high_k, high_g) = fold(
        info, 2, [((low_k, after(low_r, gate_g)), 2, 3)], [((high_k, high_r), 3, 3)]
    )
    low_r, high_r = swap_two(low_g, high_g, 2)
    da_own, da_send, pack_k, pack_g = last(
        info, branch, after(lin_a, low_g), lin_b, sum_two, att_keep, attn_t, w_cat, tok_0, tok_1
    )
    pack_r = send(pack_g, "c")
    da_rec = send(da_send, "t")

    ((first,),) = fold(
        info, 1, [((gate_k, after(gate_r, pack_g)), None, 0), ((up_k, up_r), None, 0)]
    )
    first_r = send(first, "zl")
    (low_k, low_g), (high_k, high_g) = fold(
        info,
        2,
        [((low_k, after(low_r, first)), None, 0)],
        [((high_k, high_r), None, 0)],
        weigh=3 * 10**13,
    )
    low_r, high_r = swap_two(low_g, high_g, 3)
    ((pack_k, pack_g),) = fold(info, 2, [((pack_k, after(pack_r, low_g)), 3, 15)])
    pack_r = swap(pack_g, 1, 0)
    first = add(first, after(first_r, pack_g))
    gate, up = first[..., :HID], first[..., HID:]
    gate_r, up_r = swap_two(gate, up, 3)
    ((pack_k, pack_g),) = fold(info, 2, [((pack_k, after(pack_r, gate)), None, 0)])
    pack_r = swap(pack_g, 1, 1)
    ((pack_k, pack_g),) = fold(info, 2, [((pack_k, pack_r), None, 0)])
    pack_r = swap(pack_g, 1, 2)
    gate, up = spread(gate, up, after(gate_r, pack_g), up_r)
    gate_r, up_r = swap_two(gate, up, 2)
    ((pack_k, pack_g),) = fold(info, 2, [((pack_k, after(pack_r, gate)), None, 0)])
    pack_r = swap(pack_g, 1, 3)
    ((second,),) = fold(
        info,
        1,
        [((low_k, low_r), None, 0), ((high_k, high_r), None, 0), ((pack_k, pack_r), None, 0)],
    )
    second_r = send(second, "zl")

    field = tokens.astype(F32)
    factor = factor_of(field)
    normed = field * factor
    scaled = (da_own + after(da_rec, second).astype(F32)) * gain_one
    grad_tokens = grad_mid + factor * (
        scaled - normed * jnp.mean(scaled * normed, axis=-1, keepdims=True)
    )
    grad_tokens = grad_tokens.astype(BF)

    gate, up = spread(gate, up, after(gate_r, second, grad_tokens), up_r)
    gate_r, up_r = swap_two(gate, up, 1)
    second = add(second, after(second_r, gate))
    low, high = second[..., :SPLIT], second[..., SPLIT:]
    low_r, high_r = swap_two(low, high, 3)

    out_rec = send(after(jnp.concatenate([out_0_oth, out_1_oth]), lin_b), "c")
    out_rec = after(out_rec, low)
    mine, theirs = in_order(at_t, add(out_0, out_rec[:HALF]), add(out_1, out_rec[HALF:]))
    theirs_rec = send(theirs, "t")

    gate, up = spread(gate, up, after(gate_r, mine), up_r)
    gate_r, up_r = swap_two(gate, up, 0)
    gate_c = send(gate, "c")
    up_c = send(after(up, gate_c), "c")
    low, high = spread(low, high, after(low_r, gate), high_r)
    low_r, high_r = swap_two(low, high, 2)
    grad_w_gate = wide(info, 0, gate, after(gate_c, low))
    grad_w_up = wide(info, 1, up, after(up_c, grad_w_gate))
    low, high = spread(low, high, after(low_r, grad_w_up), high_r)
    low_r, high_r = swap_two(low, high, 1)
    gate_r, up_r = after_all((gate_r, up_r), low)
    gate_c = send(gate_r, "c")
    up_c = send(after(up_r, gate_c), "c")
    hidden = jnp.where(at_t == 0, hid_0, hid_1)
    theirs_rec = after(theirs_rec, low)
    output = (hidden + mine.astype(F32) + theirs_rec.astype(F32)).astype(BF)
    low, high = spread(low, high, after(low_r, output), high_r)
    low_r, high_r = swap_two(low, high, 0)
    grad_w_gate = wide(info, 0, gate_r, after(gate_c, low), grad_w_gate)
    grad_w_up = wide(info, 1, up_r, after(up_c, grad_w_gate), grad_w_up)
    low_c, high_c = send(low, "c"), send(high, "c")
    low_r, high_r = after_all((low_r, high_r), grad_w_up)
    low = low, low_r, low_c, send(low_r, "c")
    high = high, high_r, high_c, send(high_r, "c")
    grad_wq, grad_wk, grad_wv, grad_wo, extras = small(info, *high)
    grad_w_down = tall(info, low, high)
    grad_w_gate, grad_w_up = grad_w_gate.reshape(D, 2432), grad_w_up.reshape(D, 2432)
    gains = extras[:, 1:].reshape(2, 2, 1024)
    gains = jnp.concatenate([gains[0, :, :512], gains[1, :, :384]], axis=1)
    gains = gains + send(gains, "t")
    biases = extras[0, 0, :4].reshape(512)

    return (
        output,
        grad_tokens,
        gains[0],
        grad_wq.T,
        biases[:448],
        grad_wk.T,
        biases[448:],
        grad_wv.T,
        extras[1, 0, 0, 64:],
        grad_wo,
        gains[1],
        grad_w_gate,
        grad_w_up,
        grad_w_down,
    )


def solution(mesh):
    fine = Mesh(mesh.devices.reshape(4, 2, 4, 2, 2), ("x", "zl", "y", "c", "t"))
    dp = ("x", "zl", "y", "c")
    rows, cols, split = P((*dp, "t"), None), P(None, "t"), P("t")
    down = P("t", None)
    return jax.shard_map(
        shards,
        mesh=fine,
        in_specs=(
            rows, P(dp), P(), cols, split, cols, split, cols, split, down, P(), cols, cols, down,
            rows,
        ),
        out_specs=(
            rows, rows, P(), cols, split, cols, split, cols, split, down, P(), cols, cols, down,
        ),
        check_vma=False,
    )
```

```python
import functools

import jax
import jax.numpy as jnp
import numpy as np
from jax import lax
from jax.experimental import pallas as pl
from jax.experimental.pallas import tpu as pltpu
from jax.sharding import Mesh
from jax.sharding import PartitionSpec as P

HD = 64
EPSILON = 1e-06
ROPE_BASE = 1000000.0
BF = jnp.bfloat16
F32 = jnp.float32

D = 896
HALF = 384
ROWS = 768
HEADS = 7
PIECE = 56
SLAB = 224
HID = 1280
SPLIT = 512
STEP = 1152
CHUNK = 256
MIB = 1024 * 1024

VM = pl.BlockSpec(memory_space=pltpu.VMEM)
SM = pl.BlockSpec(memory_space=pltpu.SMEM)


def sds(shape, dtype):
    return jax.ShapeDtypeStruct(shape, dtype)


def nn(a, b):
    return lax.dot_general(a, b, (((1,), (0,)), ((), ())), preferred_element_type=F32)


def nt(a, b):
    return lax.dot_general(a, b, (((1,), (1,)), ((), ())), preferred_element_type=F32)


def tn(a, b):
    return lax.dot_general(a, b, (((0,), (0,)), ((), ())), preferred_element_type=F32)


def factor_of(field):
    return lax.rsqrt(jnp.mean(field * field, axis=-1, keepdims=True) + EPSILON)


def params(mib):
    return pltpu.CompilerParams(vmem_limit_bytes=mib * MIB)


def cost(flops, size, trans=0):
    return pl.CostEstimate(flops=flops // 1000, bytes_accessed=size // 1000, transcendentals=trans // 1000)


def masks(is_long, keys_first=False):
    row = lax.broadcasted_iota(jnp.int32, (256, 256), 0)
    col = lax.broadcasted_iota(jnp.int32, (256, 256), 1)
    causal = jnp.where(row <= col if keys_first else col <= row, 0.0, -1e30).astype(F32)
    before = jnp.full((256, 256), jnp.where(is_long == 1, 0.0, -1e30).astype(F32))
    return causal, jnp.concatenate([before, causal], axis=0 if keys_first else 1)


def turns(ref, block, is_long):
    start = ref[:256, :]
    return jnp.where(is_long == 1, ref[256:, :], start) if block == 1 else start


SPANS = ((0, 0, 256), (256, 0, 512), (512, 512, 768))


def attention_kernel(info, tok_0, tok_1, gain, w_all, b_all, cosine, sine,
                     attn_in, rotated, value, stats, att_0, att_1, att_keep):
    for half, src in enumerate((tok_0, tok_1)):
        field = src[...].astype(F32)
        normed = (field * factor_of(field) * gain[...]).astype(BF)
        attn_in[HALF * half : HALF * half + HALF, :] = normed
    for block in range(3):
        rows = slice(256 * block, 256 * block + 256)
        lin = nt(attn_in[rows, :], w_all[...]) + b_all[...]
        cos_b, sin_b = turns(cosine, block, info[1]), turns(sine, block, info[1])
        for head in range(HEADS + 1):
            part = lin[:, 128 * head : 128 * head + 128]
            turned = part * cos_b + pltpu.roll(part, 64, 1) * sin_b
            rotated[rows, 128 * head : 128 * head + 128] = turned.astype(BF)
        value[rows, :] = lin[:, 1024:1152].astype(BF)
    causal, wide = masks(info[1])
    lane = lax.broadcasted_iota(jnp.int32, (256, 128), 1)
    for block, (first, low, high) in enumerate(SPANS):
        rows = slice(first, first + 256)
        mask = wide if block == 1 else causal
        keys = rotated[low:high, 1024 - 128 :]
        vals = value[low:high, :]
        kept = jnp.zeros((256, 128), F32)
        outs = []
        for head in range(HEADS):
            scores = nt(rotated[rows, 128 * head : 128 * head + 128], keys) * 0.0625 + mask
            top = jnp.max(scores, axis=-1, keepdims=True)
            expo = jnp.exp(scores - top)
            total = jnp.sum(expo, axis=-1, keepdims=True)
            kept = jnp.where(lane == head, top + jnp.log(total), kept)
            outs.append(nn(expo.astype(BF), vals) * (1.0 / total))
        stats[:, rows] = kept.T[:8, :]
        outs.append(jnp.zeros((256, 128), F32))
        for pair in range(4):
            both = jnp.where(lane < 64, outs[2 * pair], outs[2 * pair + 1])
            att_keep[rows, 128 * pair : 128 * pair + 128] = both.astype(BF)
    lane = lax.broadcasted_iota(jnp.int32, (64, 128), 1)
    for half, out in enumerate((att_0, att_1)):
        rows = slice(HALF * half, HALF * half + HALF)
        out[:HALF, :] = att_keep[rows, :384]
        for pair in range(3):
            low = HALF * half + 128 * pair
            left = att_keep[low : low + 64, 384:].astype(F32)
            right = pltpu.roll(att_keep[low + 64 : low + 128, 384:].astype(F32), 64, 1)
            out[HALF:, 128 * pair : 128 * pair + 128] = jnp.where(lane < 64, left, right).astype(BF)


def attention(info, tok_0, tok_1, gain, w_all, b_all, cosine, sine):
    return pl.pallas_call(
        attention_kernel,
        name="attention_forward",
        in_specs=[SM] + [VM] * 7,
        out_specs=[VM] * 7,
        out_shape=[
            sds((ROWS, D), BF),
            pltpu.HBM((ROWS, 1024), BF),
            pltpu.HBM((ROWS, 128), BF),
            pltpu.HBM((8, ROWS), F32),
            sds((448, 384), BF),
            sds((448, 384), BF),
            pltpu.HBM((ROWS, 512), BF),
        ],
        compiler_params=params(26),
        cost_estimate=cost(4 * 10**9, 12 * 10**6, 3 * 10**6),
    )(info, tok_0, tok_1, gain, w_all, b_all, cosine, sine)


def project_kernel(att_own, att_rec, wo_own, wo_rec, tok, gain, hidden, mlp_in, full):
    lane = lax.broadcasted_iota(jnp.int32, (64, 128), 1)
    field = tok[...].astype(F32)
    for att, weight in ((att_own, wo_own), (att_rec, wo_rec)):
        full[:, :384] = att[:HALF, :]
        for pair in range(3):
            both = att[HALF:, 128 * pair : 128 * pair + 128].astype(F32)
            low = 128 * pair
            full[low : low + 64, 384:] = jnp.where(lane < 64, both, 0.0).astype(BF)
            both = jnp.where(lane < 64, pltpu.roll(both, 64, 1), 0.0)
            full[low + 64 : low + 128, 384:] = both.astype(BF)
        field = field + nn(full[...], weight[...])
    hidden[...] = field
    mlp_in[...] = (field * factor_of(field) * gain[...]).astype(BF)


def project(att_own, att_rec, wo_own, wo_rec, tok, gain):
    return pl.pallas_call(
        project_kernel,
        name="project_norm",
        in_specs=[VM] * 6,
        out_specs=[VM] * 2,
        out_shape=[pltpu.HBM((HALF, D), F32), sds((HALF, D), BF)],
        scratch_shapes=[pltpu.VMEM((HALF, 512), BF)],
        compiler_params=params(14),
        cost_estimate=cost(7 * 10**8, 6 * 10**6),
    )(att_own, att_rec, wo_own, wo_rec, tok, gain)


def turn_kernel(info, own, rec, first, second):
    for at, src in enumerate((own, rec)):
        cols = slice(HALF * at, HALF * at + HALF)
        for slab in range(4):
            turned = src[:, SLAB * slab : SLAB * slab + SLAB].astype(F32).T.astype(BF)
            for mask, out in ((info[2], first), (info[3], second)):
                slot = lax.bitwise_xor(jnp.int32(slab), mask // 4)
                out[pl.ds(pl.multiple_of(slot * SLAB, SLAB), SLAB), cols] = turned


def turn(info, own, rec, weigh=10**6):
    return pl.pallas_call(
        turn_kernel,
        name="transpose_rows",
        in_specs=[SM] + [VM] * 2,
        out_specs=[VM] * 2,
        out_shape=[pltpu.HBM((D, 2 * HALF), BF)] * 2,
        compiler_params=params(14),
        cost_estimate=cost(weigh, 4 * 10**6),
    )(info, own, rec)


def flip_kernel(source, out):
    for block in range(3):
        rows = slice(256 * block, 256 * block + 256)
        out[:, rows] = source[rows, :].astype(F32).T.astype(BF)


def flip(source):
    return pl.pallas_call(
        flip_kernel,
        name="transpose_whole",
        in_specs=[VM],
        out_specs=VM,
        out_shape=pltpu.HBM((D, ROWS), BF),
        compiler_params=params(8),
        cost_estimate=cost(10**6, 3 * 10**6),
    )(source)


def order_kernel(info, own, rec, first, second):
    @pl.when(info[0] == 0)
    def _():
        first[...] = own[...]
        second[...] = rec[...]

    @pl.when(info[0] == 1)
    def _():
        first[...] = rec[...]
        second[...] = own[...]


def order(info, own, rec):
    return pl.pallas_call(
        order_kernel,
        name="order_rows",
        in_specs=[SM] + [VM] * 2,
        out_specs=[VM] * 2,
        out_shape=[sds(own.shape, own.dtype)] * 2,
        compiler_params=params(8),
        cost_estimate=cost(3 * 10**13, 10**6),
    )(info, own, rec)


def feed_kernel(info, m_own, m_rec, g_own, g_rec, wg, wu, wd_in, act, gate_g, up_g, *rest):
    ends, sums, wd = rest[:4], rest[4:8], rest[8]
    step = pl.program_id(0)
    wd[...] = wd_in[...]

    @pl.when((step == 0) & (info[4] == 1))
    def _():
        wd[:128, :] = jnp.zeros((128, D), BF)

    @pl.when(step == 0)
    def _():
        for total in sums:
            total[...] = jnp.zeros_like(total)

    for at, (m, g) in enumerate(((m_own, g_own), (m_rec, g_rec))):
        rows = slice(HALF * at, HALF * at + HALF)
        gate = nn(m[...], wg[...])
        up = nn(m[...], wu[...])
        grad = nt(g[...], wd[...])
        sig = 1.0 / (1.0 + jnp.exp(-gate))
        swish = gate * sig
        act[rows, :] = (swish * up).astype(BF)
        up_g[rows, :] = (grad * swish).astype(BF)
        gate_g[rows, :] = (grad * up * (sig + swish * (1.0 - sig))).astype(BF)
        sums[at][...] += nn(act[rows, :], wd[...])
        sums[2 + at][...] += nt(gate_g[rows, :], wg[...]) + nt(up_g[rows, :], wu[...])

    @pl.when(step == pl.num_programs(0) - 1)
    def _():
        for end, total in zip(ends, sums, strict=True):
            end[...] = total[...].astype(BF)


def whole(shape):
    zeros = (0,) * len(shape)
    return pl.BlockSpec(shape, lambda *_: zeros, pipeline_mode=pl.Buffered(1))


def feed(info, m_own, m_rec, g_own, g_rec, wg, wu, wd):
    rows = whole((HALF, D))

    def start(j, info):
        return pl.multiple_of(info[4] * STEP + j * CHUNK, 128)

    wide = pl.BlockSpec((pl.Element(D), pl.Element(CHUNK)), lambda j, info: (0, start(j, info)))
    tall = pl.BlockSpec((pl.Element(CHUNK), pl.Element(D)), lambda j, info: (start(j, info), 0))
    kept = pl.BlockSpec((2 * HALF, CHUNK), lambda j, info: (0, j))
    return pl.pallas_call(
        feed_kernel,
        name="feed_forward_and_back",
        grid_spec=pltpu.PrefetchScalarGridSpec(
            num_scalar_prefetch=1,
            grid=(HID // CHUNK,),
            in_specs=[rows] * 4 + [wide, wide, tall],
            out_specs=[kept] * 3 + [rows] * 4,
            scratch_shapes=[pltpu.VMEM((HALF, D), F32)] * 4 + [pltpu.VMEM((CHUNK, D), BF)],
        ),
        out_shape=[pltpu.HBM((2 * HALF, HID), BF)] * 3 + [sds((HALF, D), BF)] * 4,
        compiler_params=params(30),
        cost_estimate=cost(10**10, 20 * 10**6, 10**6),
    )(info, m_own, m_rec, g_own, g_rec, wg, wu, wd)


def halves_kernel(info, own_0, own_1, rec_0, rec_1, mine, theirs):
    for half, (own, rec) in enumerate(((own_0, rec_0), (own_1, rec_1))):
        total = (own[...].astype(F32) + rec[...].astype(F32)).astype(BF)

        @pl.when(info[0] == half)
        def _(total=total):
            mine[...] = total

        @pl.when(info[0] != half)
        def _(total=total):
            theirs[...] = total


def halves(info, *args):
    return pl.pallas_call(
        halves_kernel,
        name="sum_cores_rows",
        in_specs=[SM] + [VM] * 4,
        out_specs=[VM] * 2,
        out_shape=[sds((HALF, D), BF)] * 2,
        compiler_params=params(10),
        cost_estimate=cost(10**6, 4 * 10**6),
    )(info, *args)


def weight_kernel(left_0, left_1, right_0, right_1, *outs):
    product = nn(left_0[...], right_0[...]) + nn(left_1[...], right_1[...])
    count = 16 // len(outs)
    for piece in range(16):
        low = PIECE * piece
        outs[piece // count][piece % count] = product[low : low + PIECE, :].astype(BF)


def weight_grad(left_0, left_1, right_0, right_1, first, count, parts=2, weigh=1):
    left = whole((D, 2 * HALF))
    right = pl.BlockSpec((2 * HALF, CHUNK), lambda j: (0, j + first))
    out = pl.BlockSpec((16 // parts, PIECE, CHUNK), lambda j: (0, 0, j))
    return pl.pallas_call(
        weight_kernel,
        name="weight_gradient",
        grid=(count,),
        in_specs=[left] * 2 + [right] * 2,
        out_specs=[out] * parts,
        out_shape=[pltpu.HBM((16 // parts, PIECE, CHUNK * count), BF)] * parts,
        compiler_params=params(16),
        cost_estimate=cost(7 * 10**8 * count * weigh, 8 * 10**6),
    )(left_0, left_1, right_0, right_1)


def fold_kernel(plan, ways, info, *refs):
    ins = list(refs[: sum(count for group in plan for count, _, _ in group)])
    outs = list(refs[len(ins) :])
    for group in plan:
        out = [outs.pop(0) for _ in range(ways)]
        low = 0
        for count, mask, bits in group:
            terms = [ins.pop(0) for _ in range(count)]
            pieces, _, wide = terms[0].shape
            each = pieces // ways
            for at in range(pieces):
                piece = at
                if mask is not None:
                    piece = lax.bitwise_xor(jnp.int32(at), lax.bitwise_and(info[mask], bits))
                total = terms[0][piece].astype(F32)
                for term in terms[1:]:
                    total = total + term[piece].astype(F32)
                out[at // each][at % each, :, low : low + wide] = total.astype(BF)
            low += wide


def fold(info, ways, *groups, weigh=10**7):
    plan = [[(len(terms), mask, bits) for terms, mask, bits in group] for group in groups]
    ins = [ref for group in groups for terms, _, _ in group for ref in terms]
    shapes = []
    for group in groups:
        wide = sum(terms[0].shape[-1] for terms, _, _ in group)
        shapes += [sds((group[0][0][0].shape[0] // ways, PIECE, wide), BF)] * ways
    out = pl.pallas_call(
        functools.partial(fold_kernel, plan, ways),
        name="sum_parts",
        in_specs=[SM] + [VM] * len(ins),
        out_specs=[VM] * len(shapes),
        out_shape=shapes,
        compiler_params=params(20),
        cost_estimate=cost(weigh, 6 * 10**6),
    )(info, *ins)
    return [out[ways * at : ways * at + ways] for at in range(len(groups))]


def branch_kernel(info, dm_own_0, dm_own_1, dm_rec_0, dm_rec_1, cot_0, cot_1, hid_0, hid_1,
                  gain_two, wo_dup, grad_mid, branch, grad_att, sums):
    sum_two = jnp.zeros((1, D), F32)
    for half, (own, rec, cot, hid) in enumerate(
        ((dm_own_0, dm_rec_0, cot_0, hid_0), (dm_own_1, dm_rec_1, cot_1, hid_1))
    ):
        rows = slice(HALF * half, HALF * half + HALF)
        field = hid[...]
        factor = factor_of(field)
        normed = field * factor
        grad = own[...].astype(F32) + rec[...].astype(F32)
        scaled = grad * gain_two[...]
        middle = cot[...].astype(F32) + factor * (
            scaled - normed * jnp.mean(scaled * normed, axis=-1, keepdims=True)
        )
        branch[rows, :] = middle.astype(BF)
        part = jnp.sum(grad * normed, axis=0, keepdims=True)
        sum_two = jnp.where(info[0] == half, part, sum_two)

        @pl.when(info[0] == half)
        def _(middle=middle):
            grad_mid[...] = middle

    grad_att[...] = nt(branch[...], wo_dup[...]).astype(BF)
    sums[...] = sum_two


def branch_back(info, *args):
    return pl.pallas_call(
        branch_kernel,
        name="norm_and_projection_backward",
        in_specs=[SM] + [VM] * 10,
        out_specs=[VM] * 4,
        out_shape=[sds((HALF, D), F32), sds((ROWS, D), BF), sds((ROWS, D), BF), sds((1, D), F32)],
        compiler_params=params(26),
        cost_estimate=cost(10**9, 10**7),
    )(info, *args)


def back_kernel(blocks, info, grad_att, rotated, value, stats, cosine, sine, lin):
    causal, wide = masks(info[1], keys_first=True)
    lane = lax.broadcasted_iota(jnp.int32, (256, 128), 1)
    base = 256 * blocks[0]
    grad_k = [jnp.zeros((256, 128), F32) for _ in blocks]
    grad_v = [jnp.zeros((256, 128), F32) for _ in blocks]
    for block in blocks:
        first, low, high = SPANS[block]
        rows = slice(first, first + 256)
        to = slice(first - base, first - base + 256)
        mask = wide if block == 1 else causal
        keys = rotated[low:high, 896:1024]
        vals = value[low:high, :]
        cos_b, sin_b = turns(cosine, block, info[1]), turns(sine, block, info[1])
        turned = []
        for head in range(HEADS):
            cols = slice(128 * head, 128 * head + 128)
            query, grad_o = rotated[rows, cols], grad_att[rows, cols]
            chance = jnp.exp(nt(keys, query) * 0.0625 + mask - stats[head : head + 1, rows])
            grad_p = nt(vals, grad_o) * 0.5
            inner = jnp.sum(chance * grad_p, axis=0, keepdims=True)
            grad_s = (chance * (grad_p - inner)).astype(BF)
            low_p = chance.astype(BF)
            back = tn(grad_s, keys) * 0.125
            turned.append(back * cos_b - pltpu.roll(back, 64, 1) * sin_b)
            for at in range((high - low) // 256):
                part = slice(256 * at, 256 * at + 256)
                grad_k[(low - base) // 256 + at] += nn(grad_s[part, :], query)
                grad_v[(low - base) // 256 + at] += nn(low_p[part, :], grad_o)
        turned.append(jnp.zeros((256, 128), F32))
        for pair in range(4):
            right = pltpu.roll(turned[2 * pair + 1], 64, 1)
            lin[to, 128 * pair : 128 * pair + 128] = jnp.where(
                lane < 64, turned[2 * pair], right
            ).astype(BF)
    for at, block in enumerate(blocks):
        rows = slice(256 * at, 256 * at + 256)
        cos_b, sin_b = turns(cosine, block, info[1]), turns(sine, block, info[1])
        back = grad_k[at] * 0.125
        back = back * cos_b - pltpu.roll(back, 64, 1) * sin_b
        back = pltpu.roll(back, 64, 1).astype(BF)
        lin[rows, 384:512] = jnp.where(lane < 64, lin[rows, 384:512], back)
        lin[rows, 512:640] = jnp.where(lane < 64, 0.0, grad_v[at]).astype(BF)


def back(blocks, info, *args):
    return pl.pallas_call(
        functools.partial(back_kernel, blocks),
        name="attention_backward",
        in_specs=[SM] + [VM] * 6,
        out_specs=VM,
        out_shape=sds((256 * len(blocks), 640), BF),
        compiler_params=params(20),
        cost_estimate=cost(10**9, 10**7, 10**6),
    )(info, *args)


def last_kernel(info, branch, lin_a, lin_b, sum_two, att, attn_t, w_cat, tok_0, tok_1,
                da_own, da_send, pack_keep, pack_send, grad_in):
    grad_in[:512, :] = nn(lin_a[...], w_cat[...])
    grad_in[512:, :] = nn(lin_b[...], w_cat[...])
    mine = pl.multiple_of(info[0] * HALF, HALF)
    other = pl.multiple_of((1 - info[0]) * HALF, HALF)
    da_own[...] = grad_in[pl.ds(mine, HALF), :]
    da_send[...] = grad_in[pl.ds(other, HALF), :].astype(BF)
    sum_one = jnp.zeros((1, D), F32)
    for half, src in enumerate((tok_0, tok_1)):
        field = src[...].astype(F32)
        grad = grad_in[HALF * half : HALF * half + HALF, :]
        sum_one = sum_one + jnp.sum(grad * (field * factor_of(field)), axis=0, keepdims=True)
    sum_b = jnp.sum(lin_a[...].astype(F32), axis=0, keepdims=True)
    sum_b = sum_b + jnp.sum(lin_b[...].astype(F32), axis=0, keepdims=True)
    grad_w = nn(attn_t[:, :512], lin_a[...]) + nn(attn_t[:, 512:], lin_b[...])
    grad_o = tn(branch[...], att[...])
    first_w = grad_w[:, :512]
    second_w = jnp.concatenate([grad_o[:, :384], grad_o[:, 384:] + grad_w[:, 512:]], axis=1)
    sum_two = sum_two[...]
    extra_a = {0: sum_b[:, :512], 1: sum_one[:, :512], 2: sum_two[:, :512]}
    extra_b = {0: sum_b[:, 512:], 1: sum_one[:, 512:], 2: sum_two[:, 512:]}

    def lines(extra):
        count = extra.shape[1] // 128
        parts = [extra[:, 128 * at : 128 * at + 128] for at in range(count)]
        return jnp.concatenate([*parts, jnp.zeros((PIECE - count, 128), F32)], axis=0)

    for piece in range(16):
        rows = slice(PIECE * piece, PIECE * piece + PIECE)
        packs = []
        for grads, extra in ((first_w, extra_a), (second_w, extra_b)):
            more = lines(extra[piece]) if piece in extra else jnp.zeros((PIECE, 128), F32)
            packs.append((grads[rows, :], more))
        for at, cols in ((0, slice(0, 512)), (1, slice(512, 640))):
            low, high = packs[0][at], packs[1][at]
            pack_keep[piece, :, cols] = jnp.where(info[4] == 0, low, high).astype(BF)
            pack_send[piece, :, cols] = jnp.where(info[4] == 0, high, low).astype(BF)


def last(info, *args):
    return pl.pallas_call(
        last_kernel,
        name="attention_weight_gradients",
        in_specs=[SM] + [VM] * 9,
        out_specs=[VM] * 4,
        out_shape=[
            sds((HALF, D), F32),
            sds((HALF, D), BF),
            sds((16, PIECE, 640), BF),
            sds((16, PIECE, 640), BF),
        ],
        scratch_shapes=[pltpu.VMEM((ROWS, D), F32)],
        compiler_params=params(28),
        cost_estimate=cost(3 * 10**9, 16 * 10**6),
    )(info, *args)


def wide_kernel(got, info, own, other, *refs):
    out, stage, sems = refs[-3:]
    copies = []
    for at, (slot, src) in enumerate(((2, own), (5, other))):
        half = lax.bitwise_xor(info[slot] // 8, got)
        core = lax.rem(info[4] + at, 2)
        for piece in range(8):
            stage[at, piece] = src[piece].astype(F32)
            place = lax.bitwise_xor(jnp.int32(piece), lax.rem(info[slot], 8))
            sem = sems.at[at, piece]
            first = pltpu.make_async_copy(
                stage.at[at, piece], out.at[half, place, :, pl.ds(0, HID)], sem
            )
            second = pltpu.make_async_copy(
                stage.at[at, piece, :, pl.ds(128, HID - 128)],
                out.at[half, place, :, pl.ds(HID, HID - 128)],
                sem,
            )
            pl.when(core == 0)(first.start)
            pl.when(core == 1)(second.start)
            copies.append((core, first, second))
    for core, first, second in copies:
        pl.when(core == 0)(first.wait)
        pl.when(core == 1)(second.wait)


def lanes(pieces, low, count):
    return pl.BlockSpec(
        (pl.Element(pieces), pl.Element(PIECE), pl.Element(count)), lambda _: (0, 0, low)
    )


def wide(info, part, own, other, before=None, weigh=10**7):
    info = jnp.stack([info[0], info[1], info[2 + part], info[3], info[4], info[5 + part], info[6]])
    more = [] if before is None else [before]
    anywhere = pl.BlockSpec(memory_space=pl.ANY)
    return pl.pallas_call(
        functools.partial(wide_kernel, len(more)),
        name="gradients_wide",
        grid=(1,),
        in_specs=[SM] + [lanes(8, 0, HID)] * 2 + [anywhere] * len(more),
        out_specs=anywhere,
        out_shape=sds((2, 8, PIECE, 2432), F32),
        scratch_shapes=[pltpu.VMEM((2, 8, PIECE, HID), F32), pltpu.SemaphoreType.DMA((2, 8))],
        input_output_aliases={3: 0} if more else {},
        compiler_params=params(16),
        cost_estimate=cost(weigh, 14 * 10**6),
    )(info, own, other, *more)


def model_order(info, mask, own, got, cols):
    pieces = []
    for q in range(16):
        place = lax.bitwise_xor(jnp.int32(q), info[mask])
        at = lax.rem(place, 8)
        ours, theirs = own[at, :, cols].astype(F32), got[at, :, cols].astype(F32)
        pieces.append(jnp.where(place < 8, ours, theirs))
    return jnp.concatenate(pieces, axis=0)


def tall_kernel(info, *refs):
    down, stage, sems = refs[-3:]
    copies = []
    for step in range(19):
        tile = step if step < 10 else step - 9
        part = int(tile >= SPLIT // 128)
        own, got, other, other_got = refs[4 * part : 4 * part + 4]
        low = 128 * tile - SPLIT * part
        cols = slice(low, low + 128)

        def ours(step=step, part=part, own=own, got=got, cols=cols):
            stage[step] = model_order(info, 2 + part, own, got, cols).T

        def theirs(step=step, part=part, own=other, got=other_got, cols=cols):
            stage[step] = model_order(info, 5 + part, own, got, cols).T

        pl.when((info[4] == 0) == (step < 10))(ours)
        pl.when((info[4] == 0) != (step < 10))(theirs)
        rows = pl.ds(128 * step, 128)
        copies.append(pltpu.make_async_copy(stage.at[step], down.at[rows, :], sems.at[step]))
        copies[-1].start()
    for copy in copies:
        copy.wait()


def tall(info, first, second):
    return pl.pallas_call(
        tall_kernel,
        name="gradients_tall",
        grid=(1,),
        in_specs=[SM] + [lanes(8, at, SPLIT) for at in (HID, 0) * 2]
        + [lanes(8, at, HID - SPLIT) for at in (HID, 0) * 2],
        out_specs=pl.BlockSpec(memory_space=pl.ANY),
        out_shape=sds((2432, D), F32),
        scratch_shapes=[pltpu.VMEM((19, 128, D), F32), pltpu.SemaphoreType.DMA((19,))],
        compiler_params=params(24),
        cost_estimate=cost(10**7, 14 * 10**6),
    )(info, *first, *second)


def small_kernel(info, own, got, other, other_got, query, key, value, out, extras):
    for first in (True, False):
        here = (info[4] == 0) == first

        def write(mask, one, two, first=first):
            for tile in range(4):
                turned = model_order(info, mask, one, two, slice(128 * tile, 128 * tile + 128)).T
                big, little = (query, key) if first else (out, value)
                if tile < 3:
                    big[128 * tile : 128 * tile + 128, :] = turned
                else:
                    big[384:, :] = turned[:64, :]
                    little[...] = turned[64:, :]
            more = model_order(info, mask, one, two, slice(512, 640))
            for piece in range(3):
                extras[0 if first else 1, piece] = more[PIECE * piece : PIECE * piece + 8, :]

        @pl.when(here)
        def _(write=write):
            write(2, own, got)

        @pl.when(jnp.logical_not(here))
        def _(write=write):
            write(5, other, other_got)


def small(info, *arrays):
    kept = [(448, D), (64, D), (64, D), (448, D), (2, 3, 8, 128)]
    return pl.pallas_call(
        small_kernel,
        name="gradients_small",
        grid=(1,),
        in_specs=[SM] + [lanes(8, at + SPLIT, 640) for at in (HID, 0) * 2],
        out_specs=[VM] * len(kept),
        out_shape=[sds(shape, F32) for shape in kept],
        compiler_params=params(20),
        cost_estimate=cost(10**7, 6 * 10**6),
    )(info, *arrays)


def send(field, axis, shift=1):
    size = lax.axis_size(axis)
    return lax.ppermute(field, axis, [(i, (i + shift) % size) for i in range(size)])


def after(field, *others):
    return lax.optimization_barrier((field, *others))[0]


def after_all(fields, *others):
    return lax.optimization_barrier((*fields, *others))[: len(fields)]


def in_order(place, own, rec):
    first = place == 0
    return jnp.where(first, own, rec), jnp.where(first, rec, own)


def swapped(weight, axis=-1):
    first, second = jnp.split(weight, 2, axis=axis)
    return jnp.concatenate([-second, first], axis=axis)


def tables():
    freq_index = np.arange(HD // 2, dtype=np.float32)
    inverse = np.float32(ROPE_BASE) ** (np.float32(-2.0) * freq_index / np.float32(HD))
    angle = np.arange(512, dtype=np.float32)[:, None] * inverse.astype(np.float32)[None, :]
    cosine, sine = np.cos(angle), np.sin(angle)
    return (
        jnp.asarray(np.concatenate([cosine] * 4, axis=1)),
        jnp.asarray(np.concatenate([sine, sine, -sine, -sine], axis=1)),
    )


ORDERS = (
    (("x", "a"), ("x", "b"), ("y", "a"), ("y", "b")),
    (("x", "b"), ("x", "a"), ("y", "b"), ("y", "a")),
), (
    (("y", "a"), ("y", "b"), ("x", "a"), ("x", "b")),
    (("y", "b"), ("y", "a"), ("x", "b"), ("x", "a")),
)
CHIPS = ("x", "zl", "y", "c")


def bit(place, kind):
    return (place ^ (place >> 1)) & 1 if kind == "a" else place >> 1


def mask_of(part, core, places):
    mask = 0
    for axis, kind in ORDERS[part][core]:
        mask = 2 * mask + bit(places[axis], kind)
    return mask


def swap(field, part, *steps):
    pairs = []
    for x in range(4):
        for zl in range(2):
            for y in range(4):
                for c in range(2):
                    to = {"x": x, "y": y}
                    for axis, kind in (ORDERS[part][c][step] for step in steps):
                        to[axis] = to[axis] ^ 1 if kind == "a" else 3 - to[axis]
                    here = ((x * 2 + zl) * 4 + y) * 2 + c
                    pairs.append((here, ((to["x"] * 2 + zl) * 4 + to["y"]) * 2 + c))
    return lax.ppermute(field, CHIPS, pairs)


def swap_two(one, two, step):
    return swap(one, 0, step), swap(two, 1, step)


def spread(one, two, one_r, two_r):
    one, two = jnp.concatenate([one, one_r]), jnp.concatenate([two, two_r])
    return lax.optimization_barrier((one, two))


def add(one, two):
    return (one.astype(F32) + two.astype(F32)).astype(BF)


def shards(tokens, long_count, attn_gain, w_query, b_query, w_key, b_key, w_value, b_value,
           w_out, mlp_gain, w_gate, w_up, w_down, cotangent):
    at_x, at_y, at_c, at_t = (lax.axis_index(a) for a in ("x", "y", "c", "t"))
    places = {"x": at_x, "y": at_y}
    masks_0 = [mask_of(part, 0, places) for part in (0, 1)]
    masks_1 = [mask_of(part, 1, places) for part in (0, 1)]
    mine = [jnp.where(at_c == 0, a, b) for a, b in zip(masks_0, masks_1, strict=True)]
    theirs = [jnp.where(at_c == 0, b, a) for a, b in zip(masks_0, masks_1, strict=True)]
    info = jnp.stack([at_t, long_count[0], *mine, at_c, *theirs]).astype(jnp.int32)
    gain_one = attn_gain.astype(F32)[None, :]
    gain_two = mlp_gain.astype(F32)[None, :]

    tok_rec = send(tokens, "t")
    half_out = lax.dynamic_slice(w_out, (at_c * SLAB, 0), (SLAB, D))
    half_out = send(half_out, "t")
    cot_rec = send(cotangent, "t")

    wq, wk, wv = w_query.T, w_key.T, w_value.T
    heads = wq.reshape(HEADS, HD, D)
    heads = jnp.concatenate([heads, swapped(heads, 1)], axis=1).reshape(HEADS * 128, D)
    w_all = jnp.concatenate([heads, wk, swapped(wk, 0), wv, wv], axis=0)
    bias = b_query.reshape(HEADS, HD)
    bias = jnp.concatenate([bias, swapped(bias)], axis=-1).reshape(HEADS * 128)
    b_all = jnp.concatenate([bias, b_key, swapped(b_key), b_value, b_value]).astype(F32)[None, :]
    cosine, sine = tables()
    tok_0, tok_1 = in_order(at_t, tokens, tok_rec)
    attn_in, rotated, value, stats, att_0, att_1, att_keep = attention(
        info, tok_0, tok_1, gain_one, w_all, b_all, cosine, sine
    )
    rec_0 = send(att_0, "t")
    rec_1 = send(att_1, "t")

    half_out, wq, w_out, _ = lax.optimization_barrier((half_out, wq, w_out, att_0))
    half_out = in_order(at_c, half_out, send(half_out, "c"))
    no_rows = jnp.zeros((HD, D), BF)
    other_out = jnp.concatenate([*half_out, no_rows])
    this_out = jnp.concatenate([w_out, no_rows])
    cot_0, cot_1 = order(info, cotangent, cot_rec)
    cot_0_rec, cot_1_rec = send(cot_0, "c"), send(cot_1, "c")
    w_cat = jnp.concatenate([wq, wk, jnp.zeros((HD, D), BF), wv], axis=0)
    wo_dup = w_out.reshape(HEADS, HD, D)
    wo_dup = jnp.concatenate([wo_dup, wo_dup], axis=1).reshape(HEADS * 128, D)
    attn_t = flip(attn_in)
    rec_0, w_cat, wo_dup, attn_t, cot_0_rec, cot_1_rec = lax.optimization_barrier(
        (rec_0, w_cat, wo_dup, attn_t, cot_0_rec, cot_1_rec)
    )

    hid_0, m_0 = project(att_0, rec_0, this_out, other_out, tok_0, gain_two)
    m_0_rec = send(m_0, "c")
    g_0x, g_0y = turn(info, after(cot_0, m_0), cot_0_rec)
    act_0, gate_0, up_0, out_0, out_0_oth, dm_0, dm_0_oth = feed(
        info, m_0, after(m_0_rec, g_0x), cot_0, cot_0_rec, w_gate, w_up, w_down
    )
    hid_1, m_1 = project(att_1, after(rec_1, act_0), this_out, other_out, tok_1, gain_two)
    m_1_rec = send(m_1, "c")
    m_0x, m_0y = turn(info, after(m_0, m_1), m_0_rec)
    dm_0 = add(dm_0, after(send(dm_0_oth, "c"), m_0x))
    dm_0_rec = send(dm_0, "t")
    act_1, gate_1, up_1, out_1, out_1_oth, dm_1, dm_1_oth = feed(
        info, after(m_1, dm_0), m_1_rec, cot_1, cot_1_rec, w_gate, w_up, w_down
    )
    m_1x, m_1y = turn(info, after(m_1, dm_1, dm_0_rec), m_1_rec)
    dm_1 = add(dm_1, after(send(dm_1_oth, "c"), m_1x))
    dm_1_rec = send(dm_1, "t")

    gate_k, gate_g = weight_grad(m_0x, m_1x, gate_0, after(gate_1, dm_1, dm_0_rec), 0, 5)
    gate_r = swap(gate_g, 0, 0)
    up_k, up_g = weight_grad(m_0y, m_1y, up_0, after(up_1, gate_g), 0, 5)
    up_r = swap(up_g, 1, 0)
    g_1x, g_1y = turn(info, after(cot_1, up_g), cot_1_rec, 3 * 10**13)
    out_rec = [send(after(field, dm_1), "c") for field in (out_0_oth, out_1_oth)]
    mine, theirs = halves(info, out_0, out_1, *after_all(out_rec, g_1x))
    theirs_rec = send(theirs, "t")

    grad_mid, branch, grad_att, sum_two = branch_back(
        info, dm_0, dm_1, dm_0_rec, after(dm_1_rec, mine), cot_0, cot_1, hid_0, hid_1,
        gain_two, wo_dup,
    )
    lin_a = back((0, 1), info, grad_att, rotated, value, stats, cosine, sine)
    lin_b = back((2,), info, after(grad_att, lin_a), rotated, value, stats, cosine, sine)
    hidden = jnp.where(at_t == 0, hid_0, hid_1)
    theirs_rec = after(theirs_rec, lin_b)
    output = (hidden + mine.astype(F32) + theirs_rec.astype(F32)).astype(BF)
    da_own, da_send, pack_k, pack_g = last(
        info, branch, lin_a, after(lin_b, output), sum_two, att_keep, attn_t, w_cat, tok_0, tok_1
    )
    pack_r = send(pack_g, "c")

    (gate_k, gate_g), (up_k, up_g) = fold(
        info, 2, [((gate_k, after(gate_r, pack_g)), None, 0)], [((up_k, up_r), None, 0)]
    )
    gate_r, up_r = swap_two(gate_g, up_g, 1)
    low_k, low_g = weight_grad(g_0x, g_1x, act_0, after(act_1, gate_g), 0, 2)
    low_r = swap(low_g, 0, 0)
    ((pack_k, pack_g),) = fold(info, 2, [((pack_k, after(pack_r, low_g)), 2, 15)])
    pack_r = swap(pack_g, 0, 0)
    high_k, high_g = weight_grad(g_0y, g_1y, act_0, after(act_1, pack_g), 2, 3)
    high_r = swap(high_g, 1, 0)
    ((pack_k, pack_g),) = fold(
        info, 2, [((pack_k, after(pack_r, high_g, gate_r, up_r)), None, 0)], weigh=3 * 10**13
    )
    pack_r = swap(pack_g, 0, 1)
    (low_k, low_g), (high_k, high_g) = fold(
        info, 2, [((low_k, after(low_r, pack_g)), None, 0)], [((high_k, high_r), None, 0)]
    )
    low_r, high_r = swap_two(low_g, high_g, 1)
    da_rec = send(after(da_send, low_g), "t")
    (one_k, one_g), (two_k, two_g) = fold(
        info,
        2,
        [
            ((gate_k, after(gate_r, low_g)), 2, 3),
            ((low_k, low_r), 2, 3),
            ((pack_k, pack_r), None, 0),
        ],
        [((up_k, up_r), 3, 3), ((high_k, high_r), 3, 3)],
    )
    one_r, two_r = swap_two(one_g, two_g, 2)

    (one_k, one_g), (two_k, two_g) = fold(
        info, 2, [((one_k, one_r), None, 0)], [((two_k, two_r), None, 0)]
    )
    one_r, two_r = swap_two(one_g, two_g, 3)
    ((part,),) = fold(info, 1, [((one_k, one_r), None, 0), ((two_k, two_r), None, 0)])
    part_r = send(part, "zl")

    field = tokens.astype(F32)
    factor = factor_of(field)
    normed = field * factor
    scaled = (da_own + after(da_rec, part).astype(F32)) * gain_one
    grad_tokens = grad_mid + factor * (
        scaled - normed * jnp.mean(scaled * normed, axis=-1, keepdims=True)
    )
    grad_tokens = grad_tokens.astype(BF)
    part = add(part, after(part_r, grad_tokens))

    wide_one = HID + SPLIT + 640
    one, two = part[..., :wide_one], part[..., wide_one:]
    for step in (3, 2, 1):
        one, two = spread(one, two, *swap_two(one, two, step))
    low_r, high_r = swap_two(one[..., HID:], two[..., HID:], 0)
    gate_r, up_r = swap_two(one[..., :HID], two[..., :HID], 0)
    one_c = send(one, "c")
    two_c = send(after(two, one_c), "c")
    grad_w_gate = wide(info, 0, one, one_c, weigh=3 * 10**13)
    grad_w_up = wide(info, 1, two, after(two_c, grad_w_gate))
    low_r, high_r = after_all((low_r, high_r), grad_w_up)
    low_c, high_c = send(low_r, "c"), send(high_r, "c")
    grad_wq, grad_wk, grad_wv, grad_wo, extras = small(info, one, low_r, one_c, low_c)
    grad_w_down = tall(info, (one, low_r, one_c, low_c), (two, high_r, two_c, high_c))
    gate_r, up_r = after_all((gate_r, up_r), grad_wo, grad_w_down)
    gate_c = send(gate_r, "c")
    up_c = send(up_r, "c")
    grad_w_gate = wide(info, 0, gate_r, gate_c, grad_w_gate)
    grad_w_up = wide(info, 1, up_r, after(up_c, grad_w_gate), grad_w_up)
    grad_w_gate, grad_w_up = grad_w_gate.reshape(D, 2432), grad_w_up.reshape(D, 2432)
    gains = extras[:, 1:].reshape(2, 2, 1024)
    gains = jnp.concatenate([gains[0, :, :512], gains[1, :, :384]], axis=1)
    gains = gains + after(send(gains, "t"), grad_w_up)
    biases = extras[0, 0, :4].reshape(512)

    return (
        output,
        grad_tokens,
        gains[0],
        grad_wq.T,
        biases[:448],
        grad_wk.T,
        biases[448:],
        grad_wv.T,
        extras[1, 0, 0, 64:],
        grad_wo,
        gains[1],
        grad_w_gate,
        grad_w_up,
        grad_w_down,
    )


def solution(mesh):
    fine = Mesh(mesh.devices.reshape(4, 2, 4, 2, 2), ("x", "zl", "y", "c", "t"))
    dp = ("x", "zl", "y", "c")
    rows, cols, split = P((*dp, "t"), None), P(None, "t"), P("t")
    down = P("t", None)
    return jax.shard_map(
        shards,
        mesh=fine,
        in_specs=(
            rows, P(dp), P(), cols, split, cols, split, cols, split, down, P(), cols, cols, down,
            rows,
        ),
        out_specs=(
            rows, rows, P(), cols, split, cols, split, cols, split, down, P(), cols, cols, down,
        ),
        check_vma=False,
    )
```

```python
import functools

import jax
import jax.numpy as jnp
import numpy as np
from jax import lax
from jax.experimental import pallas as pl
from jax.experimental.pallas import tpu as pltpu
from jax.sharding import Mesh
from jax.sharding import PartitionSpec as P

HD = 64
EPSILON = 1e-06
ROPE_BASE = 1000000.0
BF = jnp.bfloat16
F32 = jnp.float32

D = 896
HALF = 384
ROWS = 768
HEADS = 7
PIECE = 56
SLAB = 224
HID = 1280
SPLIT = 512
STEP = 1152
CHUNK = 256
MIB = 1024 * 1024

VM = pl.BlockSpec(memory_space=pltpu.VMEM)
SM = pl.BlockSpec(memory_space=pltpu.SMEM)


def sds(shape, dtype):
    return jax.ShapeDtypeStruct(shape, dtype)


def nn(a, b):
    return lax.dot_general(a, b, (((1,), (0,)), ((), ())), preferred_element_type=F32)


def nt(a, b):
    return lax.dot_general(a, b, (((1,), (1,)), ((), ())), preferred_element_type=F32)


def tn(a, b):
    return lax.dot_general(a, b, (((0,), (0,)), ((), ())), preferred_element_type=F32)


def half_rows(info):
    return [
        pl.ds(pl.multiple_of(place * HALF, HALF), HALF) for place in (info[0], 1 - info[0])
    ]


def factor_of(field):
    return lax.rsqrt(jnp.mean(field * field, axis=-1, keepdims=True) + EPSILON)


def params(mib):
    return pltpu.CompilerParams(vmem_limit_bytes=mib * MIB)


def cost(flops, size, trans=0):
    return pl.CostEstimate(flops=flops // 1000, bytes_accessed=size // 1000, transcendentals=trans // 1000)


def masks(is_long, keys_first=False):
    row = lax.broadcasted_iota(jnp.int32, (256, 256), 0)
    col = lax.broadcasted_iota(jnp.int32, (256, 256), 1)
    causal = jnp.where(row <= col if keys_first else col <= row, 0.0, -1e30).astype(F32)
    before = jnp.full((256, 256), jnp.where(is_long == 1, 0.0, -1e30).astype(F32))
    return causal, jnp.concatenate([before, causal], axis=0 if keys_first else 1)


def turns(ref, block, is_long):
    start = ref[:256, :]
    return jnp.where(is_long == 1, ref[256:, :], start) if block == 1 else start


SPANS = ((0, 0, 256), (256, 0, 512), (512, 512, 768))


def attention_kernel(info, tok_0, tok_1, gain, w_all, b_all, cosine, sine,
                     attn_in, rotated, value, stats, att_0, att_1, att_keep):
    for rows, src in zip(half_rows(info), (tok_0, tok_1), strict=True):
        field = src[...].astype(F32)
        attn_in[rows, :] = (field * factor_of(field) * gain[...]).astype(BF)
    for block in range(3):
        rows = slice(256 * block, 256 * block + 256)
        lin = nt(attn_in[rows, :], w_all[...]) + b_all[...]
        cos_b, sin_b = turns(cosine, block, info[1]), turns(sine, block, info[1])
        for head in range(HEADS + 1):
            part = lin[:, 128 * head : 128 * head + 128]
            turned = part * cos_b + pltpu.roll(part, 64, 1) * sin_b
            rotated[rows, 128 * head : 128 * head + 128] = turned.astype(BF)
        value[rows, :] = lin[:, 1024:1152].astype(BF)
    causal, wide = masks(info[1])
    lane = lax.broadcasted_iota(jnp.int32, (256, 128), 1)
    for block, (first, low, high) in enumerate(SPANS):
        rows = slice(first, first + 256)
        mask = wide if block == 1 else causal
        keys = rotated[low:high, 1024 - 128 :]
        vals = value[low:high, :]
        kept = jnp.zeros((256, 128), F32)
        outs = []
        for head in range(HEADS):
            scores = nt(rotated[rows, 128 * head : 128 * head + 128], keys) * 0.0625 + mask
            top = jnp.max(scores, axis=-1, keepdims=True)
            expo = jnp.exp(scores - top)
            total = jnp.sum(expo, axis=-1, keepdims=True)
            kept = jnp.where(lane == head, top + jnp.log(total), kept)
            outs.append(nn(expo.astype(BF), vals) * (1.0 / total))
        stats[:, rows] = kept.T[:8, :]
        outs.append(jnp.zeros((256, 128), F32))
        for pair in range(4):
            both = jnp.where(lane < 64, outs[2 * pair], outs[2 * pair + 1])
            att_keep[rows, 128 * pair : 128 * pair + 128] = both.astype(BF)
    lane = lax.broadcasted_iota(jnp.int32, (64, 128), 1)
    for rows, out in zip(half_rows(info), (att_0, att_1), strict=True):
        out[:HALF, :] = att_keep[rows, :384]
        for pair in range(3):
            low = pl.multiple_of(rows.start + 128 * pair, 128)
            part = att_keep[pl.ds(low, 128), 384:].astype(F32)
            left, right = part[:64, :], pltpu.roll(part[64:, :], 64, 1)
            out[HALF:, 128 * pair : 128 * pair + 128] = jnp.where(lane < 64, left, right).astype(BF)


def attention(info, tok_0, tok_1, gain, w_all, b_all, cosine, sine):
    return pl.pallas_call(
        attention_kernel,
        name="attention_forward",
        in_specs=[SM] + [VM] * 7,
        out_specs=[VM] * 7,
        out_shape=[
            sds((ROWS, D), BF),
            pltpu.HBM((ROWS, 1024), BF),
            pltpu.HBM((ROWS, 128), BF),
            pltpu.HBM((8, ROWS), F32),
            sds((448, 384), BF),
            sds((448, 384), BF),
            pltpu.HBM((ROWS, 512), BF),
        ],
        compiler_params=params(26),
        cost_estimate=cost(4 * 10**9, 12 * 10**6, 3 * 10**6),
    )(info, tok_0, tok_1, gain, w_all, b_all, cosine, sine)


def project_kernel(att_own, att_rec, wo_own, wo_rec, tok, gain, hidden, mlp_in, full):
    lane = lax.broadcasted_iota(jnp.int32, (64, 128), 1)
    field = tok[...].astype(F32)
    for att, weight in ((att_own, wo_own), (att_rec, wo_rec)):
        full[:, :384] = att[:HALF, :]
        for pair in range(3):
            both = att[HALF:, 128 * pair : 128 * pair + 128].astype(F32)
            low = 128 * pair
            full[low : low + 64, 384:] = jnp.where(lane < 64, both, 0.0).astype(BF)
            both = jnp.where(lane < 64, pltpu.roll(both, 64, 1), 0.0)
            full[low + 64 : low + 128, 384:] = both.astype(BF)
        field = field + nn(full[...], weight[...])
    hidden[...] = field
    mlp_in[...] = (field * factor_of(field) * gain[...]).astype(BF)


def project(att_own, att_rec, wo_own, wo_rec, tok, gain):
    return pl.pallas_call(
        project_kernel,
        name="project_norm",
        in_specs=[VM] * 6,
        out_specs=[VM] * 2,
        out_shape=[pltpu.HBM((HALF, D), F32), sds((HALF, D), BF)],
        scratch_shapes=[pltpu.VMEM((HALF, 512), BF)],
        compiler_params=params(14),
        cost_estimate=cost(7 * 10**8, 6 * 10**6),
    )(att_own, att_rec, wo_own, wo_rec, tok, gain)


def turn_kernel(info, own, rec, first, second):
    for at, src in enumerate((own, rec)):
        cols = slice(HALF * at, HALF * at + HALF)
        for slab in range(4):
            turned = src[:, SLAB * slab : SLAB * slab + SLAB].astype(F32).T.astype(BF)
            for mask, out in ((info[2], first), (info[3], second)):
                slot = lax.bitwise_xor(jnp.int32(slab), mask // 4)
                out[pl.ds(pl.multiple_of(slot * SLAB, SLAB), SLAB), cols] = turned


def turn(info, own, rec, weigh=10**6):
    return pl.pallas_call(
        turn_kernel,
        name="transpose_rows",
        in_specs=[SM] + [VM] * 2,
        out_specs=[VM] * 2,
        out_shape=[pltpu.HBM((D, 2 * HALF), BF)] * 2,
        compiler_params=params(14),
        cost_estimate=cost(weigh, 4 * 10**6),
    )(info, own, rec)


def flip_kernel(source, out):
    for block in range(3):
        rows = slice(256 * block, 256 * block + 256)
        out[:, rows] = source[rows, :].astype(F32).T.astype(BF)


def flip(source):
    return pl.pallas_call(
        flip_kernel,
        name="transpose_whole",
        in_specs=[VM],
        out_specs=VM,
        out_shape=pltpu.HBM((D, ROWS), BF),
        compiler_params=params(8),
        cost_estimate=cost(3 * 10**13, 3 * 10**6),
    )(source)


def feed_kernel(info, m_own, m_rec, g_own, g_rec, wg, wu, wd_in, act, gate_g, up_g, *rest):
    ends, sums, wd = rest[:4], rest[4:8], rest[8]
    step = pl.program_id(0)
    wd[...] = wd_in[...]

    @pl.when((step == 0) & (info[4] == 1))
    def _():
        wd[:128, :] = jnp.zeros((128, D), BF)

    @pl.when(step == 0)
    def _():
        for total in sums:
            total[...] = jnp.zeros_like(total)

    for at, (m, g) in enumerate(((m_own, g_own), (m_rec, g_rec))):
        rows = slice(HALF * at, HALF * at + HALF)
        gate = nn(m[...], wg[...])
        up = nn(m[...], wu[...])
        grad = nt(g[...], wd[...])
        sig = 1.0 / (1.0 + jnp.exp(-gate))
        swish = gate * sig
        act[rows, :] = (swish * up).astype(BF)
        up_g[rows, :] = (grad * swish).astype(BF)
        gate_g[rows, :] = (grad * up * (sig + swish * (1.0 - sig))).astype(BF)
        sums[at][...] += nn(act[rows, :], wd[...])
        sums[2 + at][...] += nt(gate_g[rows, :], wg[...]) + nt(up_g[rows, :], wu[...])

    @pl.when(step == pl.num_programs(0) - 1)
    def _():
        for end, total in zip(ends, sums, strict=True):
            end[...] = total[...].astype(BF)


def whole(shape):
    zeros = (0,) * len(shape)
    return pl.BlockSpec(shape, lambda *_: zeros, pipeline_mode=pl.Buffered(1))


def feed(info, m_own, m_rec, g_own, g_rec, wg, wu, wd):
    rows = whole((HALF, D))

    def start(j, info):
        return pl.multiple_of(info[4] * STEP + j * CHUNK, 128)

    wide = pl.BlockSpec((pl.Element(D), pl.Element(CHUNK)), lambda j, info: (0, start(j, info)))
    tall = pl.BlockSpec((pl.Element(CHUNK), pl.Element(D)), lambda j, info: (start(j, info), 0))
    kept = pl.BlockSpec((2 * HALF, CHUNK), lambda j, info: (0, j))
    return pl.pallas_call(
        feed_kernel,
        name="feed_forward_and_back",
        grid_spec=pltpu.PrefetchScalarGridSpec(
            num_scalar_prefetch=1,
            grid=(HID // CHUNK,),
            in_specs=[rows] * 4 + [wide, wide, tall],
            out_specs=[kept] * 3 + [rows] * 4,
            scratch_shapes=[pltpu.VMEM((HALF, D), F32)] * 4 + [pltpu.VMEM((CHUNK, D), BF)],
        ),
        out_shape=[pltpu.HBM((2 * HALF, HID), BF)] * 3 + [sds((HALF, D), BF)] * 4,
        compiler_params=params(30),
        cost_estimate=cost(10**10, 20 * 10**6, 10**6),
    )(info, m_own, m_rec, g_own, g_rec, wg, wu, wd)


def halves_kernel(own_0, own_1, rec_0, rec_1, mine, theirs):
    for own, rec, out in ((own_0, rec_0, mine), (own_1, rec_1, theirs)):
        out[...] = (own[...].astype(F32) + rec[...].astype(F32)).astype(BF)


def halves(*args):
    return pl.pallas_call(
        halves_kernel,
        name="sum_cores_rows",
        in_specs=[VM] * 4,
        out_specs=[VM] * 2,
        out_shape=[sds((HALF, D), BF)] * 2,
        compiler_params=params(10),
        cost_estimate=cost(3 * 10**13, 4 * 10**6),
    )(*args)


def weight_kernel(left_0, left_1, right_0, right_1, *outs):
    product = nn(left_0[...], right_0[...]) + nn(left_1[...], right_1[...])
    count = 16 // len(outs)
    for piece in range(16):
        low = PIECE * piece
        outs[piece // count][piece % count] = product[low : low + PIECE, :].astype(BF)


def weight_grad(left_0, left_1, right_0, right_1, first, count, parts=2, weigh=1):
    left = whole((D, 2 * HALF))
    right = pl.BlockSpec((2 * HALF, CHUNK), lambda j: (0, j + first))
    out = pl.BlockSpec((16 // parts, PIECE, CHUNK), lambda j: (0, 0, j))
    return pl.pallas_call(
        weight_kernel,
        name="weight_gradient",
        grid=(count,),
        in_specs=[left] * 2 + [right] * 2,
        out_specs=[out] * parts,
        out_shape=[pltpu.HBM((16 // parts, PIECE, CHUNK * count), BF)] * parts,
        compiler_params=params(16),
        cost_estimate=cost(7 * 10**8 * count * weigh, 8 * 10**6),
    )(left_0, left_1, right_0, right_1)


def fold_kernel(plan, ways, info, *refs):
    ins = list(refs[: sum(count for group in plan for count, _, _ in group)])
    outs = list(refs[len(ins) :])
    for group in plan:
        out = [outs.pop(0) for _ in range(ways)]
        low = 0
        for count, mask, bits in group:
            terms = [ins.pop(0) for _ in range(count)]
            pieces, _, wide = terms[0].shape
            each = pieces // ways
            for at in range(pieces):
                piece = at
                if mask is not None:
                    piece = lax.bitwise_xor(jnp.int32(at), lax.bitwise_and(info[mask], bits))
                total = terms[0][piece].astype(F32)
                for term in terms[1:]:
                    total = total + term[piece].astype(F32)
                out[at // each][at % each, :, low : low + wide] = total.astype(BF)
            low += wide


def fold(info, ways, *groups, weigh=10**7):
    plan = [[(len(terms), mask, bits) for terms, mask, bits in group] for group in groups]
    ins = [ref for group in groups for terms, _, _ in group for ref in terms]
    shapes = []
    for group in groups:
        wide = sum(terms[0].shape[-1] for terms, _, _ in group)
        shapes += [sds((group[0][0][0].shape[0] // ways, PIECE, wide), BF)] * ways
    out = pl.pallas_call(
        functools.partial(fold_kernel, plan, ways),
        name="sum_parts",
        in_specs=[SM] + [VM] * len(ins),
        out_specs=[VM] * len(shapes),
        out_shape=shapes,
        compiler_params=params(20),
        cost_estimate=cost(weigh, 6 * 10**6),
    )(info, *ins)
    return [out[ways * at : ways * at + ways] for at in range(len(groups))]


def branch_kernel(info, dm_own_0, dm_own_1, dm_rec_0, dm_rec_1, cot_0, cot_1, hid_0, hid_1,
                  gain_two, wo_dup, grad_mid, branch, grad_att, sums):
    sets = (dm_own_0, dm_rec_0, cot_0, hid_0), (dm_own_1, dm_rec_1, cot_1, hid_1)
    for half, (rows, (own, rec, cot, hid)) in enumerate(zip(half_rows(info), sets, strict=True)):
        field = hid[...]
        factor = factor_of(field)
        normed = field * factor
        grad = own[...].astype(F32) + rec[...].astype(F32)
        scaled = grad * gain_two[...]
        middle = cot[...].astype(F32) + factor * (
            scaled - normed * jnp.mean(scaled * normed, axis=-1, keepdims=True)
        )
        branch[rows, :] = middle.astype(BF)
        if half == 0:
            sums[...] = jnp.sum(grad * normed, axis=0, keepdims=True)
            grad_mid[...] = middle
    grad_att[...] = nt(branch[...], wo_dup[...]).astype(BF)


def branch_back(info, *args):
    return pl.pallas_call(
        branch_kernel,
        name="norm_and_projection_backward",
        in_specs=[SM] + [VM] * 10,
        out_specs=[VM] * 4,
        out_shape=[sds((HALF, D), F32), sds((ROWS, D), BF), sds((ROWS, D), BF), sds((1, D), F32)],
        compiler_params=params(26),
        cost_estimate=cost(10**9, 10**7),
    )(info, *args)


def back_kernel(blocks, info, grad_att, rotated, value, stats, cosine, sine, lin):
    causal, wide = masks(info[1], keys_first=True)
    lane = lax.broadcasted_iota(jnp.int32, (256, 128), 1)
    base = 256 * blocks[0]
    grad_k = [jnp.zeros((256, 128), F32) for _ in blocks]
    grad_v = [jnp.zeros((256, 128), F32) for _ in blocks]
    for block in blocks:
        first, low, high = SPANS[block]
        rows = slice(first, first + 256)
        to = slice(first - base, first - base + 256)
        mask = wide if block == 1 else causal
        keys = rotated[low:high, 896:1024]
        vals = value[low:high, :]
        cos_b, sin_b = turns(cosine, block, info[1]), turns(sine, block, info[1])
        turned = []
        for head in range(HEADS):
            cols = slice(128 * head, 128 * head + 128)
            query, grad_o = rotated[rows, cols], grad_att[rows, cols]
            chance = jnp.exp(nt(keys, query) * 0.0625 + mask - stats[head : head + 1, rows])
            grad_p = nt(vals, grad_o) * 0.5
            inner = jnp.sum(chance * grad_p, axis=0, keepdims=True)
            grad_s = (chance * (grad_p - inner)).astype(BF)
            low_p = chance.astype(BF)
            back = tn(grad_s, keys) * 0.125
            turned.append(back * cos_b - pltpu.roll(back, 64, 1) * sin_b)
            for at in range((high - low) // 256):
                part = slice(256 * at, 256 * at + 256)
                grad_k[(low - base) // 256 + at] += nn(grad_s[part, :], query)
                grad_v[(low - base) // 256 + at] += nn(low_p[part, :], grad_o)
        turned.append(jnp.zeros((256, 128), F32))
        for pair in range(4):
            right = pltpu.roll(turned[2 * pair + 1], 64, 1)
            lin[to, 128 * pair : 128 * pair + 128] = jnp.where(
                lane < 64, turned[2 * pair], right
            ).astype(BF)
    for at, block in enumerate(blocks):
        rows = slice(256 * at, 256 * at + 256)
        cos_b, sin_b = turns(cosine, block, info[1]), turns(sine, block, info[1])
        back = grad_k[at] * 0.125
        back = back * cos_b - pltpu.roll(back, 64, 1) * sin_b
        back = pltpu.roll(back, 64, 1).astype(BF)
        lin[rows, 384:512] = jnp.where(lane < 64, lin[rows, 384:512], back)
        lin[rows, 512:640] = jnp.where(lane < 64, 0.0, grad_v[at]).astype(BF)


def back(blocks, info, *args):
    return pl.pallas_call(
        functools.partial(back_kernel, blocks),
        name="attention_backward",
        in_specs=[SM] + [VM] * 6,
        out_specs=VM,
        out_shape=sds((256 * len(blocks), 640), BF),
        compiler_params=params(20),
        cost_estimate=cost(10**9, 10**7, 10**6),
    )(info, *args)


def last_kernel(info, branch, lin_a, lin_b, sum_two, att, attn_t, w_cat, tok_0, tok_1,
                da_own, da_send, pack_keep, pack_send, grad_in):
    grad_in[:512, :] = nn(lin_a[...], w_cat[...])
    grad_in[512:, :] = nn(lin_b[...], w_cat[...])
    sum_one = jnp.zeros((1, D), F32)
    for rows, src, out in zip(half_rows(info), (tok_0, tok_1), (da_own, da_send), strict=True):
        field = src[...].astype(F32)
        grad = grad_in[rows, :]
        out[...] = grad.astype(out.dtype)
        sum_one = sum_one + jnp.sum(grad * (field * factor_of(field)), axis=0, keepdims=True)
    sum_b = jnp.sum(lin_a[...].astype(F32), axis=0, keepdims=True)
    sum_b = sum_b + jnp.sum(lin_b[...].astype(F32), axis=0, keepdims=True)
    grad_w = nn(attn_t[:, :512], lin_a[...]) + nn(attn_t[:, 512:], lin_b[...])
    grad_o = tn(branch[...], att[...])
    first_w = grad_w[:, :512]
    second_w = jnp.concatenate([grad_o[:, :384], grad_o[:, 384:] + grad_w[:, 512:]], axis=1)
    sum_two = sum_two[...]
    extra_a = {0: sum_b[:, :512], 1: sum_one[:, :512], 2: sum_two[:, :512]}
    extra_b = {0: sum_b[:, 512:], 1: sum_one[:, 512:], 2: sum_two[:, 512:]}

    def lines(extra):
        count = extra.shape[1] // 128
        parts = [extra[:, 128 * at : 128 * at + 128] for at in range(count)]
        return jnp.concatenate([*parts, jnp.zeros((PIECE - count, 128), F32)], axis=0)

    for piece in range(16):
        rows = slice(PIECE * piece, PIECE * piece + PIECE)
        packs = []
        for grads, extra in ((first_w, extra_a), (second_w, extra_b)):
            more = lines(extra[piece]) if piece in extra else jnp.zeros((PIECE, 128), F32)
            packs.append((grads[rows, :], more))
        for at, cols in ((0, slice(0, 512)), (1, slice(512, 640))):
            low, high = packs[0][at], packs[1][at]
            pack_keep[piece, :, cols] = jnp.where(info[4] == 0, low, high).astype(BF)
            pack_send[piece, :, cols] = jnp.where(info[4] == 0, high, low).astype(BF)


def last(info, *args):
    return pl.pallas_call(
        last_kernel,
        name="attention_weight_gradients",
        in_specs=[SM] + [VM] * 9,
        out_specs=[VM] * 4,
        out_shape=[
            sds((HALF, D), F32),
            sds((HALF, D), BF),
            sds((16, PIECE, 640), BF),
            sds((16, PIECE, 640), BF),
        ],
        scratch_shapes=[pltpu.VMEM((ROWS, D), F32)],
        compiler_params=params(28),
        cost_estimate=cost(3 * 10**9, 16 * 10**6),
    )(info, *args)


def wide_kernel(got, info, own, other, *refs):
    out, stage, sems = refs[-3:]
    copies = []
    for at, (slot, src) in enumerate(((2, own), (5, other))):
        half = lax.bitwise_xor(info[slot] // 8, got)
        core = lax.rem(info[4] + at, 2)
        for piece in range(8):
            stage[at, piece] = src[piece].astype(F32)
            place = lax.bitwise_xor(jnp.int32(piece), lax.rem(info[slot], 8))
            sem = sems.at[at, piece]
            first = pltpu.make_async_copy(
                stage.at[at, piece], out.at[half, place, :, pl.ds(0, HID)], sem
            )
            second = pltpu.make_async_copy(
                stage.at[at, piece, :, pl.ds(128, HID - 128)],
                out.at[half, place, :, pl.ds(HID, HID - 128)],
                sem,
            )
            pl.when(core == 0)(first.start)
            pl.when(core == 1)(second.start)
            copies.append((core, first, second))
    for core, first, second in copies:
        pl.when(core == 0)(first.wait)
        pl.when(core == 1)(second.wait)


def lanes(pieces, low, count):
    return pl.BlockSpec(
        (pl.Element(pieces), pl.Element(PIECE), pl.Element(count)), lambda _: (0, 0, low)
    )


def wide(info, part, own, other, before=None, weigh=10**7):
    info = jnp.stack([info[0], info[1], info[2 + part], info[3], info[4], info[5 + part], info[6]])
    more = [] if before is None else [before]
    anywhere = pl.BlockSpec(memory_space=pl.ANY)
    return pl.pallas_call(
        functools.partial(wide_kernel, len(more)),
        name="gradients_wide",
        grid=(1,),
        in_specs=[SM] + [lanes(8, 0, HID)] * 2 + [anywhere] * len(more),
        out_specs=anywhere,
        out_shape=sds((2, 8, PIECE, 2432), F32),
        scratch_shapes=[pltpu.VMEM((2, 8, PIECE, HID), F32), pltpu.SemaphoreType.DMA((2, 8))],
        input_output_aliases={3: 0} if more else {},
        compiler_params=params(16),
        cost_estimate=cost(weigh, 14 * 10**6),
    )(info, own, other, *more)


def model_order(info, mask, own, got, cols):
    pieces = []
    for q in range(16):
        place = lax.bitwise_xor(jnp.int32(q), info[mask])
        at = lax.rem(place, 8)
        ours, theirs = own[at, :, cols].astype(F32), got[at, :, cols].astype(F32)
        pieces.append(jnp.where(place < 8, ours, theirs))
    return jnp.concatenate(pieces, axis=0)


def tall_kernel(info, *refs):
    down, stage, sems = refs[-3:]
    copies = []
    for step in range(19):
        tile = step if step < 10 else step - 9
        part = int(tile >= SPLIT // 128)
        own, got, other, other_got = refs[4 * part : 4 * part + 4]
        low = 128 * tile - SPLIT * part
        cols = slice(low, low + 128)

        def ours(step=step, part=part, own=own, got=got, cols=cols):
            stage[step] = model_order(info, 2 + part, own, got, cols).T

        def theirs(step=step, part=part, own=other, got=other_got, cols=cols):
            stage[step] = model_order(info, 5 + part, own, got, cols).T

        pl.when((info[4] == 0) == (step < 10))(ours)
        pl.when((info[4] == 0) != (step < 10))(theirs)
        rows = pl.ds(128 * step, 128)
        copies.append(pltpu.make_async_copy(stage.at[step], down.at[rows, :], sems.at[step]))
        copies[-1].start()
    for copy in copies:
        copy.wait()


def tall(info, first, second):
    return pl.pallas_call(
        tall_kernel,
        name="gradients_tall",
        grid=(1,),
        in_specs=[SM] + [lanes(8, at, SPLIT) for at in (HID, 0) * 2]
        + [lanes(8, at, HID - SPLIT) for at in (HID, 0) * 2],
        out_specs=pl.BlockSpec(memory_space=pl.ANY),
        out_shape=sds((2432, D), F32),
        scratch_shapes=[pltpu.VMEM((19, 128, D), F32), pltpu.SemaphoreType.DMA((19,))],
        compiler_params=params(24),
        cost_estimate=cost(10**7, 14 * 10**6),
    )(info, *first, *second)


def small_kernel(info, own, got, other, other_got, query, key, value, out, extras):
    for first in (True, False):
        here = (info[4] == 0) == first

        def write(mask, one, two, first=first):
            for tile in range(4):
                turned = model_order(info, mask, one, two, slice(128 * tile, 128 * tile + 128)).T
                big, little = (query, key) if first else (out, value)
                if tile < 3:
                    big[128 * tile : 128 * tile + 128, :] = turned
                else:
                    big[384:, :] = turned[:64, :]
                    little[...] = turned[64:, :]
            more = model_order(info, mask, one, two, slice(512, 640))
            for piece in range(3):
                extras[0 if first else 1, piece] = more[PIECE * piece : PIECE * piece + 8, :]

        @pl.when(here)
        def _(write=write):
            write(2, own, got)

        @pl.when(jnp.logical_not(here))
        def _(write=write):
            write(5, other, other_got)


def small(info, *arrays):
    kept = [(448, D), (64, D), (64, D), (448, D), (2, 3, 8, 128)]
    return pl.pallas_call(
        small_kernel,
        name="gradients_small",
        grid=(1,),
        in_specs=[SM] + [lanes(8, at + SPLIT, 640) for at in (HID, 0) * 2],
        out_specs=[VM] * len(kept),
        out_shape=[sds(shape, F32) for shape in kept],
        compiler_params=params(20),
        cost_estimate=cost(10**7, 6 * 10**6),
    )(info, *arrays)


def send(field, axis, shift=1):
    size = lax.axis_size(axis)
    return lax.ppermute(field, axis, [(i, (i + shift) % size) for i in range(size)])


def after(field, *others):
    return lax.optimization_barrier((field, *others))[0]


def after_all(fields, *others):
    return lax.optimization_barrier((*fields, *others))[: len(fields)]


def in_order(place, own, rec):
    first = place == 0
    return jnp.where(first, own, rec), jnp.where(first, rec, own)


def swapped(weight, axis=-1):
    first, second = jnp.split(weight, 2, axis=axis)
    return jnp.concatenate([-second, first], axis=axis)


def tables():
    freq_index = np.arange(HD // 2, dtype=np.float32)
    inverse = np.float32(ROPE_BASE) ** (np.float32(-2.0) * freq_index / np.float32(HD))
    angle = np.arange(512, dtype=np.float32)[:, None] * inverse.astype(np.float32)[None, :]
    cosine, sine = np.cos(angle), np.sin(angle)
    return (
        jnp.asarray(np.concatenate([cosine] * 4, axis=1)),
        jnp.asarray(np.concatenate([sine, sine, -sine, -sine], axis=1)),
    )


ORDERS = (
    (("x", "a"), ("x", "b"), ("y", "a"), ("y", "b")),
    (("x", "b"), ("x", "a"), ("y", "b"), ("y", "a")),
), (
    (("y", "a"), ("y", "b"), ("x", "a"), ("x", "b")),
    (("y", "b"), ("y", "a"), ("x", "b"), ("x", "a")),
)
CHIPS = ("x", "zl", "y", "c")


def bit(place, kind):
    return (place ^ (place >> 1)) & 1 if kind == "a" else place >> 1


def mask_of(part, core, places):
    mask = 0
    for axis, kind in ORDERS[part][core]:
        mask = 2 * mask + bit(places[axis], kind)
    return mask


def swap(field, part, *steps):
    pairs = []
    for x in range(4):
        for zl in range(2):
            for y in range(4):
                for c in range(2):
                    to = {"x": x, "y": y}
                    for axis, kind in (ORDERS[part][c][step] for step in steps):
                        to[axis] = to[axis] ^ 1 if kind == "a" else 3 - to[axis]
                    here = ((x * 2 + zl) * 4 + y) * 2 + c
                    pairs.append((here, ((to["x"] * 2 + zl) * 4 + to["y"]) * 2 + c))
    return lax.ppermute(field, CHIPS, pairs)


def swap_two(one, two, step):
    return swap(one, 0, step), swap(two, 1, step)


def spread(one, two, one_r, two_r):
    one, two = jnp.concatenate([one, one_r]), jnp.concatenate([two, two_r])
    return lax.optimization_barrier((one, two))


def add(one, two):
    return (one.astype(F32) + two.astype(F32)).astype(BF)


def shards(tokens, long_count, attn_gain, w_query, b_query, w_key, b_key, w_value, b_value,
           w_out, mlp_gain, w_gate, w_up, w_down, cotangent):
    at_x, at_y, at_c, at_t = (lax.axis_index(a) for a in ("x", "y", "c", "t"))
    places = {"x": at_x, "y": at_y}
    masks_0 = [mask_of(part, 0, places) for part in (0, 1)]
    masks_1 = [mask_of(part, 1, places) for part in (0, 1)]
    mine = [jnp.where(at_c == 0, a, b) for a, b in zip(masks_0, masks_1, strict=True)]
    theirs = [jnp.where(at_c == 0, b, a) for a, b in zip(masks_0, masks_1, strict=True)]
    info = jnp.stack([at_t, long_count[0], *mine, at_c, *theirs]).astype(jnp.int32)
    gain_one = attn_gain.astype(F32)[None, :]
    gain_two = mlp_gain.astype(F32)[None, :]

    tok_0, tok_1 = tokens, send(tokens, "t")
    half_out = lax.dynamic_slice(w_out, (at_c * SLAB, 0), (SLAB, D))
    half_out = send(half_out, "t")
    cot_1 = send(cotangent[: HALF // 2], "t")

    wq, wk, wv = w_query.T, w_key.T, w_value.T
    heads = wq.reshape(HEADS, HD, D)
    heads = jnp.concatenate([heads, swapped(heads, 1)], axis=1).reshape(HEADS * 128, D)
    w_all = jnp.concatenate([heads, wk, swapped(wk, 0), wv, wv], axis=0)
    bias = b_query.reshape(HEADS, HD)
    bias = jnp.concatenate([bias, swapped(bias)], axis=-1).reshape(HEADS * 128)
    b_all = jnp.concatenate([bias, b_key, swapped(b_key), b_value, b_value]).astype(F32)[None, :]
    cosine, sine = tables()
    attn_in, rotated, value, stats, att_0, att_1, att_keep = attention(
        info, tok_0, tok_1, gain_one, w_all, b_all, cosine, sine
    )
    rec_0 = send(att_1, "t")

    half_out, wq, w_out, _ = lax.optimization_barrier((half_out, wq, w_out, att_0))
    half_rec = send(half_out, "c")
    rec_1 = send(after(att_0, half_rec), "t")
    cot_0, cot_0_rec = cotangent, send(cotangent, "c")
    g_0x, g_0y = turn(info, after(cot_0, half_rec), cot_0_rec)
    cot_1 = jnp.concatenate([cot_1, send(after(cotangent, g_0x)[HALF // 2 :], "t")])
    cot_1_rec = send(cot_1, "c")
    half_out = in_order(at_c, half_out, half_rec)
    no_rows = jnp.zeros((HD, D), BF)
    other_out = jnp.concatenate([*half_out, no_rows])
    this_out = jnp.concatenate([w_out, no_rows])
    w_cat = jnp.concatenate([wq, wk, jnp.zeros((HD, D), BF), wv], axis=0)
    wo_dup = w_out.reshape(HEADS, HD, D)
    wo_dup = jnp.concatenate([wo_dup, wo_dup], axis=1).reshape(HEADS * 128, D)
    rec_0, w_cat, wo_dup, g_0x, g_0y = lax.optimization_barrier((rec_0, w_cat, wo_dup, g_0x, g_0y))

    hid_0, m_0 = project(att_0, rec_0, this_out, other_out, tok_0, gain_two)
    m_0_rec = send(m_0, "c")
    attn_t = flip(after(attn_in, m_0))
    act_0, gate_0, up_0, out_0, out_0_oth, dm_0, dm_0_oth = feed(
        info, m_0, after(m_0_rec, attn_t), cot_0, cot_0_rec, w_gate, w_up, w_down
    )
    hid_1, m_1 = project(att_1, after(rec_1, act_0), this_out, other_out, tok_1, gain_two)
    m_1_rec = send(m_1, "c")
    m_0x, m_0y = turn(info, after(m_0, m_1), m_0_rec)
    dm_0 = add(dm_0, after(send(dm_0_oth, "c"), m_0x))
    dm_0_rec = send(dm_0, "t")
    act_1, gate_1, up_1, out_1, out_1_oth, dm_1, dm_1_oth = feed(
        info, after(m_1, dm_0), m_1_rec, cot_1, cot_1_rec, w_gate, w_up, w_down
    )
    m_1x, m_1y = turn(info, after(m_1, dm_1, dm_0_rec), m_1_rec)
    g_1x, g_1y = turn(info, after(cot_1, m_1x), cot_1_rec)
    dm_1 = add(dm_1, after(send(dm_1_oth, "c"), g_1x))
    dm_1_rec = send(dm_1, "t")

    gate_k, gate_g = weight_grad(m_0x, m_1x, gate_0, after(gate_1, dm_1, dm_0_rec), 0, 5)
    gate_r = swap(gate_g, 0, 0)
    up_k, up_g = weight_grad(m_0y, m_1y, up_0, after(up_1, gate_g), 0, 5)
    up_r = swap(up_g, 1, 0)
    out_rec = [send(after(field, dm_1), "c") for field in (out_0_oth, out_1_oth)]
    mine, theirs = halves(out_0, out_1, *after_all(out_rec, up_g))
    theirs_rec = send(theirs, "t")

    grad_mid, branch, grad_att, sum_two = branch_back(
        info, dm_0, dm_1, after(dm_1_rec, mine), dm_0_rec, cot_0, cot_1, hid_0, hid_1,
        gain_two, wo_dup,
    )
    lin_a = back((0, 1), info, grad_att, rotated, value, stats, cosine, sine)
    lin_b = back((2,), info, after(grad_att, lin_a), rotated, value, stats, cosine, sine)
    theirs_rec = after(theirs_rec, lin_b)
    output = (hid_0 + mine.astype(F32) + theirs_rec.astype(F32)).astype(BF)
    da_own, da_send, pack_k, pack_g = last(
        info, branch, lin_a, after(lin_b, output), sum_two, att_keep, attn_t, w_cat, tok_0, tok_1
    )
    pack_r = send(pack_g, "c")

    (gate_k, gate_g), (up_k, up_g) = fold(
        info, 2, [((gate_k, after(gate_r, pack_g)), None, 0)], [((up_k, up_r), None, 0)]
    )
    gate_r, up_r = swap_two(gate_g, up_g, 1)
    low_k, low_g = weight_grad(g_0x, g_1x, act_0, after(act_1, gate_g), 0, 2)
    low_r = swap(low_g, 0, 0)
    ((pack_k, pack_g),) = fold(info, 2, [((pack_k, after(pack_r, low_g)), 2, 15)])
    pack_r = swap(pack_g, 0, 0)
    high_k, high_g = weight_grad(g_0y, g_1y, act_0, after(act_1, pack_g), 2, 3)
    high_r = swap(high_g, 1, 0)
    ((pack_k, pack_g),) = fold(
        info, 2, [((pack_k, after(pack_r, high_g, gate_r, up_r)), None, 0)], weigh=3 * 10**13
    )
    pack_r = swap(pack_g, 0, 1)
    (low_k, low_g), (high_k, high_g) = fold(
        info, 2, [((low_k, after(low_r, pack_g)), None, 0)], [((high_k, high_r), None, 0)]
    )
    low_r, high_r = swap_two(low_g, high_g, 1)
    da_rec = send(after(da_send, low_g), "t")
    (one_k, one_g), (two_k, two_g) = fold(
        info,
        2,
        [
            ((gate_k, after(gate_r, low_g)), 2, 3),
            ((low_k, low_r), 2, 3),
            ((pack_k, pack_r), None, 0),
        ],
        [((up_k, up_r), 3, 3), ((high_k, high_r), 3, 3)],
    )
    one_r, two_r = swap_two(one_g, two_g, 2)

    (one_k, one_g), (two_k, two_g) = fold(
        info, 2, [((one_k, one_r), None, 0)], [((two_k, two_r), None, 0)]
    )
    one_r, two_r = swap_two(one_g, two_g, 3)
    ((part,),) = fold(info, 1, [((one_k, one_r), None, 0), ((two_k, two_r), None, 0)])
    part_r = send(part, "zl")

    field = tokens.astype(F32)
    factor = factor_of(field)
    normed = field * factor
    scaled = (da_own + after(da_rec, part).astype(F32)) * gain_one
    grad_tokens = grad_mid + factor * (
        scaled - normed * jnp.mean(scaled * normed, axis=-1, keepdims=True)
    )
    grad_tokens = grad_tokens.astype(BF)
    part = add(part, after(part_r, grad_tokens))

    wide_one = HID + SPLIT + 640
    one, two = part[..., :wide_one], part[..., wide_one:]
    for step in (3, 2, 1):
        one, two = spread(one, two, *swap_two(one, two, step))
    low_r, high_r = swap_two(one[..., HID:], two[..., HID:], 0)
    gate_r, up_r = swap_two(one[..., :HID], two[..., :HID], 0)
    one_c = send(one, "c")
    two_c = send(after(two, one_c), "c")
    grad_w_gate = wide(info, 0, one, one_c, weigh=3 * 10**13)
    grad_w_up = wide(info, 1, two, after(two_c, grad_w_gate))
    low_r, high_r = after_all((low_r, high_r), grad_w_up)
    low_c, high_c = send(low_r, "c"), send(high_r, "c")
    grad_wq, grad_wk, grad_wv, grad_wo, extras = small(info, one, low_r, one_c, low_c)
    grad_w_down = tall(info, (one, low_r, one_c, low_c), (two, high_r, two_c, high_c))
    gate_r, up_r = after_all((gate_r, up_r), grad_wo, grad_w_down)
    gate_c = send(gate_r, "c")
    up_c = send(up_r, "c")
    grad_w_gate = wide(info, 0, gate_r, gate_c, grad_w_gate)
    grad_w_up = wide(info, 1, up_r, after(up_c, grad_w_gate), grad_w_up)
    grad_w_gate, grad_w_up = grad_w_gate.reshape(D, 2432), grad_w_up.reshape(D, 2432)
    gains = extras[:, 1:].reshape(2, 2, 1024)
    gains = jnp.concatenate([gains[0, :, :512], gains[1, :, :384]], axis=1)
    gains = gains + after(send(gains, "t"), grad_w_up)
    biases = extras[0, 0, :4].reshape(512)

    return (
        output,
        grad_tokens,
        gains[0],
        grad_wq.T,
        biases[:448],
        grad_wk.T,
        biases[448:],
        grad_wv.T,
        extras[1, 0, 0, 64:],
        grad_wo,
        gains[1],
        grad_w_gate,
        grad_w_up,
        grad_w_down,
    )


def solution(mesh):
    fine = Mesh(mesh.devices.reshape(4, 2, 4, 2, 2), ("x", "zl", "y", "c", "t"))
    dp = ("x", "zl", "y", "c")
    rows, cols, split = P((*dp, "t"), None), P(None, "t"), P("t")
    down = P("t", None)
    return jax.shard_map(
        shards,
        mesh=fine,
        in_specs=(
            rows, P(dp), P(), cols, split, cols, split, cols, split, down, P(), cols, cols, down,
            rows,
        ),
        out_specs=(
            rows, rows, P(), cols, split, cols, split, cols, split, down, P(), cols, cols, down,
        ),
        check_vma=False,
    )
```

```python
import functools

import jax
import jax.numpy as jnp
import numpy as np
from jax import lax
from jax.experimental import pallas as pl
from jax.experimental.pallas import tpu as pltpu
from jax.sharding import Mesh
from jax.sharding import PartitionSpec as P

HD = 64
EPSILON = 1e-06
ROPE_BASE = 1000000.0
BF = jnp.bfloat16
F32 = jnp.float32

D = 896
HALF = 384
ROWS = 768
HEADS = 7
PIECE = 56
SLAB = 224
HID = 1280
SPLIT = 512
STEP = 1152
CHUNK = 256
MIB = 1024 * 1024

VM = pl.BlockSpec(memory_space=pltpu.VMEM)
SM = pl.BlockSpec(memory_space=pltpu.SMEM)


def sds(shape, dtype):
    return jax.ShapeDtypeStruct(shape, dtype)


def nn(a, b):
    return lax.dot_general(a, b, (((1,), (0,)), ((), ())), preferred_element_type=F32)


def nt(a, b):
    return lax.dot_general(a, b, (((1,), (1,)), ((), ())), preferred_element_type=F32)


def tn(a, b):
    return lax.dot_general(a, b, (((0,), (0,)), ((), ())), preferred_element_type=F32)


def half_rows(info):
    return [
        pl.ds(pl.multiple_of(place * HALF, HALF), HALF) for place in (info[0], 1 - info[0])
    ]


def factor_of(field):
    return lax.rsqrt(jnp.mean(field * field, axis=-1, keepdims=True) + EPSILON)


def params(mib):
    return pltpu.CompilerParams(vmem_limit_bytes=mib * MIB)


def cost(flops, size, trans=0):
    return pl.CostEstimate(flops=flops // 1000, bytes_accessed=size // 1000, transcendentals=trans // 1000)


def masks(is_long, keys_first=False):
    row = lax.broadcasted_iota(jnp.int32, (256, 256), 0)
    col = lax.broadcasted_iota(jnp.int32, (256, 256), 1)
    causal = jnp.where(row <= col if keys_first else col <= row, 0.0, -1e30).astype(F32)
    before = jnp.full((256, 256), jnp.where(is_long == 1, 0.0, -1e30).astype(F32))
    return causal, jnp.concatenate([before, causal], axis=0 if keys_first else 1)


def turns(ref, block, is_long):
    pair = ref[:256, :]
    if block == 1:
        pair = jnp.where(is_long == 1, ref[256:, :], pair)
    lane = lax.broadcasted_iota(jnp.int32, (256, 128), 1)
    swapped_pair = pltpu.roll(pair, 32, 1)
    cosine_here = lax.rem(lane, 64) < 32
    cosine = jnp.where(cosine_here, pair, swapped_pair)
    sine = jnp.where(cosine_here, swapped_pair, pair)
    return cosine, jnp.where(lane < 64, sine, -sine)


SPANS = ((0, 0, 256), (256, 0, 512), (512, 512, 768))


def attention_kernel(info, tok_0, tok_1, gain, w_all, b_all, table,
                     attn_in, rotated, value, stats, att_0, att_1, att_keep):
    for rows, src in zip(half_rows(info), (tok_0, tok_1), strict=True):
        field = src[...].astype(F32)
        attn_in[rows, :] = (field * factor_of(field) * gain[...]).astype(BF)
    for block in range(3):
        rows = slice(256 * block, 256 * block + 256)
        lin = nt(attn_in[rows, :], w_all[...]) + b_all[...]
        cos_b, sin_b = turns(table, block, info[1])
        for head in range(HEADS + 1):
            part = lin[:, 128 * head : 128 * head + 128]
            turned = part * cos_b + pltpu.roll(part, 64, 1) * sin_b
            rotated[rows, 128 * head : 128 * head + 128] = turned.astype(BF)
        value[rows, :] = lin[:, 1024:1152].astype(BF)
    causal, wide = masks(info[1])
    lane = lax.broadcasted_iota(jnp.int32, (256, 128), 1)
    for block, (first, low, high) in enumerate(SPANS):
        rows = slice(first, first + 256)
        mask = wide if block == 1 else causal
        keys = rotated[low:high, 1024 - 128 :]
        vals = value[low:high, :]
        kept = jnp.zeros((256, 128), F32)
        outs = []
        for head in range(HEADS):
            scores = nt(rotated[rows, 128 * head : 128 * head + 128], keys) * 0.0625 + mask
            top = jnp.max(scores, axis=-1, keepdims=True)
            expo = jnp.exp(scores - top)
            total = jnp.sum(expo, axis=-1, keepdims=True)
            kept = jnp.where(lane == head, top + jnp.log(total), kept)
            outs.append(nn(expo.astype(BF), vals) * (1.0 / total))
        stats[:, rows] = kept.T[:8, :]
        outs.append(jnp.zeros((256, 128), F32))
        for pair in range(4):
            both = jnp.where(lane < 64, outs[2 * pair], outs[2 * pair + 1])
            att_keep[rows, 128 * pair : 128 * pair + 128] = both.astype(BF)
    lane = lax.broadcasted_iota(jnp.int32, (64, 128), 1)
    for rows, out in zip(half_rows(info), (att_0, att_1), strict=True):
        out[:HALF, :] = att_keep[rows, :384]
        for pair in range(3):
            low = pl.multiple_of(rows.start + 128 * pair, 128)
            part = att_keep[pl.ds(low, 128), 384:].astype(F32)
            left, right = part[:64, :], pltpu.roll(part[64:, :], 64, 1)
            out[HALF:, 128 * pair : 128 * pair + 128] = jnp.where(lane < 64, left, right).astype(BF)


def attention(info, *args):
    return pl.pallas_call(
        attention_kernel,
        name="attention_forward",
        in_specs=[SM] + [VM] * 6,
        out_specs=[VM] * 7,
        out_shape=[
            sds((ROWS, D), BF),
            pltpu.HBM((ROWS, 1024), BF),
            pltpu.HBM((ROWS, 128), BF),
            pltpu.HBM((8, ROWS), F32),
            sds((448, 384), BF),
            sds((448, 384), BF),
            pltpu.HBM((ROWS, 512), BF),
        ],
        compiler_params=params(26),
        cost_estimate=cost(4 * 10**9, 12 * 10**6, 3 * 10**6),
    )(info, *args)


def project_kernel(att_own, att_rec, wo_own, wo_rec, tok, gain, hidden, mlp_in, full):
    lane = lax.broadcasted_iota(jnp.int32, (64, 128), 1)
    field = tok[...].astype(F32)
    for att, weight in ((att_own, wo_own), (att_rec, wo_rec)):
        full[:, :384] = att[:HALF, :]
        for pair in range(3):
            both = att[HALF:, 128 * pair : 128 * pair + 128].astype(F32)
            low = 128 * pair
            full[low : low + 64, 384:] = jnp.where(lane < 64, both, 0.0).astype(BF)
            both = jnp.where(lane < 64, pltpu.roll(both, 64, 1), 0.0)
            full[low + 64 : low + 128, 384:] = both.astype(BF)
        field = field + nn(full[...], weight[...])
    hidden[...] = field
    mlp_in[...] = (field * factor_of(field) * gain[...]).astype(BF)


def project(att_own, att_rec, wo_own, wo_rec, tok, gain):
    return pl.pallas_call(
        project_kernel,
        name="project_norm",
        in_specs=[VM] * 6,
        out_specs=[VM] * 2,
        out_shape=[pltpu.HBM((HALF, D), F32), sds((HALF, D), BF)],
        scratch_shapes=[pltpu.VMEM((HALF, 512), BF)],
        compiler_params=params(14),
        cost_estimate=cost(7 * 10**8, 6 * 10**6),
    )(att_own, att_rec, wo_own, wo_rec, tok, gain)


def turn_kernel(info, own, rec, first, second):
    for at, src in enumerate((own, rec)):
        cols = slice(HALF * at, HALF * at + HALF)
        for slab in range(4):
            turned = src[:, SLAB * slab : SLAB * slab + SLAB].astype(F32).T.astype(BF)
            for mask, out in ((info[2], first), (info[3], second)):
                slot = lax.bitwise_xor(jnp.int32(slab), mask // 4)
                out[pl.ds(pl.multiple_of(slot * SLAB, SLAB), SLAB), cols] = turned


def turn(info, own, rec, weigh=10**6):
    return pl.pallas_call(
        turn_kernel,
        name="transpose_rows",
        in_specs=[SM] + [VM] * 2,
        out_specs=[VM] * 2,
        out_shape=[pltpu.HBM((D, 2 * HALF), BF)] * 2,
        compiler_params=params(14),
        cost_estimate=cost(weigh, 4 * 10**6),
    )(info, own, rec)


def flip_kernel(source, out):
    for block in range(3):
        rows = slice(256 * block, 256 * block + 256)
        out[:, rows] = source[rows, :].astype(F32).T.astype(BF)


def flip(source):
    return pl.pallas_call(
        flip_kernel,
        name="transpose_whole",
        in_specs=[VM],
        out_specs=VM,
        out_shape=pltpu.HBM((D, ROWS), BF),
        compiler_params=params(8),
        cost_estimate=cost(3 * 10**13, 3 * 10**6),
    )(source)


def feed_kernel(info, m_own, m_rec, g_own, g_rec, wg, wu, wd_in, act, gate_g, up_g, *rest):
    ends, sums, wd = rest[:4], rest[4:8], rest[8]
    step = pl.program_id(0)
    wd[...] = wd_in[...]

    @pl.when((step == 0) & (info[4] == 1))
    def _():
        wd[:128, :] = jnp.zeros((128, D), BF)

    @pl.when(step == 0)
    def _():
        for total in sums:
            total[...] = jnp.zeros_like(total)

    for at, (m, g) in enumerate(((m_own, g_own), (m_rec, g_rec))):
        rows = slice(HALF * at, HALF * at + HALF)
        gate = nn(m[...], wg[...])
        up = nn(m[...], wu[...])
        grad = nt(g[...], wd[...])
        sig = 1.0 / (1.0 + jnp.exp(-gate))
        swish = gate * sig
        act[rows, :] = (swish * up).astype(BF)
        up_g[rows, :] = (grad * swish).astype(BF)
        gate_g[rows, :] = (grad * up * (sig + swish * (1.0 - sig))).astype(BF)
        sums[at][...] += nn(act[rows, :], wd[...])
        sums[2 + at][...] += nt(gate_g[rows, :], wg[...]) + nt(up_g[rows, :], wu[...])

    @pl.when(step == pl.num_programs(0) - 1)
    def _():
        for end, total in zip(ends, sums, strict=True):
            end[...] = total[...].astype(BF)


def whole(shape):
    zeros = (0,) * len(shape)
    return pl.BlockSpec(shape, lambda *_: zeros, pipeline_mode=pl.Buffered(1))


def feed(info, m_own, m_rec, g_own, g_rec, wg, wu, wd):
    rows = whole((HALF, D))

    def start(j, info):
        return pl.multiple_of(info[4] * STEP + j * CHUNK, 128)

    wide = pl.BlockSpec((pl.Element(D), pl.Element(CHUNK)), lambda j, info: (0, start(j, info)))
    tall = pl.BlockSpec((pl.Element(CHUNK), pl.Element(D)), lambda j, info: (start(j, info), 0))
    kept = pl.BlockSpec((2 * HALF, CHUNK), lambda j, info: (0, j))
    return pl.pallas_call(
        feed_kernel,
        name="feed_forward_and_back",
        grid_spec=pltpu.PrefetchScalarGridSpec(
            num_scalar_prefetch=1,
            grid=(HID // CHUNK,),
            in_specs=[rows] * 4 + [wide, wide, tall],
            out_specs=[kept] * 3 + [rows] * 4,
            scratch_shapes=[pltpu.VMEM((HALF, D), F32)] * 4 + [pltpu.VMEM((CHUNK, D), BF)],
        ),
        out_shape=[pltpu.HBM((2 * HALF, HID), BF)] * 3 + [sds((HALF, D), BF)] * 4,
        compiler_params=params(30),
        cost_estimate=cost(10**10, 20 * 10**6, 10**6),
    )(info, m_own, m_rec, g_own, g_rec, wg, wu, wd)


def halves_kernel(own_0, own_1, rec_0, rec_1, mine, theirs):
    for own, rec, out in ((own_0, rec_0, mine), (own_1, rec_1, theirs)):
        out[...] = (own[...].astype(F32) + rec[...].astype(F32)).astype(BF)


def halves(*args):
    return pl.pallas_call(
        halves_kernel,
        name="sum_cores_rows",
        in_specs=[VM] * 4,
        out_specs=[VM] * 2,
        out_shape=[sds((HALF, D), BF)] * 2,
        compiler_params=params(10),
        cost_estimate=cost(3 * 10**13, 4 * 10**6),
    )(*args)


def weight_kernel(left_0, left_1, right_0, right_1, *outs):
    product = nn(left_0[...], right_0[...]) + nn(left_1[...], right_1[...])
    count = 16 // len(outs)
    for piece in range(16):
        low = PIECE * piece
        outs[piece // count][piece % count] = product[low : low + PIECE, :].astype(BF)


def weight_grad(left_0, left_1, right_0, right_1, first, count, parts=2, weigh=1):
    left = whole((D, 2 * HALF))
    right = pl.BlockSpec((2 * HALF, CHUNK), lambda j: (0, j + first))
    out = pl.BlockSpec((16 // parts, PIECE, CHUNK), lambda j: (0, 0, j))
    return pl.pallas_call(
        weight_kernel,
        name="weight_gradient",
        grid=(count,),
        in_specs=[left] * 2 + [right] * 2,
        out_specs=[out] * parts,
        out_shape=[pltpu.HBM((16 // parts, PIECE, CHUNK * count), BF)] * parts,
        compiler_params=params(16),
        cost_estimate=cost(7 * 10**8 * count * weigh, 8 * 10**6),
    )(left_0, left_1, right_0, right_1)


def fold_kernel(plan, ways, info, *refs):
    ins = list(refs[: sum(count for group in plan for count, _, _ in group)])
    outs = list(refs[len(ins) :])
    for group in plan:
        out = [outs.pop(0) for _ in range(ways)]
        low = 0
        for count, mask, bits in group:
            terms = [ins.pop(0) for _ in range(count)]
            pieces, _, wide = terms[0].shape
            each = pieces // ways
            for at in range(pieces):
                piece = at
                if mask is not None:
                    piece = lax.bitwise_xor(jnp.int32(at), lax.bitwise_and(info[mask], bits))
                total = terms[0][piece].astype(F32)
                for term in terms[1:]:
                    total = total + term[piece].astype(F32)
                out[at // each][at % each, :, low : low + wide] = total.astype(BF)
            low += wide


def fold(info, ways, *groups, weigh=10**7):
    plan = [[(len(terms), mask, bits) for terms, mask, bits in group] for group in groups]
    ins = [ref for group in groups for terms, _, _ in group for ref in terms]
    shapes = []
    for group in groups:
        wide = sum(terms[0].shape[-1] for terms, _, _ in group)
        shapes += [sds((group[0][0][0].shape[0] // ways, PIECE, wide), BF)] * ways
    out = pl.pallas_call(
        functools.partial(fold_kernel, plan, ways),
        name="sum_parts",
        in_specs=[SM] + [VM] * len(ins),
        out_specs=[VM] * len(shapes),
        out_shape=shapes,
        compiler_params=params(20),
        cost_estimate=cost(weigh, 6 * 10**6),
    )(info, *ins)
    return [out[ways * at : ways * at + ways] for at in range(len(groups))]


def branch_kernel(info, dm_own_0, dm_own_1, dm_rec_0, dm_rec_1, cot_0, cot_1, hid_0, hid_1,
                  gain_two, wo_dup, grad_mid, branch, grad_att, sums):
    sets = (dm_own_0, dm_rec_0, cot_0, hid_0), (dm_own_1, dm_rec_1, cot_1, hid_1)
    for half, (rows, (own, rec, cot, hid)) in enumerate(zip(half_rows(info), sets, strict=True)):
        field = hid[...]
        factor = factor_of(field)
        normed = field * factor
        grad = own[...].astype(F32) + rec[...].astype(F32)
        scaled = grad * gain_two[...]
        middle = cot[...].astype(F32) + factor * (
            scaled - normed * jnp.mean(scaled * normed, axis=-1, keepdims=True)
        )
        branch[rows, :] = middle.astype(BF)
        if half == 0:
            sums[...] = jnp.sum(grad * normed, axis=0, keepdims=True)
            grad_mid[...] = middle
    grad_att[...] = nt(branch[...], wo_dup[...]).astype(BF)


def branch_back(info, *args):
    return pl.pallas_call(
        branch_kernel,
        name="norm_and_projection_backward",
        in_specs=[SM] + [VM] * 10,
        out_specs=[VM] * 4,
        out_shape=[sds((HALF, D), F32), sds((ROWS, D), BF), sds((ROWS, D), BF), sds((1, D), F32)],
        compiler_params=params(26),
        cost_estimate=cost(10**9, 10**7),
    )(info, *args)


def back_kernel(blocks, info, grad_att, rotated, value, stats, table, lin):
    causal, wide = masks(info[1], keys_first=True)
    lane = lax.broadcasted_iota(jnp.int32, (256, 128), 1)
    base = 256 * blocks[0]
    grad_k = [jnp.zeros((256, 128), F32) for _ in blocks]
    grad_v = [jnp.zeros((256, 128), F32) for _ in blocks]
    for block in blocks:
        first, low, high = SPANS[block]
        rows = slice(first, first + 256)
        to = slice(first - base, first - base + 256)
        mask = wide if block == 1 else causal
        keys = rotated[low:high, 896:1024]
        vals = value[low:high, :]
        cos_b, sin_b = turns(table, block, info[1])
        turned = []
        for head in range(HEADS):
            cols = slice(128 * head, 128 * head + 128)
            query, grad_o = rotated[rows, cols], grad_att[rows, cols]
            chance = jnp.exp(nt(keys, query) * 0.0625 + mask - stats[head : head + 1, rows])
            grad_p = nt(vals, grad_o) * 0.5
            inner = jnp.sum(chance * grad_p, axis=0, keepdims=True)
            grad_s = (chance * (grad_p - inner)).astype(BF)
            low_p = chance.astype(BF)
            back = tn(grad_s, keys) * 0.125
            turned.append(back * cos_b - pltpu.roll(back, 64, 1) * sin_b)
            for at in range((high - low) // 256):
                part = slice(256 * at, 256 * at + 256)
                grad_k[(low - base) // 256 + at] += nn(grad_s[part, :], query)
                grad_v[(low - base) // 256 + at] += nn(low_p[part, :], grad_o)
        turned.append(jnp.zeros((256, 128), F32))
        for pair in range(4):
            right = pltpu.roll(turned[2 * pair + 1], 64, 1)
            lin[to, 128 * pair : 128 * pair + 128] = jnp.where(
                lane < 64, turned[2 * pair], right
            ).astype(BF)
    for at, block in enumerate(blocks):
        rows = slice(256 * at, 256 * at + 256)
        cos_b, sin_b = turns(table, block, info[1])
        back = grad_k[at] * 0.125
        back = back * cos_b - pltpu.roll(back, 64, 1) * sin_b
        back = pltpu.roll(back, 64, 1).astype(BF)
        lin[rows, 384:512] = jnp.where(lane < 64, lin[rows, 384:512], back)
        lin[rows, 512:640] = jnp.where(lane < 64, 0.0, grad_v[at]).astype(BF)


def back(blocks, info, *args):
    return pl.pallas_call(
        functools.partial(back_kernel, blocks),
        name="attention_backward",
        in_specs=[SM] + [VM] * 5,
        out_specs=VM,
        out_shape=sds((256 * len(blocks), 640), BF),
        compiler_params=params(20),
        cost_estimate=cost(10**9, 10**7, 10**6),
    )(info, *args)


def last_kernel(info, branch, lin_a, lin_b, sum_two, att, attn_t, w_cat, tok_0, tok_1,
                da_own, da_send, pack_keep, pack_send, grad_in):
    grad_in[:512, :] = nn(lin_a[...], w_cat[...])
    grad_in[512:, :] = nn(lin_b[...], w_cat[...])
    sum_one = jnp.zeros((1, D), F32)
    for rows, src, out in zip(half_rows(info), (tok_0, tok_1), (da_own, da_send), strict=True):
        field = src[...].astype(F32)
        grad = grad_in[rows, :]
        out[...] = grad.astype(out.dtype)
        sum_one = sum_one + jnp.sum(grad * (field * factor_of(field)), axis=0, keepdims=True)
    sum_b = jnp.sum(lin_a[...].astype(F32), axis=0, keepdims=True)
    sum_b = sum_b + jnp.sum(lin_b[...].astype(F32), axis=0, keepdims=True)
    grad_w = nn(attn_t[:, :512], lin_a[...]) + nn(attn_t[:, 512:], lin_b[...])
    grad_o = tn(branch[...], att[...])
    first_w = grad_w[:, :512]
    second_w = jnp.concatenate([grad_o[:, :384], grad_o[:, 384:] + grad_w[:, 512:]], axis=1)
    sum_two = sum_two[...]
    extra_a = {0: sum_b[:, :512], 1: sum_one[:, :512], 2: sum_two[:, :512]}
    extra_b = {0: sum_b[:, 512:], 1: sum_one[:, 512:], 2: sum_two[:, 512:]}

    def lines(extra):
        count = extra.shape[1] // 128
        parts = [extra[:, 128 * at : 128 * at + 128] for at in range(count)]
        return jnp.concatenate([*parts, jnp.zeros((PIECE - count, 128), F32)], axis=0)

    for piece in range(16):
        rows = slice(PIECE * piece, PIECE * piece + PIECE)
        packs = []
        for grads, extra in ((first_w, extra_a), (second_w, extra_b)):
            more = lines(extra[piece]) if piece in extra else jnp.zeros((PIECE, 128), F32)
            packs.append((grads[rows, :], more))
        for at, cols in ((0, slice(0, 512)), (1, slice(512, 640))):
            low, high = packs[0][at], packs[1][at]
            pack_keep[piece, :, cols] = jnp.where(info[4] == 0, low, high).astype(BF)
            pack_send[piece, :, cols] = jnp.where(info[4] == 0, high, low).astype(BF)


def last(info, *args):
    return pl.pallas_call(
        last_kernel,
        name="attention_weight_gradients",
        in_specs=[SM] + [VM] * 9,
        out_specs=[VM] * 4,
        out_shape=[
            sds((HALF, D), F32),
            sds((HALF, D), BF),
            sds((16, PIECE, 640), BF),
            sds((16, PIECE, 640), BF),
        ],
        scratch_shapes=[pltpu.VMEM((ROWS, D), F32)],
        compiler_params=params(28),
        cost_estimate=cost(3 * 10**9, 16 * 10**6),
    )(info, *args)


def wide_kernel(got, info, own, other, *refs):
    out, stage, sems = refs[-3:]
    copies = []
    for at, (slot, src) in enumerate(((2, own), (5, other))):
        half = lax.bitwise_xor(info[slot] // 8, got)
        core = lax.rem(info[4] + at, 2)
        for piece in range(8):
            stage[at, piece] = src[piece].astype(F32)
            place = lax.bitwise_xor(jnp.int32(piece), lax.rem(info[slot], 8))
            sem = sems.at[at, piece]
            first = pltpu.make_async_copy(
                stage.at[at, piece], out.at[half, place, :, pl.ds(0, HID)], sem
            )
            second = pltpu.make_async_copy(
                stage.at[at, piece, :, pl.ds(128, HID - 128)],
                out.at[half, place, :, pl.ds(HID, HID - 128)],
                sem,
            )
            pl.when(core == 0)(first.start)
            pl.when(core == 1)(second.start)
            copies.append((core, first, second))
    for core, first, second in copies:
        pl.when(core == 0)(first.wait)
        pl.when(core == 1)(second.wait)


def lanes(pieces, low, count):
    return pl.BlockSpec(
        (pl.Element(pieces), pl.Element(PIECE), pl.Element(count)), lambda _: (0, 0, low)
    )


def wide(info, part, own, other, before=None, weigh=10**7):
    info = jnp.stack([info[0], info[1], info[2 + part], info[3], info[4], info[5 + part], info[6]])
    more = [] if before is None else [before]
    anywhere = pl.BlockSpec(memory_space=pl.ANY)
    return pl.pallas_call(
        functools.partial(wide_kernel, len(more)),
        name="gradients_wide",
        grid=(1,),
        in_specs=[SM] + [lanes(8, 0, HID)] * 2 + [anywhere] * len(more),
        out_specs=anywhere,
        out_shape=sds((2, 8, PIECE, 2432), F32),
        scratch_shapes=[pltpu.VMEM((2, 8, PIECE, HID), F32), pltpu.SemaphoreType.DMA((2, 8))],
        input_output_aliases={3: 0} if more else {},
        compiler_params=params(16),
        cost_estimate=cost(weigh, 14 * 10**6),
    )(info, own, other, *more)


def model_order(info, mask, own, got, cols):
    pieces = []
    for q in range(16):
        place = lax.bitwise_xor(jnp.int32(q), info[mask])
        at = lax.rem(place, 8)
        ours, theirs = own[at, :, cols].astype(F32), got[at, :, cols].astype(F32)
        pieces.append(jnp.where(place < 8, ours, theirs))
    return jnp.concatenate(pieces, axis=0)


def tall_kernel(info, *refs):
    down, stage, sems = refs[-3:]
    copies = []
    for step in range(19):
        tile = step if step < 10 else step - 9
        part = int(tile >= SPLIT // 128)
        own, got, other, other_got = refs[4 * part : 4 * part + 4]
        low = 128 * tile - SPLIT * part
        cols = slice(low, low + 128)

        def ours(step=step, part=part, own=own, got=got, cols=cols):
            stage[step] = model_order(info, 2 + part, own, got, cols).T

        def theirs(step=step, part=part, own=other, got=other_got, cols=cols):
            stage[step] = model_order(info, 5 + part, own, got, cols).T

        pl.when((info[4] == 0) == (step < 10))(ours)
        pl.when((info[4] == 0) != (step < 10))(theirs)
        rows = pl.ds(128 * step, 128)
        copies.append(pltpu.make_async_copy(stage.at[step], down.at[rows, :], sems.at[step]))
        copies[-1].start()
    for copy in copies:
        copy.wait()


def tall(info, first, second):
    return pl.pallas_call(
        tall_kernel,
        name="gradients_tall",
        grid=(1,),
        in_specs=[SM] + [lanes(8, at, SPLIT) for at in (HID, 0) * 2]
        + [lanes(8, at, HID - SPLIT) for at in (HID, 0) * 2],
        out_specs=pl.BlockSpec(memory_space=pl.ANY),
        out_shape=sds((2432, D), F32),
        scratch_shapes=[pltpu.VMEM((19, 128, D), F32), pltpu.SemaphoreType.DMA((19,))],
        compiler_params=params(24),
        cost_estimate=cost(10**7, 14 * 10**6),
    )(info, *first, *second)


def small_kernel(info, own, got, other, other_got, query, key, value, out, extras):
    for first in (True, False):
        here = (info[4] == 0) == first

        def write(mask, one, two, first=first):
            for tile in range(4):
                turned = model_order(info, mask, one, two, slice(128 * tile, 128 * tile + 128)).T
                big, little = (query, key) if first else (out, value)
                if tile < 3:
                    big[128 * tile : 128 * tile + 128, :] = turned
                else:
                    big[384:, :] = turned[:64, :]
                    little[...] = turned[64:, :]
            more = model_order(info, mask, one, two, slice(512, 640))
            for piece in range(3):
                extras[0 if first else 1, piece] = more[PIECE * piece : PIECE * piece + 8, :]

        @pl.when(here)
        def _(write=write):
            write(2, own, got)

        @pl.when(jnp.logical_not(here))
        def _(write=write):
            write(5, other, other_got)


def small(info, *arrays):
    kept = [(448, D), (64, D), (64, D), (448, D), (2, 3, 8, 128)]
    return pl.pallas_call(
        small_kernel,
        name="gradients_small",
        grid=(1,),
        in_specs=[SM] + [lanes(8, at + SPLIT, 640) for at in (HID, 0) * 2],
        out_specs=[VM] * len(kept),
        out_shape=[sds(shape, F32) for shape in kept],
        compiler_params=params(20),
        cost_estimate=cost(10**7, 6 * 10**6),
    )(info, *arrays)


def send(field, axis, shift=1):
    size = lax.axis_size(axis)
    return lax.ppermute(field, axis, [(i, (i + shift) % size) for i in range(size)])


def after(field, *others):
    return lax.optimization_barrier((field, *others))[0]


def after_all(fields, *others):
    return lax.optimization_barrier((*fields, *others))[: len(fields)]


def in_order(place, own, rec):
    first = place == 0
    return jnp.where(first, own, rec), jnp.where(first, rec, own)


def swapped(weight, axis=-1):
    first, second = jnp.split(weight, 2, axis=axis)
    return jnp.concatenate([-second, first], axis=axis)


def angles():
    freq_index = np.arange(HD // 2, dtype=np.float32)
    inverse = np.float32(ROPE_BASE) ** (np.float32(-2.0) * freq_index / np.float32(HD))
    angle = np.arange(512, dtype=np.float32)[:, None] * inverse.astype(np.float32)[None, :]
    return jnp.asarray(np.concatenate([np.cos(angle), np.sin(angle)] * 2, axis=1))


ORDERS = (
    (("x", "a"), ("x", "b"), ("y", "a"), ("y", "b")),
    (("x", "b"), ("x", "a"), ("y", "b"), ("y", "a")),
), (
    (("y", "a"), ("y", "b"), ("x", "a"), ("x", "b")),
    (("y", "b"), ("y", "a"), ("x", "b"), ("x", "a")),
)
CHIPS = ("x", "zl", "y", "c")


def bit(place, kind):
    return (place ^ (place >> 1)) & 1 if kind == "a" else place >> 1


def mask_of(part, core, places):
    mask = 0
    for axis, kind in ORDERS[part][core]:
        mask = 2 * mask + bit(places[axis], kind)
    return mask


def swap(field, part, *steps):
    pairs = []
    for x in range(4):
        for zl in range(2):
            for y in range(4):
                for c in range(2):
                    to = {"x": x, "y": y}
                    for axis, kind in (ORDERS[part][c][step] for step in steps):
                        to[axis] = to[axis] ^ 1 if kind == "a" else 3 - to[axis]
                    here = ((x * 2 + zl) * 4 + y) * 2 + c
                    pairs.append((here, ((to["x"] * 2 + zl) * 4 + to["y"]) * 2 + c))
    return lax.ppermute(field, CHIPS, pairs)


def swap_two(one, two, step):
    return swap(one, 0, step), swap(two, 1, step)


def spread(one, two, one_r, two_r):
    one, two = jnp.concatenate([one, one_r]), jnp.concatenate([two, two_r])
    return lax.optimization_barrier((one, two))


def add(one, two):
    return (one.astype(F32) + two.astype(F32)).astype(BF)


def shards(tokens, long_count, attn_gain, w_query, b_query, w_key, b_key, w_value, b_value,
           w_out, mlp_gain, w_gate, w_up, w_down, cotangent):
    at_x, at_y, at_c, at_t = (lax.axis_index(a) for a in ("x", "y", "c", "t"))
    places = {"x": at_x, "y": at_y}
    masks_0 = [mask_of(part, 0, places) for part in (0, 1)]
    masks_1 = [mask_of(part, 1, places) for part in (0, 1)]
    mine = [jnp.where(at_c == 0, a, b) for a, b in zip(masks_0, masks_1, strict=True)]
    theirs = [jnp.where(at_c == 0, b, a) for a, b in zip(masks_0, masks_1, strict=True)]
    info = jnp.stack([at_t, long_count[0], *mine, at_c, *theirs]).astype(jnp.int32)
    gain_one = attn_gain.astype(F32)[None, :]
    gain_two = mlp_gain.astype(F32)[None, :]

    tok_0, tok_1 = tokens, send(tokens, "t")
    half_out = lax.dynamic_slice(w_out, (at_c * SLAB, 0), (SLAB, D))
    half_out = send(half_out, "t")
    cot_1 = send(cotangent[: HALF // 2], "t")

    wq, wk, wv = w_query.T, w_key.T, w_value.T
    heads = wq.reshape(HEADS, HD, D)
    heads = jnp.concatenate([heads, swapped(heads, 1)], axis=1).reshape(HEADS * 128, D)
    w_all = jnp.concatenate([heads, wk, swapped(wk, 0), wv, wv], axis=0)
    bias = b_query.reshape(HEADS, HD)
    bias = jnp.concatenate([bias, swapped(bias)], axis=-1).reshape(HEADS * 128)
    b_all = jnp.concatenate([bias, b_key, swapped(b_key), b_value, b_value]).astype(F32)[None, :]
    table = angles()
    attn_in, rotated, value, stats, att_0, att_1, att_keep = attention(
        info, tok_0, tok_1, gain_one, w_all, b_all, table
    )
    rec_0 = send(att_1, "t")

    half_out, wq, w_out, _ = lax.optimization_barrier((half_out, wq, w_out, att_0))
    half_rec = send(half_out, "c")
    rec_1 = send(after(att_0, half_rec), "t")
    cot_0, cot_0_rec = cotangent, send(cotangent, "c")
    g_0x, g_0y = turn(info, after(cot_0, half_rec), cot_0_rec)
    cot_1 = jnp.concatenate([cot_1, send(after(cotangent, g_0x)[HALF // 2 :], "t")])
    cot_1_rec = send(cot_1, "c")
    half_out = in_order(at_c, half_out, half_rec)
    no_rows = jnp.zeros((HD, D), BF)
    other_out = jnp.concatenate([*half_out, no_rows])
    this_out = jnp.concatenate([w_out, no_rows])
    w_cat = jnp.concatenate([wq, wk, jnp.zeros((HD, D), BF), wv], axis=0)
    wo_dup = w_out.reshape(HEADS, HD, D)
    wo_dup = jnp.concatenate([wo_dup, wo_dup], axis=1).reshape(HEADS * 128, D)
    rec_0, w_cat, wo_dup, g_0x, g_0y = lax.optimization_barrier((rec_0, w_cat, wo_dup, g_0x, g_0y))

    hid_0, m_0 = project(att_0, rec_0, this_out, other_out, tok_0, gain_two)
    m_0_rec = send(m_0, "c")
    attn_t = flip(after(attn_in, m_0))
    act_0, gate_0, up_0, out_0, out_0_oth, dm_0, dm_0_oth = feed(
        info, m_0, after(m_0_rec, attn_t), cot_0, cot_0_rec, w_gate, w_up, w_down
    )
    hid_1, m_1 = project(att_1, after(rec_1, act_0), this_out, other_out, tok_1, gain_two)
    m_1_rec = send(m_1, "c")
    m_0x, m_0y = turn(info, after(m_0, m_1), m_0_rec)
    dm_0 = add(dm_0, after(send(dm_0_oth, "c"), m_0x))
    dm_0_rec = send(dm_0, "t")
    act_1, gate_1, up_1, out_1, out_1_oth, dm_1, dm_1_oth = feed(
        info, after(m_1, dm_0), m_1_rec, cot_1, cot_1_rec, w_gate, w_up, w_down
    )
    m_1x, m_1y = turn(info, after(m_1, dm_1, dm_0_rec), m_1_rec)
    g_1x, g_1y = turn(info, after(cot_1, m_1x), cot_1_rec)
    dm_1 = add(dm_1, after(send(dm_1_oth, "c"), g_1x))
    dm_1_rec = send(dm_1, "t")

    gate_k, gate_g = weight_grad(m_0x, m_1x, gate_0, after(gate_1, dm_1, dm_0_rec), 0, 5)
    gate_r = swap(gate_g, 0, 0)
    up_k, up_g = weight_grad(m_0y, m_1y, up_0, after(up_1, gate_g), 0, 5)
    up_r = swap(up_g, 1, 0)
    low_k, low_g = weight_grad(g_0x, g_1x, act_0, after(act_1, up_g), 0, 2)
    low_r = swap(low_g, 0, 0)
    out_rec = [send(after(field, dm_1), "c") for field in (out_0_oth, out_1_oth)]
    mine, theirs = halves(out_0, out_1, *after_all(out_rec, low_g))
    theirs_rec = send(theirs, "t")

    grad_mid, branch, grad_att, sum_two = branch_back(
        info, dm_0, dm_1, after(dm_1_rec, mine), dm_0_rec, cot_0, cot_1, hid_0, hid_1,
        gain_two, wo_dup,
    )
    lin_a = back((0, 1), info, grad_att, rotated, value, stats, table)
    lin_b = back((2,), info, after(grad_att, lin_a), rotated, value, stats, table)
    theirs_rec = after(theirs_rec, lin_b)
    output = (hid_0 + mine.astype(F32) + theirs_rec.astype(F32)).astype(BF)
    da_own, da_send, pack_k, pack_g = last(
        info, branch, lin_a, after(lin_b, output), sum_two, att_keep, attn_t, w_cat, tok_0, tok_1
    )
    pack_r = send(pack_g, "c")

    (gate_k, gate_g), (up_k, up_g) = fold(
        info, 2, [((gate_k, after(gate_r, pack_g)), None, 0)], [((up_k, up_r), None, 0)]
    )
    gate_r, up_r = swap_two(gate_g, up_g, 1)
    ((pack_k, pack_g),) = fold(info, 2, [((pack_k, after(pack_r, gate_g)), 2, 15)])
    pack_r = swap(pack_g, 0, 0)
    high_k, high_g = weight_grad(g_0y, g_1y, act_0, after(act_1, pack_g), 2, 3)
    high_r = swap(high_g, 1, 0)
    ((pack_k, pack_g),) = fold(
        info, 2, [((pack_k, after(pack_r, high_g, gate_r, up_r)), None, 0)], weigh=3 * 10**13
    )
    pack_r = swap(pack_g, 0, 1)
    (low_k, low_g), (high_k, high_g) = fold(
        info, 2, [((low_k, after(low_r, pack_g)), None, 0)], [((high_k, high_r), None, 0)]
    )
    low_r, high_r = swap_two(low_g, high_g, 1)
    da_rec = send(after(da_send, low_g), "t")
    (one_k, one_g), (two_k, two_g) = fold(
        info,
        2,
        [
            ((gate_k, after(gate_r, low_g)), 2, 3),
            ((low_k, low_r), 2, 3),
            ((pack_k, pack_r), None, 0),
        ],
        [((up_k, up_r), 3, 3), ((high_k, high_r), 3, 3)],
    )
    one_r, two_r = swap_two(one_g, two_g, 2)

    (one_k, one_g), (two_k, two_g) = fold(
        info, 2, [((one_k, one_r), None, 0)], [((two_k, two_r), None, 0)]
    )
    one_r, two_r = swap_two(one_g, two_g, 3)
    ((part,),) = fold(info, 1, [((one_k, one_r), None, 0), ((two_k, two_r), None, 0)])
    part_r = send(part, "zl")

    field = tokens.astype(F32)
    factor = factor_of(field)
    normed = field * factor
    scaled = (da_own + after(da_rec, part).astype(F32)) * gain_one
    grad_tokens = grad_mid + factor * (
        scaled - normed * jnp.mean(scaled * normed, axis=-1, keepdims=True)
    )
    grad_tokens = grad_tokens.astype(BF)
    part = add(part, after(part_r, grad_tokens))

    wide_one = HID + SPLIT + 640
    one, two = part[..., :wide_one], part[..., wide_one:]
    for step in (3, 2, 1):
        one, two = spread(one, two, *swap_two(one, two, step))
    low_r, high_r = swap_two(one[..., HID:], two[..., HID:], 0)
    gate_r, up_r = swap_two(one[..., :HID], two[..., :HID], 0)
    one_c = send(one, "c")
    two_c = send(after(two, one_c), "c")
    grad_w_gate = wide(info, 0, one, one_c, weigh=3 * 10**13)
    grad_w_up = wide(info, 1, two, after(two_c, grad_w_gate))
    low_r, high_r = after_all((low_r, high_r), grad_w_up)
    low_c, high_c = send(low_r, "c"), send(high_r, "c")
    grad_wq, grad_wk, grad_wv, grad_wo, extras = small(info, one, low_r, one_c, low_c)
    grad_w_down = tall(info, (one, low_r, one_c, low_c), (two, high_r, two_c, high_c))
    gate_r, up_r = after_all((gate_r, up_r), grad_wo, grad_w_down)
    gate_c = send(gate_r, "c")
    up_c = send(up_r, "c")
    grad_w_gate = wide(info, 0, gate_r, gate_c, grad_w_gate)
    grad_w_up = wide(info, 1, up_r, after(up_c, grad_w_gate), grad_w_up)
    grad_w_gate, grad_w_up = grad_w_gate.reshape(D, 2432), grad_w_up.reshape(D, 2432)
    gains = extras[:, 1:].reshape(2, 2, 1024)
    gains = jnp.concatenate([gains[0, :, :512], gains[1, :, :384]], axis=1)
    gains = gains + after(send(gains, "t"), grad_w_up)
    biases = extras[0, 0, :4].reshape(512)

    return (
        output,
        grad_tokens,
        gains[0],
        grad_wq.T,
        biases[:448],
        grad_wk.T,
        biases[448:],
        grad_wv.T,
        extras[1, 0, 0, 64:],
        grad_wo,
        gains[1],
        grad_w_gate,
        grad_w_up,
        grad_w_down,
    )


def solution(mesh):
    fine = Mesh(mesh.devices.reshape(4, 2, 4, 2, 2), ("x", "zl", "y", "c", "t"))
    dp = ("x", "zl", "y", "c")
    rows, cols, split = P((*dp, "t"), None), P(None, "t"), P("t")
    down = P("t", None)
    return jax.shard_map(
        shards,
        mesh=fine,
        in_specs=(
            rows, P(dp), P(), cols, split, cols, split, cols, split, down, P(), cols, cols, down,
            rows,
        ),
        out_specs=(
            rows, rows, P(), cols, split, cols, split, cols, split, down, P(), cols, cols, down,
        ),
        check_vma=False,
    )
```

```python
import functools

import jax
import jax.numpy as jnp
import numpy as np
from jax import lax
from jax.experimental import pallas as pl
from jax.experimental.pallas import tpu as pltpu
from jax.sharding import Mesh
from jax.sharding import PartitionSpec as P

HD = 64
EPSILON = 1e-06
ROPE_BASE = 1000000.0
BF = jnp.bfloat16
F32 = jnp.float32

D = 896
HALF = 384
ROWS = 768
HEADS = 7
PIECE = 56
SLAB = 224
HID = 1280
SPLIT = 512
STEP = 1152
CHUNK = 256
MIB = 1024 * 1024

VM = pl.BlockSpec(memory_space=pltpu.VMEM)
SM = pl.BlockSpec(memory_space=pltpu.SMEM)


def sds(shape, dtype):
    return jax.ShapeDtypeStruct(shape, dtype)


def nn(a, b):
    return lax.dot_general(a, b, (((1,), (0,)), ((), ())), preferred_element_type=F32)


def nt(a, b):
    return lax.dot_general(a, b, (((1,), (1,)), ((), ())), preferred_element_type=F32)


def tn(a, b):
    return lax.dot_general(a, b, (((0,), (0,)), ((), ())), preferred_element_type=F32)


def half_rows(info):
    return [
        pl.ds(pl.multiple_of(place * HALF, HALF), HALF) for place in (info[0], 1 - info[0])
    ]


def factor_of(field):
    return lax.rsqrt(jnp.mean(field * field, axis=-1, keepdims=True) + EPSILON)


def params(mib):
    return pltpu.CompilerParams(vmem_limit_bytes=mib * MIB)


def cost(flops, size, trans=0):
    return pl.CostEstimate(flops=flops // 1000, bytes_accessed=size // 1000, transcendentals=trans // 1000)


def masks(is_long, keys_first=False):
    row = lax.broadcasted_iota(jnp.int32, (256, 256), 0)
    col = lax.broadcasted_iota(jnp.int32, (256, 256), 1)
    causal = jnp.where(row <= col if keys_first else col <= row, 0.0, -1e30).astype(F32)
    before = jnp.full((256, 256), jnp.where(is_long == 1, 0.0, -1e30).astype(F32))
    return causal, jnp.concatenate([before, causal], axis=0 if keys_first else 1)


def turns(ref, block, is_long):
    pair = ref[:256, :]
    if block == 1:
        pair = jnp.where(is_long == 1, ref[256:, :], pair)
    lane = lax.broadcasted_iota(jnp.int32, (256, 128), 1)
    swapped_pair = pltpu.roll(pair, 32, 1)
    cosine_here = lax.rem(lane, 64) < 32
    cosine = jnp.where(cosine_here, pair, swapped_pair)
    sine = jnp.where(cosine_here, swapped_pair, pair)
    return cosine, jnp.where(lane < 64, sine, -sine)


SPANS = ((0, 0, 256), (256, 0, 512), (512, 512, 768))


def attention_kernel(info, tok_0, tok_1, gain, w_all, b_all, table,
                     attn_in, rotated, value, stats, att_0, att_1, att_keep):
    for rows, src in zip(half_rows(info), (tok_0, tok_1), strict=True):
        field = src[...].astype(F32)
        attn_in[rows, :] = (field * factor_of(field) * gain[...]).astype(BF)
    for block in range(3):
        rows = slice(256 * block, 256 * block + 256)
        lin = nt(attn_in[rows, :], w_all[...]) + b_all[...]
        cos_b, sin_b = turns(table, block, info[1])
        for head in range(HEADS + 1):
            part = lin[:, 128 * head : 128 * head + 128]
            turned = part * cos_b + pltpu.roll(part, 64, 1) * sin_b
            rotated[rows, 128 * head : 128 * head + 128] = turned.astype(BF)
        value[rows, :] = lin[:, 1024:1152].astype(BF)
    causal, wide = masks(info[1])
    lane = lax.broadcasted_iota(jnp.int32, (256, 128), 1)
    for block, (first, low, high) in enumerate(SPANS):
        rows = slice(first, first + 256)
        mask = wide if block == 1 else causal
        keys = rotated[low:high, 1024 - 128 :]
        vals = value[low:high, :]
        kept = jnp.zeros((256, 128), F32)
        outs = []
        for head in range(HEADS):
            scores = nt(rotated[rows, 128 * head : 128 * head + 128], keys) * 0.0625 + mask
            top = jnp.max(scores, axis=-1, keepdims=True)
            expo = jnp.exp(scores - top)
            total = jnp.sum(expo, axis=-1, keepdims=True)
            kept = jnp.where(lane == head, top + jnp.log(total), kept)
            outs.append(nn(expo.astype(BF), vals) * (1.0 / total))
        stats[:, rows] = kept.T[:8, :]
        outs.append(jnp.zeros((256, 128), F32))
        for pair in range(4):
            both = jnp.where(lane < 64, outs[2 * pair], outs[2 * pair + 1])
            att_keep[rows, 128 * pair : 128 * pair + 128] = both.astype(BF)
    lane = lax.broadcasted_iota(jnp.int32, (64, 128), 1)
    for rows, out in zip(half_rows(info), (att_0, att_1), strict=True):
        out[:HALF, :] = att_keep[rows, :384]
        for pair in range(3):
            low = pl.multiple_of(rows.start + 128 * pair, 128)
            part = att_keep[pl.ds(low, 128), 384:].astype(F32)
            left, right = part[:64, :], pltpu.roll(part[64:, :], 64, 1)
            out[HALF:, 128 * pair : 128 * pair + 128] = jnp.where(lane < 64, left, right).astype(BF)


def attention(info, *args):
    return pl.pallas_call(
        attention_kernel,
        name="attention_forward",
        in_specs=[SM] + [VM] * 6,
        out_specs=[VM] * 7,
        out_shape=[
            sds((ROWS, D), BF),
            pltpu.HBM((ROWS, 1024), BF),
            pltpu.HBM((ROWS, 128), BF),
            pltpu.HBM((8, ROWS), F32),
            sds((448, 384), BF),
            sds((448, 384), BF),
            pltpu.HBM((ROWS, 512), BF),
        ],
        compiler_params=params(26),
        cost_estimate=cost(4 * 10**9, 12 * 10**6, 3 * 10**6),
    )(info, *args)


def project_kernel(att_own, att_rec, wo_own, wo_rec, tok, gain, hidden, mlp_in, full):
    lane = lax.broadcasted_iota(jnp.int32, (64, 128), 1)
    field = tok[...].astype(F32)
    for att, weight in ((att_own, wo_own), (att_rec, wo_rec)):
        full[:, :384] = att[:HALF, :]
        for pair in range(3):
            both = att[HALF:, 128 * pair : 128 * pair + 128].astype(F32)
            low = 128 * pair
            full[low : low + 64, 384:] = jnp.where(lane < 64, both, 0.0).astype(BF)
            both = jnp.where(lane < 64, pltpu.roll(both, 64, 1), 0.0)
            full[low + 64 : low + 128, 384:] = both.astype(BF)
        field = field + nn(full[...], weight[...])
    hidden[...] = field
    mlp_in[...] = (field * factor_of(field) * gain[...]).astype(BF)


def project(att_own, att_rec, wo_own, wo_rec, tok, gain):
    return pl.pallas_call(
        project_kernel,
        name="project_norm",
        in_specs=[VM] * 6,
        out_specs=[VM] * 2,
        out_shape=[pltpu.HBM((HALF, D), F32), sds((HALF, D), BF)],
        scratch_shapes=[pltpu.VMEM((HALF, 512), BF)],
        compiler_params=params(14),
        cost_estimate=cost(7 * 10**8, 6 * 10**6),
    )(att_own, att_rec, wo_own, wo_rec, tok, gain)


def turn_kernel(info, own, rec, first, second):
    for at, src in enumerate((own, rec)):
        cols = slice(HALF * at, HALF * at + HALF)
        for slab in range(4):
            turned = src[:, SLAB * slab : SLAB * slab + SLAB].astype(F32).T.astype(BF)
            for mask, out in ((info[2], first), (info[3], second)):
                slot = lax.bitwise_xor(jnp.int32(slab), mask // 4)
                out[pl.ds(pl.multiple_of(slot * SLAB, SLAB), SLAB), cols] = turned


def turn(info, own, rec, weigh=10**6):
    return pl.pallas_call(
        turn_kernel,
        name="transpose_rows",
        in_specs=[SM] + [VM] * 2,
        out_specs=[VM] * 2,
        out_shape=[pltpu.HBM((D, 2 * HALF), BF)] * 2,
        compiler_params=params(14),
        cost_estimate=cost(weigh, 4 * 10**6),
    )(info, own, rec)


def flip_kernel(source, out):
    for block in range(3):
        rows = slice(256 * block, 256 * block + 256)
        out[:, rows] = source[rows, :].astype(F32).T.astype(BF)


def flip(source):
    return pl.pallas_call(
        flip_kernel,
        name="transpose_whole",
        in_specs=[VM],
        out_specs=VM,
        out_shape=pltpu.HBM((D, ROWS), BF),
        compiler_params=params(8),
        cost_estimate=cost(3 * 10**13, 3 * 10**6),
    )(source)


def feed_kernel(info, m_own, m_rec, g_own, g_rec, wg, wu, wd_in, act, gate_g, up_g, *rest):
    ends, sums, wd = rest[:4], rest[4:8], rest[8]
    step = pl.program_id(0)
    wd[...] = wd_in[...]

    @pl.when((step == 0) & (info[4] == 1))
    def _():
        wd[:128, :] = jnp.zeros((128, D), BF)

    @pl.when(step == 0)
    def _():
        for total in sums:
            total[...] = jnp.zeros_like(total)

    for at, (m, g) in enumerate(((m_own, g_own), (m_rec, g_rec))):
        rows = slice(HALF * at, HALF * at + HALF)
        gate = nn(m[...], wg[...])
        up = nn(m[...], wu[...])
        grad = nt(g[...], wd[...])
        sig = 1.0 / (1.0 + jnp.exp(-gate))
        swish = gate * sig
        act[rows, :] = (swish * up).astype(BF)
        up_g[rows, :] = (grad * swish).astype(BF)
        gate_g[rows, :] = (grad * up * (sig + swish * (1.0 - sig))).astype(BF)
        sums[at][...] += nn(act[rows, :], wd[...])
        sums[2 + at][...] += nt(gate_g[rows, :], wg[...]) + nt(up_g[rows, :], wu[...])

    @pl.when(step == pl.num_programs(0) - 1)
    def _():
        for end, total in zip(ends, sums, strict=True):
            end[...] = total[...].astype(BF)


def whole(shape):
    zeros = (0,) * len(shape)
    return pl.BlockSpec(shape, lambda *_: zeros, pipeline_mode=pl.Buffered(1))


def feed(info, m_own, m_rec, g_own, g_rec, wg, wu, wd):
    rows = whole((HALF, D))

    def start(j, info):
        return pl.multiple_of(info[4] * STEP + j * CHUNK, 128)

    wide = pl.BlockSpec((pl.Element(D), pl.Element(CHUNK)), lambda j, info: (0, start(j, info)))
    tall = pl.BlockSpec((pl.Element(CHUNK), pl.Element(D)), lambda j, info: (start(j, info), 0))
    kept = pl.BlockSpec((2 * HALF, CHUNK), lambda j, info: (0, j))
    return pl.pallas_call(
        feed_kernel,
        name="feed_forward_and_back",
        grid_spec=pltpu.PrefetchScalarGridSpec(
            num_scalar_prefetch=1,
            grid=(HID // CHUNK,),
            in_specs=[rows] * 4 + [wide, wide, tall],
            out_specs=[kept] * 3 + [rows] * 4,
            scratch_shapes=[pltpu.VMEM((HALF, D), F32)] * 4 + [pltpu.VMEM((CHUNK, D), BF)],
        ),
        out_shape=[pltpu.HBM((2 * HALF, HID), BF)] * 3 + [sds((HALF, D), BF)] * 4,
        compiler_params=params(30),
        cost_estimate=cost(10**10, 20 * 10**6, 10**6),
    )(info, m_own, m_rec, g_own, g_rec, wg, wu, wd)


def halves_kernel(own_0, own_1, rec_0, rec_1, mine, theirs):
    for own, rec, out in ((own_0, rec_0, mine), (own_1, rec_1, theirs)):
        out[...] = (own[...].astype(F32) + rec[...].astype(F32)).astype(BF)


def halves(*args):
    return pl.pallas_call(
        halves_kernel,
        name="sum_cores_rows",
        in_specs=[VM] * 4,
        out_specs=[VM] * 2,
        out_shape=[sds((HALF, D), BF)] * 2,
        compiler_params=params(10),
        cost_estimate=cost(3 * 10**13, 4 * 10**6),
    )(*args)


def weight_kernel(left_0, left_1, right_0, right_1, *outs):
    product = nn(left_0[...], right_0[...]) + nn(left_1[...], right_1[...])
    count = 16 // len(outs)
    for piece in range(16):
        low = PIECE * piece
        outs[piece // count][piece % count] = product[low : low + PIECE, :].astype(BF)


def weight_grad(left_0, left_1, right_0, right_1, first, count, parts=2, weigh=1):
    left = whole((D, 2 * HALF))
    right = pl.BlockSpec((2 * HALF, CHUNK), lambda j: (0, j + first))
    out = pl.BlockSpec((16 // parts, PIECE, CHUNK), lambda j: (0, 0, j))
    return pl.pallas_call(
        weight_kernel,
        name="weight_gradient",
        grid=(count,),
        in_specs=[left] * 2 + [right] * 2,
        out_specs=[out] * parts,
        out_shape=[pltpu.HBM((16 // parts, PIECE, CHUNK * count), BF)] * parts,
        compiler_params=params(16),
        cost_estimate=cost(7 * 10**8 * count * weigh, 8 * 10**6),
    )(left_0, left_1, right_0, right_1)


def fold_kernel(plan, ways, info, *refs):
    ins = list(refs[: sum(count for group in plan for count, _, _ in group)])
    outs = list(refs[len(ins) :])
    for group in plan:
        out = [outs.pop(0) for _ in range(ways)]
        low = 0
        for count, mask, bits in group:
            terms = [ins.pop(0) for _ in range(count)]
            pieces, _, wide = terms[0].shape
            each = pieces // ways
            for at in range(pieces):
                piece = at
                if mask is not None:
                    piece = lax.bitwise_xor(jnp.int32(at), lax.bitwise_and(info[mask], bits))
                total = terms[0][piece].astype(F32)
                for term in terms[1:]:
                    total = total + term[piece].astype(F32)
                out[at // each][at % each, :, low : low + wide] = total.astype(BF)
            low += wide


def fold(info, ways, *groups, weigh=10**7):
    plan = [[(len(terms), mask, bits) for terms, mask, bits in group] for group in groups]
    ins = [ref for group in groups for terms, _, _ in group for ref in terms]
    shapes = []
    for group in groups:
        wide = sum(terms[0].shape[-1] for terms, _, _ in group)
        shapes += [sds((group[0][0][0].shape[0] // ways, PIECE, wide), BF)] * ways
    out = pl.pallas_call(
        functools.partial(fold_kernel, plan, ways),
        name="sum_parts",
        in_specs=[SM] + [VM] * len(ins),
        out_specs=[VM] * len(shapes),
        out_shape=shapes,
        compiler_params=params(20),
        cost_estimate=cost(weigh, 6 * 10**6),
    )(info, *ins)
    return [out[ways * at : ways * at + ways] for at in range(len(groups))]


def branch_kernel(info, dm_own_0, dm_own_1, dm_rec_0, dm_rec_1, cot_0, cot_1, hid_0, hid_1,
                  gain_two, wo_dup, grad_mid, branch, grad_att, sums):
    sets = (dm_own_0, dm_rec_0, cot_0, hid_0), (dm_own_1, dm_rec_1, cot_1, hid_1)
    for half, (rows, (own, rec, cot, hid)) in enumerate(zip(half_rows(info), sets, strict=True)):
        field = hid[...]
        factor = factor_of(field)
        normed = field * factor
        grad = own[...].astype(F32) + rec[...].astype(F32)
        scaled = grad * gain_two[...]
        middle = cot[...].astype(F32) + factor * (
            scaled - normed * jnp.mean(scaled * normed, axis=-1, keepdims=True)
        )
        branch[rows, :] = middle.astype(BF)
        if half == 0:
            sums[...] = jnp.sum(grad * normed, axis=0, keepdims=True)
            grad_mid[...] = middle
    grad_att[...] = nt(branch[...], wo_dup[...]).astype(BF)


def branch_back(info, *args):
    return pl.pallas_call(
        branch_kernel,
        name="norm_and_projection_backward",
        in_specs=[SM] + [VM] * 10,
        out_specs=[VM] * 4,
        out_shape=[sds((HALF, D), F32), sds((ROWS, D), BF), sds((ROWS, D), BF), sds((1, D), F32)],
        compiler_params=params(26),
        cost_estimate=cost(10**9, 10**7),
    )(info, *args)


def back_kernel(blocks, info, grad_att, rotated, value, stats, table, lin):
    causal, wide = masks(info[1], keys_first=True)
    lane = lax.broadcasted_iota(jnp.int32, (256, 128), 1)
    base = 256 * blocks[0]
    grad_k = [jnp.zeros((256, 128), F32) for _ in blocks]
    grad_v = [jnp.zeros((256, 128), F32) for _ in blocks]
    for block in blocks:
        first, low, high = SPANS[block]
        rows = slice(first, first + 256)
        to = slice(first - base, first - base + 256)
        mask = wide if block == 1 else causal
        keys = rotated[low:high, 896:1024]
        vals = value[low:high, :]
        cos_b, sin_b = turns(table, block, info[1])
        turned = []
        for head in range(HEADS):
            cols = slice(128 * head, 128 * head + 128)
            query, grad_o = rotated[rows, cols], grad_att[rows, cols]
            chance = jnp.exp(nt(keys, query) * 0.0625 + mask - stats[head : head + 1, rows])
            grad_p = nt(vals, grad_o) * 0.5
            inner = jnp.sum(chance * grad_p, axis=0, keepdims=True)
            grad_s = (chance * (grad_p - inner)).astype(BF)
            low_p = chance.astype(BF)
            back = tn(grad_s, keys) * 0.125
            turned.append(back * cos_b - pltpu.roll(back, 64, 1) * sin_b)
            for at in range((high - low) // 256):
                part = slice(256 * at, 256 * at + 256)
                grad_k[(low - base) // 256 + at] += nn(grad_s[part, :], query)
                grad_v[(low - base) // 256 + at] += nn(low_p[part, :], grad_o)
        turned.append(jnp.zeros((256, 128), F32))
        for pair in range(4):
            right = pltpu.roll(turned[2 * pair + 1], 64, 1)
            lin[to, 128 * pair : 128 * pair + 128] = jnp.where(
                lane < 64, turned[2 * pair], right
            ).astype(BF)
    for at, block in enumerate(blocks):
        rows = slice(256 * at, 256 * at + 256)
        cos_b, sin_b = turns(table, block, info[1])
        back = grad_k[at] * 0.125
        back = back * cos_b - pltpu.roll(back, 64, 1) * sin_b
        back = pltpu.roll(back, 64, 1).astype(BF)
        lin[rows, 384:512] = jnp.where(lane < 64, lin[rows, 384:512], back)
        lin[rows, 512:640] = jnp.where(lane < 64, 0.0, grad_v[at]).astype(BF)


def back(blocks, info, *args):
    return pl.pallas_call(
        functools.partial(back_kernel, blocks),
        name="attention_backward",
        in_specs=[SM] + [VM] * 5,
        out_specs=VM,
        out_shape=sds((256 * len(blocks), 640), BF),
        compiler_params=params(20),
        cost_estimate=cost(10**9, 10**7, 10**6),
    )(info, *args)


def last_kernel(info, branch, lin_a, lin_b, sum_two, att, attn_t, w_cat, tok_0, tok_1,
                da_own, da_send, pack_keep, pack_send, grad_in):
    grad_in[:512, :] = nn(lin_a[...], w_cat[...])
    grad_in[512:, :] = nn(lin_b[...], w_cat[...])
    sum_one = jnp.zeros((1, D), F32)
    for rows, src, out in zip(half_rows(info), (tok_0, tok_1), (da_own, da_send), strict=True):
        field = src[...].astype(F32)
        grad = grad_in[rows, :]
        out[...] = grad.astype(out.dtype)
        sum_one = sum_one + jnp.sum(grad * (field * factor_of(field)), axis=0, keepdims=True)
    sum_b = jnp.sum(lin_a[...].astype(F32), axis=0, keepdims=True)
    sum_b = sum_b + jnp.sum(lin_b[...].astype(F32), axis=0, keepdims=True)
    grad_w = nn(attn_t[:, :512], lin_a[...]) + nn(attn_t[:, 512:], lin_b[...])
    grad_o = tn(branch[...], att[...])
    first_w = grad_w[:, :512]
    second_w = jnp.concatenate([grad_o[:, :384], grad_o[:, 384:] + grad_w[:, 512:]], axis=1)
    sum_two = sum_two[...]
    extra_a = {0: sum_b[:, :512], 1: sum_one[:, :512], 2: sum_two[:, :512]}
    extra_b = {0: sum_b[:, 512:], 1: sum_one[:, 512:], 2: sum_two[:, 512:]}

    def lines(extra):
        count = extra.shape[1] // 128
        parts = [extra[:, 128 * at : 128 * at + 128] for at in range(count)]
        return jnp.concatenate([*parts, jnp.zeros((PIECE - count, 128), F32)], axis=0)

    for piece in range(16):
        rows = slice(PIECE * piece, PIECE * piece + PIECE)
        packs = []
        for grads, extra in ((first_w, extra_a), (second_w, extra_b)):
            more = lines(extra[piece]) if piece in extra else jnp.zeros((PIECE, 128), F32)
            packs.append((grads[rows, :], more))
        for at, cols in ((0, slice(0, 512)), (1, slice(512, 640))):
            low, high = packs[0][at], packs[1][at]
            pack_keep[piece, :, cols] = jnp.where(info[4] == 0, low, high).astype(BF)
            pack_send[piece, :, cols] = jnp.where(info[4] == 0, high, low).astype(BF)


def last(info, *args):
    return pl.pallas_call(
        last_kernel,
        name="attention_weight_gradients",
        in_specs=[SM] + [VM] * 9,
        out_specs=[VM] * 4,
        out_shape=[
            sds((HALF, D), F32),
            sds((HALF, D), BF),
            sds((16, PIECE, 640), BF),
            sds((16, PIECE, 640), BF),
        ],
        scratch_shapes=[pltpu.VMEM((ROWS, D), F32)],
        compiler_params=params(28),
        cost_estimate=cost(3 * 10**9, 16 * 10**6),
    )(info, *args)


def wide_kernel(got, info, own, other, *refs):
    out, stage, sems = refs[-3:]
    copies = []
    for at, (slot, src) in enumerate(((2, own), (5, other))):
        half = lax.bitwise_xor(info[slot] // 8, got)
        core = lax.rem(info[4] + at, 2)
        for piece in range(8):
            stage[at, piece] = src[piece].astype(F32)
            place = lax.bitwise_xor(jnp.int32(piece), lax.rem(info[slot], 8))
            sem = sems.at[at, piece]
            first = pltpu.make_async_copy(
                stage.at[at, piece], out.at[half, place, :, pl.ds(0, HID)], sem
            )
            second = pltpu.make_async_copy(
                stage.at[at, piece, :, pl.ds(128, HID - 128)],
                out.at[half, place, :, pl.ds(HID, HID - 128)],
                sem,
            )
            pl.when(core == 0)(first.start)
            pl.when(core == 1)(second.start)
            copies.append((core, first, second))
    for core, first, second in copies:
        pl.when(core == 0)(first.wait)
        pl.when(core == 1)(second.wait)


def lanes(pieces, low, count):
    return pl.BlockSpec(
        (pl.Element(pieces), pl.Element(PIECE), pl.Element(count)), lambda _: (0, 0, low)
    )


def wide(info, part, own, other, before=None, weigh=10**7):
    info = jnp.stack([info[0], info[1], info[2 + part], info[3], info[4], info[5 + part], info[6]])
    more = [] if before is None else [before]
    anywhere = pl.BlockSpec(memory_space=pl.ANY)
    return pl.pallas_call(
        functools.partial(wide_kernel, len(more)),
        name="gradients_wide",
        grid=(1,),
        in_specs=[SM] + [lanes(8, 0, HID)] * 2 + [anywhere] * len(more),
        out_specs=anywhere,
        out_shape=sds((2, 8, PIECE, 2432), F32),
        scratch_shapes=[pltpu.VMEM((2, 8, PIECE, HID), F32), pltpu.SemaphoreType.DMA((2, 8))],
        input_output_aliases={3: 0} if more else {},
        compiler_params=params(16),
        cost_estimate=cost(weigh, 14 * 10**6),
    )(info, own, other, *more)


def model_order(info, mask, own, got, cols):
    pieces = []
    for q in range(16):
        place = lax.bitwise_xor(jnp.int32(q), info[mask])
        at = lax.rem(place, 8)
        ours, theirs = own[at, :, cols].astype(F32), got[at, :, cols].astype(F32)
        pieces.append(jnp.where(place < 8, ours, theirs))
    return jnp.concatenate(pieces, axis=0)


def tall_kernel(info, *refs):
    down, stage, sems = refs[-3:]
    copies = []
    for step in range(19):
        tile = step if step < 10 else step - 9
        part = int(tile >= SPLIT // 128)
        own, got, other, other_got = refs[4 * part : 4 * part + 4]
        low = 128 * tile - SPLIT * part
        cols = slice(low, low + 128)

        def ours(step=step, part=part, own=own, got=got, cols=cols):
            stage[step] = model_order(info, 2 + part, own, got, cols).T

        def theirs(step=step, part=part, own=other, got=other_got, cols=cols):
            stage[step] = model_order(info, 5 + part, own, got, cols).T

        pl.when((info[4] == 0) == (step < 10))(ours)
        pl.when((info[4] == 0) != (step < 10))(theirs)
        rows = pl.ds(128 * step, 128)
        copies.append(pltpu.make_async_copy(stage.at[step], down.at[rows, :], sems.at[step]))
        copies[-1].start()
    for copy in copies:
        copy.wait()


def tall(info, first, second):
    return pl.pallas_call(
        tall_kernel,
        name="gradients_tall",
        grid=(1,),
        in_specs=[SM] + [lanes(8, at, SPLIT) for at in (HID, 0) * 2]
        + [lanes(8, at, HID - SPLIT) for at in (HID, 0) * 2],
        out_specs=pl.BlockSpec(memory_space=pl.ANY),
        out_shape=sds((2432, D), F32),
        scratch_shapes=[pltpu.VMEM((19, 128, D), F32), pltpu.SemaphoreType.DMA((19,))],
        compiler_params=params(24),
        cost_estimate=cost(10**7, 14 * 10**6),
    )(info, *first, *second)


def small_kernel(info, own, got, other, other_got, query, key, value, out, extras):
    for first in (True, False):
        here = (info[4] == 0) == first

        def write(mask, one, two, first=first):
            for tile in range(4):
                turned = model_order(info, mask, one, two, slice(128 * tile, 128 * tile + 128)).T
                big, little = (query, key) if first else (out, value)
                if tile < 3:
                    big[128 * tile : 128 * tile + 128, :] = turned
                else:
                    big[384:, :] = turned[:64, :]
                    little[...] = turned[64:, :]
            more = model_order(info, mask, one, two, slice(512, 640))
            for piece in range(3):
                extras[0 if first else 1, piece] = more[PIECE * piece : PIECE * piece + 8, :]

        @pl.when(here)
        def _(write=write):
            write(2, own, got)

        @pl.when(jnp.logical_not(here))
        def _(write=write):
            write(5, other, other_got)


def small(info, *arrays):
    kept = [(448, D), (64, D), (64, D), (448, D), (2, 3, 8, 128)]
    return pl.pallas_call(
        small_kernel,
        name="gradients_small",
        grid=(1,),
        in_specs=[SM] + [lanes(8, at + SPLIT, 640) for at in (HID, 0) * 2],
        out_specs=[VM] * len(kept),
        out_shape=[sds(shape, F32) for shape in kept],
        compiler_params=params(20),
        cost_estimate=cost(10**7, 6 * 10**6),
    )(info, *arrays)


def send(field, axis, shift=1):
    size = lax.axis_size(axis)
    return lax.ppermute(field, axis, [(i, (i + shift) % size) for i in range(size)])


def after(field, *others):
    return lax.optimization_barrier((field, *others))[0]


def after_all(fields, *others):
    return lax.optimization_barrier((*fields, *others))[: len(fields)]


def in_order(place, own, rec):
    first = place == 0
    return jnp.where(first, own, rec), jnp.where(first, rec, own)


def swapped(weight, axis=-1):
    first, second = jnp.split(weight, 2, axis=axis)
    return jnp.concatenate([-second, first], axis=axis)


def angles():
    freq_index = np.arange(HD // 2, dtype=np.float32)
    inverse = np.float32(ROPE_BASE) ** (np.float32(-2.0) * freq_index / np.float32(HD))
    angle = np.arange(512, dtype=np.float32)[:, None] * inverse.astype(np.float32)[None, :]
    return jnp.asarray(np.concatenate([np.cos(angle), np.sin(angle)] * 2, axis=1))


ORDERS = (
    (("x", "a"), ("x", "b"), ("y", "a"), ("y", "b")),
    (("x", "b"), ("x", "a"), ("y", "b"), ("y", "a")),
), (
    (("y", "a"), ("y", "b"), ("x", "a"), ("x", "b")),
    (("y", "b"), ("y", "a"), ("x", "b"), ("x", "a")),
)
CHIPS = ("x", "zl", "y", "c")


def bit(place, kind):
    return (place ^ (place >> 1)) & 1 if kind == "a" else place >> 1


def mask_of(part, core, places):
    mask = 0
    for axis, kind in ORDERS[part][core]:
        mask = 2 * mask + bit(places[axis], kind)
    return mask


def swap(field, part, *steps):
    pairs = []
    for x in range(4):
        for zl in range(2):
            for y in range(4):
                for c in range(2):
                    to = {"x": x, "y": y}
                    for axis, kind in (ORDERS[part][c][step] for step in steps):
                        to[axis] = to[axis] ^ 1 if kind == "a" else 3 - to[axis]
                    here = ((x * 2 + zl) * 4 + y) * 2 + c
                    pairs.append((here, ((to["x"] * 2 + zl) * 4 + to["y"]) * 2 + c))
    return lax.ppermute(field, CHIPS, pairs)


def swap_two(one, two, step):
    return swap(one, 0, step), swap(two, 1, step)


def spread(one, two, one_r, two_r):
    one, two = jnp.concatenate([one, one_r]), jnp.concatenate([two, two_r])
    return lax.optimization_barrier((one, two))


def add(one, two):
    return (one.astype(F32) + two.astype(F32)).astype(BF)


def shards(tokens, long_count, attn_gain, w_query, b_query, w_key, b_key, w_value, b_value,
           w_out, mlp_gain, w_gate, w_up, w_down, cotangent):
    at_x, at_y, at_c, at_t = (lax.axis_index(a) for a in ("x", "y", "c", "t"))
    places = {"x": at_x, "y": at_y}
    masks_0 = [mask_of(part, 0, places) for part in (0, 1)]
    masks_1 = [mask_of(part, 1, places) for part in (0, 1)]
    mine = [jnp.where(at_c == 0, a, b) for a, b in zip(masks_0, masks_1, strict=True)]
    theirs = [jnp.where(at_c == 0, b, a) for a, b in zip(masks_0, masks_1, strict=True)]
    info = jnp.stack([at_t, long_count[0], *mine, at_c, *theirs]).astype(jnp.int32)
    gain_one = attn_gain.astype(F32)[None, :]
    gain_two = mlp_gain.astype(F32)[None, :]

    tok_0, tok_1 = tokens, send(tokens, "t")
    half_out = lax.dynamic_slice(w_out, (at_c * SLAB, 0), (SLAB, D))
    half_out = send(half_out, "t")

    wq, wk, wv = w_query.T, w_key.T, w_value.T
    heads = wq.reshape(HEADS, HD, D)
    heads = jnp.concatenate([heads, swapped(heads, 1)], axis=1).reshape(HEADS * 128, D)
    w_all = jnp.concatenate([heads, wk, swapped(wk, 0), wv, wv], axis=0)
    bias = b_query.reshape(HEADS, HD)
    bias = jnp.concatenate([bias, swapped(bias)], axis=-1).reshape(HEADS * 128)
    b_all = jnp.concatenate([bias, b_key, swapped(b_key), b_value, b_value]).astype(F32)[None, :]
    table = angles()
    attn_in, rotated, value, stats, att_0, att_1, att_keep = attention(
        info, tok_0, tok_1, gain_one, w_all, b_all, table
    )
    rec_0 = send(att_1, "t")

    half_out, wq, w_out, _ = lax.optimization_barrier((half_out, wq, w_out, att_0))
    half_rec = send(half_out, "c")
    rec_1 = send(after(att_0, half_rec), "t")
    cot_0, cot_0_rec = cotangent, send(cotangent, "c")
    half_out = in_order(at_c, half_out, half_rec)
    no_rows = jnp.zeros((HD, D), BF)
    other_out = jnp.concatenate([*half_out, no_rows])
    this_out = jnp.concatenate([w_out, no_rows])
    g_0x, g_0y = turn(info, after(cot_0, other_out, this_out), cot_0_rec)
    cot_1 = send(after(cotangent, half_rec)[: HALF // 2], "t")
    cot_1 = jnp.concatenate([cot_1, send(after(cotangent, g_0x)[HALF // 2 :], "t")])
    cot_1_rec = send(cot_1, "c")
    w_cat = jnp.concatenate([wq, wk, jnp.zeros((HD, D), BF), wv], axis=0)
    wo_dup = w_out.reshape(HEADS, HD, D)
    wo_dup = jnp.concatenate([wo_dup, wo_dup], axis=1).reshape(HEADS * 128, D)
    rec_0, w_cat, wo_dup, g_0x, g_0y = lax.optimization_barrier((rec_0, w_cat, wo_dup, g_0x, g_0y))

    hid_0, m_0 = project(att_0, rec_0, this_out, other_out, tok_0, gain_two)
    m_0_rec = send(m_0, "c")
    attn_t = flip(after(attn_in, m_0))
    act_0, gate_0, up_0, out_0, out_0_oth, dm_0, dm_0_oth = feed(
        info, m_0, after(m_0_rec, attn_t), cot_0, cot_0_rec, w_gate, w_up, w_down
    )
    hid_1, m_1 = project(att_1, after(rec_1, act_0), this_out, other_out, tok_1, gain_two)
    m_1_rec = send(m_1, "c")
    m_0x, m_0y = turn(info, after(m_0, m_1), m_0_rec)
    dm_0 = add(dm_0, after(send(dm_0_oth, "c"), m_0x))
    dm_0_rec = send(dm_0, "t")
    act_1, gate_1, up_1, out_1, out_1_oth, dm_1, dm_1_oth = feed(
        info, after(m_1, dm_0), m_1_rec, cot_1, cot_1_rec, w_gate, w_up, w_down
    )
    m_1x, m_1y = turn(info, after(m_1, dm_1, dm_0_rec), m_1_rec)
    g_1x, g_1y = turn(info, after(cot_1, m_1x), cot_1_rec)
    dm_1 = add(dm_1, after(send(dm_1_oth, "c"), g_1x))
    dm_1_rec = send(dm_1, "t")

    gate_k, gate_g = weight_grad(m_0x, m_1x, gate_0, after(gate_1, dm_1, dm_0_rec), 0, 5)
    gate_r = swap(gate_g, 0, 0)
    up_k, up_g = weight_grad(m_0y, m_1y, up_0, after(up_1, gate_g), 0, 5)
    up_r = swap(up_g, 1, 0)
    low_k, low_g = weight_grad(g_0x, g_1x, act_0, after(act_1, up_g), 0, 2)
    low_r = swap(low_g, 0, 0)
    out_rec = [send(after(field, dm_1), "c") for field in (out_0_oth, out_1_oth)]
    mine, theirs = halves(out_0, out_1, *after_all(out_rec, low_g))
    theirs_rec = send(theirs, "t")

    grad_mid, branch, grad_att, sum_two = branch_back(
        info, dm_0, dm_1, after(dm_1_rec, mine), dm_0_rec, cot_0, cot_1, hid_0, hid_1,
        gain_two, wo_dup,
    )
    lin_a = back((0, 1), info, grad_att, rotated, value, stats, table)
    lin_b = back((2,), info, after(grad_att, lin_a), rotated, value, stats, table)
    theirs_rec = after(theirs_rec, lin_b)
    output = (hid_0 + mine.astype(F32) + theirs_rec.astype(F32)).astype(BF)
    da_own, da_send, pack_k, pack_g = last(
        info, branch, lin_a, after(lin_b, output), sum_two, att_keep, attn_t, w_cat, tok_0, tok_1
    )
    pack_r = send(pack_g, "c")

    (gate_k, gate_g), (up_k, up_g) = fold(
        info, 2, [((gate_k, after(gate_r, pack_g)), None, 0)], [((up_k, up_r), None, 0)]
    )
    gate_r, up_r = swap_two(gate_g, up_g, 1)
    ((pack_k, pack_g),) = fold(info, 2, [((pack_k, after(pack_r, gate_g)), 2, 15)])
    pack_r = swap(pack_g, 0, 0)
    high_k, high_g = weight_grad(g_0y, g_1y, act_0, after(act_1, pack_g), 2, 3)
    high_r = swap(high_g, 1, 0)
    ((pack_k, pack_g),) = fold(
        info, 2, [((pack_k, after(pack_r, high_g, gate_r, up_r)), None, 0)], weigh=3 * 10**13
    )
    pack_r = swap(pack_g, 0, 1)
    (low_k, low_g), (high_k, high_g) = fold(
        info, 2, [((low_k, after(low_r, pack_g)), None, 0)], [((high_k, high_r), None, 0)]
    )
    low_r, high_r = swap_two(low_g, high_g, 1)
    da_rec = send(after(da_send, low_g), "t")
    (one_k, one_g), (two_k, two_g) = fold(
        info,
        2,
        [
            ((gate_k, after(gate_r, low_g)), 2, 3),
            ((low_k, low_r), 2, 3),
            ((pack_k, pack_r), None, 0),
        ],
        [((up_k, up_r), 3, 3), ((high_k, high_r), 3, 3)],
    )
    one_r, two_r = swap_two(one_g, two_g, 2)

    (one_k, one_g), (two_k, two_g) = fold(
        info, 2, [((one_k, one_r), None, 0)], [((two_k, two_r), None, 0)]
    )
    one_r, two_r = swap_two(one_g, two_g, 3)
    ((part,),) = fold(info, 1, [((one_k, one_r), None, 0), ((two_k, two_r), None, 0)])
    part_r = send(part, "zl")

    field = tokens.astype(F32)
    factor = factor_of(field)
    normed = field * factor
    scaled = (da_own + after(da_rec, part).astype(F32)) * gain_one
    grad_tokens = grad_mid + factor * (
        scaled - normed * jnp.mean(scaled * normed, axis=-1, keepdims=True)
    )
    grad_tokens = grad_tokens.astype(BF)
    part = add(part, after(part_r, grad_tokens))

    wide_one = HID + SPLIT + 640
    one, two = part[..., :wide_one], part[..., wide_one:]
    for step in (3, 2, 1):
        one, two = spread(one, two, *swap_two(one, two, step))
    low_r, high_r = swap_two(one[..., HID:], two[..., HID:], 0)
    gate_r, up_r = swap_two(one[..., :HID], two[..., :HID], 0)
    one_c = send(one, "c")
    two_c = send(after(two, one_c), "c")
    grad_w_gate = wide(info, 0, one, one_c, weigh=3 * 10**13)
    grad_w_up = wide(info, 1, two, after(two_c, grad_w_gate))
    low_r, high_r = after_all((low_r, high_r), grad_w_up)
    low_c, high_c = send(low_r, "c"), send(high_r, "c")
    grad_wq, grad_wk, grad_wv, grad_wo, extras = small(info, one, low_r, one_c, low_c)
    grad_w_down = tall(info, (one, low_r, one_c, low_c), (two, high_r, two_c, high_c))
    gate_r, up_r = after_all((gate_r, up_r), grad_wo, grad_w_down)
    gate_c = send(gate_r, "c")
    up_c = send(up_r, "c")
    grad_w_gate = wide(info, 0, gate_r, gate_c, grad_w_gate)
    grad_w_up = wide(info, 1, up_r, after(up_c, grad_w_gate), grad_w_up)
    grad_w_gate, grad_w_up = grad_w_gate.reshape(D, 2432), grad_w_up.reshape(D, 2432)
    gains = extras[:, 1:].reshape(2, 2, 1024)
    gains = jnp.concatenate([gains[0, :, :512], gains[1, :, :384]], axis=1)
    gains = gains + after(send(gains, "t"), grad_w_up)
    biases = extras[0, 0, :4].reshape(512)

    return (
        output,
        grad_tokens,
        gains[0],
        grad_wq.T,
        biases[:448],
        grad_wk.T,
        biases[448:],
        grad_wv.T,
        extras[1, 0, 0, 64:],
        grad_wo,
        gains[1],
        grad_w_gate,
        grad_w_up,
        grad_w_down,
    )


def solution(mesh):
    fine = Mesh(mesh.devices.reshape(4, 2, 4, 2, 2), ("x", "zl", "y", "c", "t"))
    dp = ("x", "zl", "y", "c")
    rows, cols, split = P((*dp, "t"), None), P(None, "t"), P("t")
    down = P("t", None)
    return jax.shard_map(
        shards,
        mesh=fine,
        in_specs=(
            rows, P(dp), P(), cols, split, cols, split, cols, split, down, P(), cols, cols, down,
            rows,
        ),
        out_specs=(
            rows, rows, P(), cols, split, cols, split, cols, split, down, P(), cols, cols, down,
        ),
        check_vma=False,
    )
```
